32 devices in a mesh: items: 8 (over z, x), seq: 4 (over y, core).
Axes of the slice: x: 2, y: 2, z: 4, core: 2. Of those that a mesh axis runs over, the one named last changes fastest.
Arguments:
- tokens: bfloat16 [32768, 768], P(('items', 'seq')), may hold values from -6 to 6
- out_grad: bfloat16 [32768, 768], P(('items', 'seq')), may hold values from -6 to 6
- time_table: bfloat16 [2000, 768], replicated, may hold values from -6 to 6
- time_step: int32 [256, 2], P('items'), may hold values from 0 to 1999
- tile_split: int32 [256], P('items'), may hold values 0 or 1
- block_slot: int32 [192], replicated, may hold values from 0 to 191, as said below
- weight_slots: float32 [192, 192, 192], P('items')
- momentum_slots: float32 [192, 192, 192], P('items')
- stat_left: float32 [192, 192, 192], P('items')
- stat_right: float32 [192, 192, 192], P('items')
- root_left: float32 [192, 192, 192], P('items')
- root_right: float32 [192, 192, 192], P('items')
- vectors: float32 [12, 768], P(None, 'items')
- vector_first: float32 [12, 768], P(None, 'items')
- vector_second: float32 [12, 768], P(None, 'items')
Outputs:
- output: bfloat16 [32768, 768], P(('items', 'seq'))
- input_grad: bfloat16 [32768, 768], P(('items', 'seq'))
- matrix_grad: float32 [192, 192, 192], P('items')
- matrix_momentum: float32 [192, 192, 192], P('items')
- matrix_new: float32 [192, 192, 192], P('items')
- stat_left_new: float32 [192, 192, 192], P('items')
- stat_right_new: float32 [192, 192, 192], P('items')
- vector_grad: float32 [12, 768], P(None, 'items')
- vector_first_new: float32 [12, 768], P(None, 'items')
- vector_second_new: float32 [12, 768], P(None, 'items')
- vector_new: float32 [12, 768], P(None, 'items')
The draws below stay inside these ranges and needn't reach their ends.
Inputs may be any that keep to these rules, and one draw needn't show every extreme that they name: block_slot is a permutation of the 192 slots; slot j lies with items index j // 24.
All inputs are finite; a program needn't handle non-finite values. No bound on the sum of `tile_split` on one device may be relied on, other than what follows from the above.
Results may differ from the reference program's by a relative error of at most 0.011.
Values may be sent and summed in bfloat16 or wider, within the bound.
A program may use at most 256 MiB of HBM per device.

```python
import math
import jax
import jax.numpy as jnp
from jax import lax

D = 768
HEADS = 12
FF = 3072
HD = 64
TILE = 128
TSTEPS = 2000
BLK = 192
GROUP = 4096
TOKENS = 32768
TILES = 256
NBLK = 192
VROWS = 12
N_ITEMS = 8


gradient_factors = [1.3, 0.2, 0.3, 0.5]


def gradient_size():
    return GROUP / math.sqrt(TOKENS)


def slot_order(key):
    return jax.random.permutation(jax.random.fold_in(key, 7), NBLK).astype(jnp.int32)


def block_kinds(key):
    ordering = slot_order(key)
    owner_block = jnp.zeros((NBLK,), jnp.int32).at[ordering].set(jnp.arange(NBLK, dtype=jnp.int32))
    row_blocks = D // BLK
    first_end = row_blocks * (3 * D // BLK)
    second_end = first_end + row_blocks * row_blocks
    third_end = second_end + row_blocks * (FF // BLK)
    return (owner_block >= first_end).astype(jnp.int32) + (owner_block >= second_end).astype(jnp.int32) + (owner_block >= third_end).astype(jnp.int32)


def kind_pick(kinds, table_values):
    return jnp.take(jnp.array(table_values, jnp.float32), kinds)


def statistic_draw(key, salt):
    kinds = block_kinds(key)
    key = jax.random.fold_in(key, salt)
    level = kind_pick(kinds, gradient_factors) * gradient_size()
    diagonal = 4.0 ** jax.random.uniform(key, (NBLK, BLK), jnp.float32)
    diagonal = diagonal * 0.05 * BLK * (level * level)[:, None]
    return jnp.eye(BLK, dtype=jnp.float32)[None] * diagonal[:, :, None]


def root_draw(key, salt):
    kinds = block_kinds(key)
    key = jax.random.fold_in(key, salt)
    level = kind_pick(kinds, gradient_factors) * gradient_size()
    root_scale = (0.05 * BLK * level * level) ** (-0.25)
    diagonal = 0.5 * 4.0 ** jax.random.uniform(key, (NBLK, BLK), jnp.float32)
    noise = jax.random.normal(jax.random.fold_in(key, 1), (NBLK, BLK, BLK), jnp.float32) * (0.5 / math.sqrt(BLK))
    symmetric = 0.5 * (noise + jnp.swapaxes(noise, 1, 2))
    identity = jnp.eye(BLK, dtype=jnp.float32)[None]
    return (identity * diagonal[:, :, None] + (1.0 - identity) * symmetric) * root_scale[:, None, None]


def row_factors():
    return jnp.where(jnp.arange(VROWS) >= 8, 0.3, 1.0).astype(jnp.float32)[:, None]


def draw_block_slot(key, part):
    return slot_order(key)


def draw_weight_slots(key, part):
    kinds = block_kinds(key)
    key = jax.random.fold_in(key, 1)
    spread = kind_pick(kinds, [D ** (-0.5), (D // HD) ** (-0.5), D ** (-0.5), FF ** (-0.5)])
    return jax.random.normal(key, (NBLK, BLK, BLK), jnp.float32) * spread[:, None, None]


def draw_momentum_slots(key, part):
    kinds = block_kinds(key)
    key = jax.random.fold_in(key, 2)
    level = kind_pick(kinds, gradient_factors) * gradient_size()
    return jax.random.normal(key, (NBLK, BLK, BLK), jnp.float32) * level[:, None, None]


def draw_stat_left(key, part):
    return statistic_draw(key, 3)


def draw_stat_right(key, part):
    return statistic_draw(key, 4)


def draw_root_left(key, part):
    return root_draw(key, 5)


def draw_root_right(key, part):
    return root_draw(key, 6)


def draw_vectors(key, part):
    key = jax.random.fold_in(key, 8)
    gains = jax.random.uniform(key, (2, D), jnp.float32, 0.6, 1.4)
    shifts = 0.2 * jax.random.normal(jax.random.fold_in(key, 1), (VROWS - 2, D), jnp.float32)
    return jnp.concatenate([gains, shifts], 0)


def draw_vector_first(key, part):
    key = jax.random.fold_in(key, 9)
    return 0.11 * gradient_size() * row_factors() * jax.random.normal(key, (VROWS, D), jnp.float32)


def draw_vector_second(key, part):
    key = jax.random.fold_in(key, 10)
    level = gradient_size() * row_factors()
    return 0.001 * level * level * 4.0 ** jax.random.uniform(key, (VROWS, D), jnp.float32)


def set_ends(values, rng, low, largest):
    longest = values.shape.index(max(values.shape))
    spots = []
    for shift in (0, 1):
        where = [jax.random.randint(jax.random.fold_in(rng, axis), (), 0, length) for axis, length in enumerate(values.shape)]
        where[longest] = (where[longest] + shift) % values.shape[longest]
        spots.append(tuple(where))
    return values.at[spots[0]].set(low).at[spots[1]].set(largest)


def steps_of(rng, dims, shards, smallest, largest):
    factor_of = 1.0
    for dim, blocks in shards:
        steps = jax.random.uniform(jax.random.fold_in(jax.random.fold_in(rng, 6), dim), (blocks,), jnp.float32, smallest / len(shards), largest / len(shards))
        factor_of = factor_of * jnp.repeat(jnp.exp(steps), dims[dim] // blocks).reshape((-1,) + (1,) * (len(dims) - 1 - dim))
    return factor_of


def normal_values(stream_key, extent, deviation, reach, split=(), kind=jnp.bfloat16):
    loudness = steps_of(stream_key, extent, split, -0.22, 0.18) if split else 1.0
    values = jax.random.normal(stream_key, extent, jnp.float32) * deviation * loudness
    return jnp.minimum(jnp.maximum(values, -reach), reach).astype(kind)


def setup_inputs(seed: int = 0) -> dict:
    streams_of = jax.random.split(jax.random.key(seed), 16)
    tokens = normal_values(streams_of[0], (TOKENS, D), 1.0, 6.0, ((0, 32),))
    out_grad = normal_values(streams_of[1], (TOKENS, D), 1.0, 6.0, ((0, 32),))
    time_table = normal_values(streams_of[2], (TSTEPS, D), 1.0, 6.0)
    time_step = set_ends(jax.random.randint(streams_of[3], (TILES, 2), 0, TSTEPS), jax.random.fold_in(streams_of[3], 1), 0, TSTEPS - 1).astype(jnp.int32)
    tile_split = set_ends((jax.random.randint(streams_of[4], (TILES,), 0, 2) < 1).astype(jnp.int32), jax.random.fold_in(streams_of[4], 1), 0, 1)
    block_slot = draw_block_slot(jax.random.fold_in(streams_of[15], 71), 0)
    weight_slots = draw_weight_slots(jax.random.fold_in(streams_of[15], 71), 0)
    momentum_slots = draw_momentum_slots(jax.random.fold_in(streams_of[15], 71), 0)
    stat_left = draw_stat_left(jax.random.fold_in(streams_of[15], 71), 0)
    stat_right = draw_stat_right(jax.random.fold_in(streams_of[15], 71), 0)
    root_left = draw_root_left(jax.random.fold_in(streams_of[15], 71), 0)
    root_right = draw_root_right(jax.random.fold_in(streams_of[15], 71), 0)
    vectors = draw_vectors(jax.random.fold_in(streams_of[15], 71), 0)
    vector_first = draw_vector_first(jax.random.fold_in(streams_of[15], 71), 0)
    vector_second = draw_vector_second(jax.random.fold_in(streams_of[15], 71), 0)
    return dict(tokens=tokens, out_grad=out_grad, time_table=time_table, time_step=time_step, tile_split=tile_split, block_slot=block_slot, weight_slots=weight_slots, momentum_slots=momentum_slots, stat_left=stat_left, stat_right=stat_right, root_left=root_left, root_right=root_right, vectors=vectors, vector_first=vector_first, vector_second=vector_second)


@jax.custom_vjp
def low(v):
    return lax.optimization_barrier(v.astype(jnp.bfloat16)).astype(jnp.float32)

@jax.custom_vjp
def low_back(v):
    return v

def low_keep(v):
    return (low(v), None)

def low_pass(kept, grad):
    return (grad,)

def back_keep(v):
    return (v, None)

def back_low(kept, grad):
    return (low(grad),)
low.defvjp(low_keep, low_pass)
low_back.defvjp(back_keep, back_low)
highest = lax.Precision.HIGHEST
masked_score = -1000000000.0
norm_epsilon = 1e-05

def layer_norm(values, gain, shift):
    average = lax.optimization_barrier(jnp.mean(values, -1, keepdims=True))
    centred = values - average
    spread = lax.optimization_barrier(jnp.mean(centred * centred, -1, keepdims=True))
    return centred * lax.rsqrt(spread + norm_epsilon) * gain + shift

def gelu_exact(values):
    return jax.nn.gelu(values, approximate=False)

def tile_mask(split_block, tile_width):
    halves = jnp.arange(tile_width) // (tile_width // 2)
    same_half = halves[:, None] == halves[None, :]
    return ((split_block[:, None, None] == 0) | same_half[None])[:, None]

def block_split(matrix):
    rows_all, cols_all = matrix.shape
    return matrix.reshape(rows_all // BLK, BLK, cols_all // BLK, BLK).transpose(0, 2, 1, 3).reshape(-1, BLK, BLK)

def block_join(blocks, rows_all, cols_all):
    return blocks.reshape(rows_all // BLK, cols_all // BLK, BLK, BLK).transpose(0, 2, 1, 3).reshape(rows_all, cols_all)

def matmul(left, right):
    return jnp.dot(left, right, preferred_element_type=jnp.float32, precision=highest)

def attend_group(qkv_group, split_group):
    tile_count = GROUP // TILE
    shaped = qkv_group.reshape(tile_count // 4, 4, TILE, 3, HEADS, HD)
    splits = split_group.reshape(tile_count // 4, 4)

    def one_block(inputs_pair):
        packed, split_block = inputs_pair
        queries = packed[:, :, 0]
        key_rows = packed[:, :, 1]
        value_rows = packed[:, :, 2]
        scores = low_back(jnp.einsum('tqhd,tkhd->thqk', queries, key_rows, precision=highest) * HD ** (-0.5))
        scores = jnp.where(tile_mask(split_block, TILE), scores, masked_score)
        maximum = lax.optimization_barrier(jnp.max(scores, -1, keepdims=True))
        exponent = jnp.exp(scores - maximum)
        probability = exponent / lax.optimization_barrier(jnp.sum(exponent, -1, keepdims=True))
        return jnp.einsum('thqk,tkhd->tqhd', low(probability), value_rows, precision=highest)
    mixed = lax.map(jax.checkpoint(one_block), (shaped, splits))
    return mixed.reshape(GROUP, D)

def group_forward(params, hidden_zero, split_group):
    w_qkv, w_out, w_up, w_down, vector_rows = params
    normed_one = low(layer_norm(hidden_zero, vector_rows[0], vector_rows[2]))
    qkv_bias = jnp.concatenate([vector_rows[4], jnp.zeros_like(vector_rows[4]), vector_rows[5]])
    qkv = low_back(low(matmul(normed_one, w_qkv) + qkv_bias))
    mixed = low_back(low(attend_group(qkv, split_group)))
    attn_out = low_back(matmul(mixed, w_out) + vector_rows[6])
    hidden_one = hidden_zero + attn_out
    normed_two = low(layer_norm(hidden_one, vector_rows[1], vector_rows[3]))
    upper = low_back(matmul(normed_two, w_up) + vector_rows[8:].reshape(FF))
    active = low(gelu_exact(upper))
    return hidden_one + matmul(active, w_down) + vector_rows[7]

def full_forward(params, hidden, tile_split):

    def one_group(carry, inputs_pair):
        return (carry, jax.checkpoint(group_forward)(params, inputs_pair[0], inputs_pair[1]))
    _, outputs = lax.scan(one_group, jnp.zeros((), jnp.float32), (hidden.reshape(N_ITEMS, GROUP, D), tile_split.reshape(N_ITEMS, GROUP // TILE)))
    return outputs.reshape(TOKENS, D)

def reference(tokens, out_grad, time_table, time_step, tile_split, block_slot, weight_slots, momentum_slots, stat_left, stat_right, root_left, root_right, vectors, vector_first, vector_second):
    position = jnp.arange(TOKENS, dtype=jnp.int32)
    tile_global = position // TILE
    chosen = position % TILE // (TILE // 2) * jnp.take(tile_split, tile_global)
    step_index = jnp.take(time_step.reshape(-1), tile_global * 2 + chosen)
    hidden_zero = tokens.astype(jnp.float32) + jnp.take(time_table, step_index, axis=0).astype(jnp.float32)
    blocks = low(jnp.take(weight_slots, block_slot, axis=0))
    row_blocks = D // BLK
    count_qkv = row_blocks * (3 * D // BLK)
    count_out = row_blocks * row_blocks
    count_up = row_blocks * (FF // BLK)
    w_qkv = block_join(blocks[:count_qkv], D, 3 * D)
    w_out = block_join(blocks[count_qkv:count_qkv + count_out], D, D)
    w_up = block_join(blocks[count_qkv + count_out:count_qkv + count_out + count_up], D, FF)
    w_down = block_join(blocks[count_qkv + count_out + count_up:], FF, D)
    params = (w_qkv, w_out, w_up, w_down, low(vectors))

    def whole(param_tuple, hidden):
        return full_forward(param_tuple, hidden, tile_split)
    result, pull = jax.vjp(whole, params, hidden_zero)
    grad_params, grad_hidden = pull(out_grad.astype(jnp.float32))
    output = result.astype(jnp.bfloat16)
    input_grad = grad_hidden.astype(jnp.bfloat16)
    grad_blocks = jnp.concatenate([block_split(grad_params[0]), block_split(grad_params[1]), block_split(grad_params[2]), block_split(grad_params[3])], 0)
    slot_block = jnp.zeros((NBLK,), jnp.int32).at[block_slot].set(jnp.arange(NBLK, dtype=jnp.int32))
    matrix_grad = jnp.take(grad_blocks, slot_block, axis=0) / N_ITEMS
    vector_grad = grad_params[4] / N_ITEMS
    matrix_momentum = 0.9 * momentum_slots + matrix_grad
    stat_left_new = 0.95 * stat_left + 0.05 * jnp.einsum('sij,skj->sik', matrix_grad, matrix_grad, precision=highest)
    stat_right_new = 0.95 * stat_right + 0.05 * jnp.einsum('sji,sjk->sik', matrix_grad, matrix_grad, precision=highest)
    direction = jnp.einsum('sij,sjk->sik', root_left, matrix_momentum, precision=highest)
    direction = jnp.einsum('sij,sjk->sik', direction, root_right, precision=highest)
    weight_scale = jnp.sqrt(lax.optimization_barrier(jnp.mean(weight_slots * weight_slots, (1, 2), keepdims=True)) + 1e-06)
    direction_scale = lax.rsqrt(lax.optimization_barrier(jnp.mean(direction * direction, (1, 2), keepdims=True)) + 1e-06)
    matrix_new = weight_slots - 0.3 * weight_scale * direction * direction_scale
    vector_first_new = 0.9 * vector_first + 0.1 * vector_grad
    vector_second_new = 0.999 * vector_second + 0.001 * vector_grad * vector_grad
    vector_new = vectors - 0.1 * vector_first_new / (jnp.sqrt(vector_second_new) + 1e-08)
    return (output, input_grad, matrix_grad, matrix_momentum, matrix_new, stat_left_new, stat_right_new, vector_grad, vector_first_new, vector_second_new, vector_new)
```

```python
import functools
import jax
import jax.numpy as jnp
from jax import lax
from jax.experimental import pallas as pl
from jax.experimental.pallas import tpu as pltpu
from jax.sharding import PartitionSpec as P

D = 768
HEADS = 12
HD = 64
TILE = 128
BLK = 192
NBLK = 192
HALF = 96
WIDE = 384
MESH = pl.DeviceIdType.MESH
BF16 = jnp.bfloat16
F32 = jnp.float32
MIB = 2 ** 20
highest = lax.Precision.HIGHEST
masked_score = -1000000000.0
norm_epsilon = 1e-05
score_scale = HD ** (-0.5)


def place():
    it = lax.axis_index("items")
    sq = lax.axis_index("seq")
    return it // 2, it % 2, sq // 2, sq % 2


def greet(partners):
    barrier = pltpu.get_barrier_semaphore()
    for partner in partners:
        pl.semaphore_signal(barrier, inc=1, device_id=partner, device_id_type=MESH)
    pl.semaphore_wait(barrier, len(partners))


class Copies:
    def __init__(self, send_sem, recv_sem):
        self.send_sem, self.recv_sem = send_sem, recv_sem
        self.sent = []

    def start(self, index, src, dst, device):
        made = pltpu.make_async_remote_copy(
            src_ref=src, dst_ref=dst,
            send_sem=self.send_sem.at[index], recv_sem=self.recv_sem.at[index],
            device_id=device, device_id_type=MESH,
        )
        made.start()
        self.sent.append(made)

    def wait(self, index, dst, device):
        pltpu.make_async_remote_copy(
            src_ref=dst, dst_ref=dst,
            send_sem=self.send_sem.at[index], recv_sem=self.recv_sem.at[index],
            device_id=device, device_id_type=MESH,
        ).wait_recv()

    def finish(self):
        for made in self.sent:
            made.wait_send()


GATHER_X_FIRST = (True, False, True, True, False, True)


def gather_kernel(slots_ref, vec_ref, blocks_ref, vecs_ref, raw, own, vec_own, raw_sem, own_sem, send_sem, recv_sem, vsend, vrecv):
    z, x, y, c = place()
    me = z * 2 + x
    quarter = y * 2 + c
    across_x = (z * 2 + (1 - x), quarter)
    across_y = (me, (1 - y) * 2 + c)
    across_c = (me, y * 2 + (1 - c))
    far = [(z + d) % 4 for d in (1, 2, 3)]
    along_z = [(f * 2 + x, quarter) for f in far]
    others = along_z + [(f * 2 + (1 - x), quarter) for f in far] + [across_x]

    def loads(j):
        slot = (quarter * 6 + j * 6) % 24
        return pltpu.make_async_copy(slots_ref.at[pl.ds(slot, 6)], raw.at[pl.ds(slot, 6)], raw_sem.at[j])

    for j in range(4):
        loads(j).start()
    greet(others + [across_y, across_c])
    copies = Copies(send_sem, recv_sem)
    vcopies = Copies(vsend, vrecv)
    vec_own[...] = jnp.zeros_like(vec_own)
    vec_own[0:12, 0:96] = vec_ref[...]
    for i, d in enumerate((1, 2, 3)):
        vcopies.start(i, vec_own, vecs_ref.at[me], along_z[i])
        vcopies.start(3 + i, vec_own, vecs_ref.at[me], (far[i] * 2 + (1 - x), quarter))
    vcopies.start(6, vec_own, vecs_ref.at[me], across_x)

    def cast(slot):
        own[slot, :, 0:192] = raw[slot, 0:HALF, :].astype(BF16)
        own[slot, :, 192:384] = raw[slot, HALF:BLK, :].astype(BF16)

    base = quarter * 6
    base_y = ((1 - y) * 2 + c) * 6
    def send_z(k):
        slot = base + k
        for i in range(3):
            copies.start((k, i), own.at[slot], blocks_ref.at[me, slot], along_z[i])

    def core(k, index, owner, slot):
        copies.start((k, index), blocks_ref.at[owner, slot], blocks_ref.at[owner, slot], across_c)

    def phase_two(k):
        slot = base + k
        if GATHER_X_FIRST[k]:
            copies.start((k, 3), own.at[slot], blocks_ref.at[me, slot], across_x)
        else:
            copies.start((k, 6), own.at[slot], blocks_ref.at[me, slot], across_x)
            slot_y = base_y + k
            copies.start((k, 7), own.at[slot_y], blocks_ref.at[me, slot_y], across_x)
        for i in range(3):
            owner = ((z - (i + 1)) % 4) * 2 + x
            ref = blocks_ref.at[owner, slot]
            copies.wait((k, i), ref, along_z[i])
            if GATHER_X_FIRST[k]:
                copies.start((k, 4 + i), ref, ref, across_x)
                copies.start((k, 7 + i), ref, ref, across_y)
            else:
                copies.start((k, 3 + i), ref, ref, across_y)
                copies.start((k, 8 + i), ref, ref, across_x)
            core(k, 14 + i, owner, slot)

    def phase_three(k):
        slot = base + k
        slot_y = base_y + k
        if GATHER_X_FIRST[k]:
            for p in range(4):
                owner = ((z - p) % 4) * 2 + (1 - x)
                ref = blocks_ref.at[owner, slot]
                copies.wait((k, 3 + p), ref, across_x)
                copies.start((k, 10 + p), ref, ref, across_y)
                core(k, 17 + p, owner, slot)
        else:
            for i in range(3):
                owner = ((z - (i + 1)) % 4) * 2 + x
                ref = blocks_ref.at[owner, slot_y]
                copies.wait((k, 3 + i), ref, across_y)
                copies.start((k, 11 + i), ref, ref, across_x)
                core(k, 17 + i, owner, slot_y)

    def phase_four(k):
        slot = base + k
        slot_y = base_y + k
        if GATHER_X_FIRST[k]:
            for i in range(3):
                owner = ((z - (i + 1)) % 4) * 2 + x
                copies.wait((k, 7 + i), blocks_ref.at[owner, slot_y], across_y)
                core(k, 21 + i, owner, slot_y)
            for p in range(4):
                owner = ((z - p) % 4) * 2 + (1 - x)
                copies.wait((k, 10 + p), blocks_ref.at[owner, slot_y], across_y)
                core(k, 24 + p, owner, slot_y)
        else:
            mine = z * 2 + (1 - x)
            copies.wait((k, 6), blocks_ref.at[mine, slot], across_x)
            core(k, 20, mine, slot)
            copies.wait((k, 7), blocks_ref.at[mine, slot_y], across_x)
            core(k, 21, mine, slot_y)
            for i in range(3):
                owner = ((z - (i + 1)) % 4) * 2 + (1 - x)
                copies.wait((k, 8 + i), blocks_ref.at[owner, slot], across_x)
                core(k, 22 + i, owner, slot)
            for i in range(3):
                owner = ((z - (i + 1)) % 4) * 2 + (1 - x)
                copies.wait((k, 11 + i), blocks_ref.at[owner, slot_y], across_x)
                core(k, 25 + i, owner, slot_y)

    base_c = (y * 2 + (1 - c)) * 6
    base_yc = ((1 - y) * 2 + (1 - c)) * 6

    def core_waits(k):
        slot_c = base_c + k
        slot_yc = base_yc + k
        def w(index, owner, slot):
            copies.wait((k, index), blocks_ref.at[owner, slot], across_c)
        same = [((z - (i + 1)) % 4) * 2 + x for i in range(3)]
        cross = [((z - p) % 4) * 2 + (1 - x) for p in range(4)]
        for i in range(3):
            w(14 + i, same[i], slot_c)
        if GATHER_X_FIRST[k]:
            for p in range(4):
                w(17 + p, cross[p], slot_c)
            for i in range(3):
                w(21 + i, same[i], slot_yc)
            for p in range(4):
                w(24 + p, cross[p], slot_yc)
        else:
            for i in range(3):
                w(17 + i, same[i], slot_yc)
            w(20, cross[0], slot_c)
            w(21, cross[0], slot_yc)
            for i in range(3):
                w(22 + i, cross[1 + i], slot_c)
            for i in range(3):
                w(25 + i, cross[1 + i], slot_yc)

    steps = 6
    loads(0).wait()
    for k in range(2):
        cast(base + k)
        send_z(k)
    for k in range(2, steps):
        cast(base + k)
    loads(2).wait()
    for k in range(steps):
        cast(base_y + k)
    for t in range(steps + 2):
        if t < steps:
            phase_two(t)
            if t + 2 < steps:
                send_z(t + 2)
        if 1 <= t <= steps:
            phase_three(t - 1)
        if t == 0:
            loads(1).wait()
            loads(3).wait()
            lax.fori_loop(0, 6, lambda k, carry: (cast(base_c + k), cast(base_yc + k), carry)[2], 0)
            local = pltpu.make_async_copy(own, blocks_ref.at[me], own_sem)
            local.start()
            vecs_ref[me] = vec_own[...]
        if t >= 2:
            phase_four(t - 2)
    for k in range(steps):
        core_waits(k)
    local.wait()
    for i in range(3):
        vcopies.wait(i, vecs_ref.at[((z - (i + 1)) % 4) * 2 + x], along_z[i])
        vcopies.wait(3 + i, vecs_ref.at[((z - (i + 1)) % 4) * 2 + (1 - x)], along_z[i])
    vcopies.wait(6, vecs_ref.at[z * 2 + (1 - x)], across_x)
    copies.finish()
    vcopies.finish()


def gather_weights(slots, vectors):
    return pl.pallas_call(
        gather_kernel,
        out_shape=(
            jax.ShapeDtypeStruct((8, 24, HALF, WIDE), BF16),
            jax.ShapeDtypeStruct((8, 16, 128), F32),
        ),
        in_specs=[pl.BlockSpec(memory_space=pl.ANY), pl.BlockSpec(memory_space=pltpu.VMEM)],
        out_specs=(pl.BlockSpec(memory_space=pl.ANY), pl.BlockSpec(memory_space=pltpu.VMEM)),
        scratch_shapes=[
            pltpu.VMEM((24, BLK, BLK), F32),
            pltpu.VMEM((24, HALF, WIDE), BF16),
            pltpu.VMEM((16, 128), F32),
            pltpu.SemaphoreType.DMA((4,)),
            pltpu.SemaphoreType.DMA,
            pltpu.SemaphoreType.DMA((6, 28)),
            pltpu.SemaphoreType.DMA((6, 28)),
            pltpu.SemaphoreType.DMA((7,)),
            pltpu.SemaphoreType.DMA((7,)),
        ],
        compiler_params=pltpu.CompilerParams(collective_id=0, has_side_effects=True, vmem_limit_bytes=24 * MIB),
        name="gather_weights",
    )(slots, vectors)


SCATTER_Y_FIRST = (True, False, True, False, True, False)


def scatter_kernel(part_ref, vec_ref, sum_ref, vsum_ref, acc, from_c, from_y, from_x, from_z, fin, va, vb, vz, load_sem, out_sem, send_sem, recv_sem, vsend, vrecv):
    z, x, y, c = place()
    me = z * 2 + x
    quarter = y * 2 + c
    across_x = (z * 2 + (1 - x), quarter)
    across_y = (me, (1 - y) * 2 + c)
    across_c = (me, y * 2 + (1 - c))
    far = [(z + d) % 4 for d in (1, 2, 3)]
    along_z = [(f * 2 + x, quarter) for f in far]
    steps = 6

    def load(k, yy):
        slot = (yy * 2 + c) * 6 + k
        return pltpu.make_async_copy(part_ref.at[:, slot], acc.at[k, yy], load_sem.at[k, yy])

    for k in range(steps):
        for yy in range(2):
            load(k, yy).start()
    greet([across_x, across_y, across_c] + along_z)
    copies = Copies(send_sem, recv_sem)
    vcopies = Copies(vsend, vrecv)
    for k in range(steps):
        for yy in range(2):
            slot = (yy * 2 + (1 - c)) * 6 + k
            copies.start((k, yy), part_ref.at[:, slot], from_c.at[k, yy], across_c)
    vcopies.start(0, vec_ref, va, across_c)

    def core_add(k):
        for yy in range(2):
            load(k, yy).wait()
            copies.wait((k, yy), from_c.at[k, yy], across_c)

        def owner_add(o, carry):
            for yy in range(2):
                acc[k, yy, o] = acc[k, yy, o] + from_c[k, yy, o]
            return carry

        lax.fori_loop(0, 8, owner_add, 0)
        if SCATTER_Y_FIRST[k]:
            copies.start((k, 2), acc.at[k, 1 - y], from_y.at[k], across_y)
        else:
            for yy in range(2):
                for zz in range(4):
                    copies.start((k, 2 + yy * 4 + zz), acc.at[k, yy, zz * 2 + (1 - x)], from_x.at[k, yy, zz], across_x)

    def second_add(k):
        if SCATTER_Y_FIRST[k]:
            copies.wait((k, 2), from_y.at[k], across_y)

            def owner_add(o, carry):
                acc[k, y, o] = acc[k, y, o] + from_y[k, o]
                return carry

            lax.fori_loop(0, 8, owner_add, 0)
            for zz in range(4):
                copies.start((k, 3 + zz), acc.at[k, y, zz * 2 + (1 - x)], from_x.at[k, 0, zz], across_x)
        else:
            for yy in range(2):
                for zz in range(4):
                    copies.wait((k, 2 + yy * 4 + zz), from_x.at[k, yy, zz], across_x)

            def z_add(zz, carry):
                for yy in range(2):
                    acc[k, yy, zz * 2 + x] = acc[k, yy, zz * 2 + x] + from_x[k, yy, zz]
                return carry

            lax.fori_loop(0, 4, z_add, 0)
            for zz in range(4):
                copies.start((k, 10 + zz), acc.at[k, 1 - y, zz * 2 + x], from_y.at[k, zz], across_y)

    def third_add(k):
        if SCATTER_Y_FIRST[k]:
            for zz in range(4):
                copies.wait((k, 3 + zz), from_x.at[k, 0, zz], across_x)

            def z_add(zz, carry):
                acc[k, y, zz * 2 + x] = acc[k, y, zz * 2 + x] + from_x[k, 0, zz]
                return carry
        else:
            for zz in range(4):
                copies.wait((k, 10 + zz), from_y.at[k, zz], across_y)

            def z_add(zz, carry):
                acc[k, y, zz * 2 + x] = acc[k, y, zz * 2 + x] + from_y[k, zz]
                return carry

        lax.fori_loop(0, 4, z_add, 0)
        for i in range(3):
            copies.start((k, 14 + i), acc.at[k, y, far[i] * 2 + x], from_z.at[k, i], along_z[i])

    def last_add(k):
        for i in range(3):
            copies.wait((k, 14 + i), from_z.at[k, i], along_z[i])
        total = acc[k, y, me].astype(F32)
        for i in range(3):
            total = total + from_z[k, i].astype(F32)
        slot = quarter * 6 + k
        fin[slot] = total.astype(BF16)
        copies.start((k, 17), fin.at[slot], fin.at[slot], across_y)
        copies.start((k, 18), fin.at[slot], fin.at[slot], across_c)
        pltpu.make_async_copy(fin.at[slot], sum_ref.at[slot], out_sem.at[k, 0]).start()

    def spread(k):
        slot_y = ((1 - y) * 2 + c) * 6 + k
        copies.wait((k, 17), fin.at[slot_y], across_y)
        copies.start((k, 19), fin.at[slot_y], fin.at[slot_y], across_c)
        pltpu.make_async_copy(fin.at[slot_y], sum_ref.at[slot_y], out_sem.at[k, 1]).start()

    def spread_core(k):
        for j, (yy, index) in enumerate(((y, 18), (1 - y, 19))):
            slot = (yy * 2 + (1 - c)) * 6 + k
            copies.wait((k, index), fin.at[slot], across_c)
            pltpu.make_async_copy(fin.at[slot], sum_ref.at[slot], out_sem.at[k, 2 + j]).start()

    def vec_step(t):
        if t == 0:
            vcopies.wait(0, va, across_c)
            va[...] = va[...] + vec_ref[...]
            vcopies.start(1, va, vb.at[0], across_y)
        elif t == 1:
            vcopies.wait(1, vb.at[0], across_y)
            vb[1] = va[...] + vb[0]
            vcopies.start(2, vb.at[1], vb.at[2], across_x)
        elif t == 2:
            vcopies.wait(2, vb.at[2], across_x)
            vb[3] = vb[1] + vb[2]
            for i in range(3):
                vcopies.start(3 + i, vb.at[3, far[i] * 2 + x], vz.at[i], along_z[i])
        elif t == 3:
            for i in range(3):
                vcopies.wait(3 + i, vz.at[i], along_z[i])
            vsum_ref[...] = vb[3, me] + vz[0] + vz[1] + vz[2]

    for t in range(steps + 5):
        if t < steps:
            core_add(t)
        if 1 <= t <= steps:
            second_add(t - 1)
        if 2 <= t <= steps + 1:
            third_add(t - 2)
        if 3 <= t <= steps + 2:
            last_add(t - 3)
        if 4 <= t <= steps + 3:
            spread(t - 4)
        if 5 <= t:
            spread_core(t - 5)
        vec_step(t)
    for k in range(steps):
        for j in range(4):
            pltpu.make_async_copy(fin.at[0], sum_ref.at[0], out_sem.at[k, j]).wait()
    copies.finish()
    vcopies.finish()


def scatter_sums(parts, vecs):
    return pl.pallas_call(
        scatter_kernel,
        out_shape=(
            jax.ShapeDtypeStruct((24, HALF, WIDE), BF16),
            jax.ShapeDtypeStruct((16, 128), F32),
        ),
        in_specs=[pl.BlockSpec(memory_space=pl.ANY), pl.BlockSpec(memory_space=pltpu.VMEM)],
        out_specs=(pl.BlockSpec(memory_space=pl.ANY), pl.BlockSpec(memory_space=pltpu.VMEM)),
        scratch_shapes=[
            pltpu.VMEM((6, 2, 8, HALF, WIDE), BF16),
            pltpu.VMEM((6, 2, 8, HALF, WIDE), BF16),
            pltpu.VMEM((6, 8, HALF, WIDE), BF16),
            pltpu.VMEM((6, 2, 4, HALF, WIDE), BF16),
            pltpu.VMEM((6, 3, HALF, WIDE), BF16),
            pltpu.VMEM((24, HALF, WIDE), BF16),
            pltpu.VMEM((8, 16, 128), F32),
            pltpu.VMEM((4, 8, 16, 128), F32),
            pltpu.VMEM((3, 16, 128), F32),
            pltpu.SemaphoreType.DMA((6, 2)),
            pltpu.SemaphoreType.DMA((6, 4)),
            pltpu.SemaphoreType.DMA((6, 20)),
            pltpu.SemaphoreType.DMA((6, 20)),
            pltpu.SemaphoreType.DMA((6,)),
            pltpu.SemaphoreType.DMA((6,)),
        ],
        compiler_params=pltpu.CompilerParams(collective_id=1, has_side_effects=True, vmem_limit_bytes=40 * MIB),
        name="scatter_sums",
    )(parts, vecs)


def dot_nn(left, right):
    return jnp.dot(left, right, preferred_element_type=F32)


def dot_nt(left, right):
    return lax.dot_general(left, right, (((1,), (1,)), ((), ())), preferred_element_type=F32)


def dot_tn(left, right):
    return lax.dot_general(left, right, (((0,), (0,)), ((), ())), preferred_element_type=F32)


def normalised(values):
    average = jnp.mean(values, -1, keepdims=True)
    centred = values - average
    spread = jnp.mean(centred * centred, -1, keepdims=True)
    scale = lax.rsqrt(spread + norm_epsilon)
    return centred * scale, scale


def norm_back(cotangent, hat, scale, gain):
    inner = cotangent * gain
    first = jnp.mean(inner, -1, keepdims=True)
    second = jnp.mean(inner * hat, -1, keepdims=True)
    return scale * (inner - first - hat * second)


ROWS = 256
TOK_TILES_MAX = 8


def layer_kernel(
    step_ref, split_ref, slot_ref, tok_ref, grad_ref, table_ref, blocks_ref, vec_ref,
    out_ref, in_grad_ref, parts_ref, dvec_ref,
    par, dpar, table_rows, h0, a, qkv, prob, mixed, h1, c, acc_o, acc_d, r, du, dqkv,
    w_qkv, w_out, w_up, w_down, stage, emit, table_sem, stage_sem, emit_sem,
):
    tok_rows = tok_ref.shape[0]
    tiles = tok_rows // TILE
    row_tiles = tok_rows // ROWS
    first_tile = lax.axis_index("seq") * tiles

    def block_of(chunk, i, j):
        if isinstance(chunk, int) and chunk < 3:
            return i * 12 + chunk * 4 + j
        if isinstance(chunk, int) and chunk == 3:
            return 48 + i * 4 + j
        raise ValueError

    def up_block(part, i, j):
        return 64 + i * 16 + part * 4 + j

    def down_block(part, i, j):
        return 128 + part * 16 + i * 4 + j

    def fetch(buffer, block):
        for i in range(4):
            for j in range(4):
                pltpu.make_async_copy(
                    blocks_ref.at[slot_ref[block(i, j)]], stage.at[buffer, i * 4 + j], stage_sem.at[buffer]
                ).start()

    def settle(buffer):
        pltpu.make_async_copy(stage.at[buffer], stage.at[buffer], stage_sem.at[buffer]).wait()

    def assemble(buffer, dst):
        def row_block(i, carry):
            for j in range(4):
                tile = i * 4 + j
                top = pl.ds(pl.multiple_of(i * BLK, 64), HALF)
                low = pl.ds(pl.multiple_of(i * BLK + HALF, 32), HALF)
                dst[top, j * BLK : (j + 1) * BLK] = stage[buffer, tile, :, 0:BLK]
                dst[low, j * BLK : (j + 1) * BLK] = stage[buffer, tile, :, BLK:WIDE]
            return carry

        lax.fori_loop(0, 4, row_block, 0)

    def emit_wait(buffer):
        pltpu.make_async_copy(emit.at[buffer], emit.at[buffer], emit_sem.at[buffer]).wait()

    def emit_rows(buffer, i, value):
        low = value.astype(BF16)
        for j in range(4):
            emit[buffer, i * 4 + j, :, 0:BLK] = low[0:HALF, j * BLK : (j + 1) * BLK]
            emit[buffer, i * 4 + j, :, BLK:WIDE] = low[HALF:BLK, j * BLK : (j + 1) * BLK]

    def emit_send(buffer, block):
        for i in range(4):
            for j in range(4):
                pltpu.make_async_copy(
                    emit.at[buffer, i * 4 + j], parts_ref.at[slot_ref[block(i, j)]], emit_sem.at[buffer]
                ).start()

    def weight_grad(buffer, left, right, block):
        total = dot_tn(left, right)
        for i in range(4):
            emit_rows(buffer, i, total[i * BLK : (i + 1) * BLK])
        emit_send(buffer, block)

    fetch(0, functools.partial(block_of, 0))
    fetch(1, functools.partial(block_of, 1))
    for t in range(tiles):
        for e in range(2):
            step = step_ref[first_tile + t, 0] if e == 0 else step_ref[first_tile + t, split_ref[first_tile + t]]
            pltpu.make_async_copy(table_ref.at[step // 16], table_rows.at[t * 2 + e], table_sem).start()

    if len(vec_ref.shape) == 3:
        for owner in range(vec_ref.shape[0]):
            par[0:12, owner * 96 : (owner + 1) * 96] = vec_ref[owner, 0:12, 0:96].astype(BF16).astype(F32)
    else:
        par[0:12, :] = vec_ref[...].astype(BF16).astype(F32)
    dpar[...] = jnp.zeros_like(dpar)

    def param(row):
        return par[row : row + 1, :]

    def add_grad(row, value):
        dpar[row : row + 1, :] = dpar[row : row + 1, :] + value

    def col_sum(value):
        return jnp.sum(value.astype(F32), 0, keepdims=True)

    pltpu.make_async_copy(table_rows, table_rows, table_sem).wait()
    rows_iota = lax.broadcasted_iota(jnp.int32, (16, D), 0)
    for t in range(tiles):
        for e in range(2):
            step = step_ref[first_tile + t, 0] if e == 0 else step_ref[first_tile + t, split_ref[first_tile + t]]
            chosen = jnp.sum(jnp.where(rows_iota == step % 16, table_rows[t * 2 + e].astype(F32), 0.0), 0, keepdims=True)
            span = slice(t * TILE + e * 64, t * TILE + (e + 1) * 64)
            value = tok_ref[span, :].astype(F32) + chosen
            h0[span, :] = value
            hat, _ = normalised(value)
            a[span, :] = (hat * param(0) + param(2)).astype(BF16)

    for n in range(3):
        settle(n % 2)
        assemble(n % 2, w_qkv.at[n])
        if n == 0:
            fetch(0, functools.partial(block_of, 2))
        elif n == 1:
            fetch(1, functools.partial(block_of, 3))
        else:
            fetch(0, functools.partial(up_block, 0))
        for m in range(row_tiles):
            span = slice(m * ROWS, (m + 1) * ROWS)
            value = dot_nn(a[span, :], w_qkv[n])
            if n == 0:
                value = value + param(4)
            elif n == 2:
                value = value + param(5)
            qkv[n, span, :] = value.astype(BF16)
    settle(1)
    assemble(1, w_out)
    fetch(1, functools.partial(down_block, 0))

    lane = lax.broadcasted_iota(jnp.int32, (TILE, TILE), 1)
    first_head = lane < HD
    row_half = lax.broadcasted_iota(jnp.int32, (2 * TILE, TILE), 0) % TILE // (TILE // 2)
    col_half = lax.broadcasted_iota(jnp.int32, (2 * TILE, TILE), 1) // (TILE // 2)
    same_half = row_half == col_half

    def both(value):
        zero = jnp.zeros_like(value)
        return jnp.concatenate([jnp.where(first_head, value, zero), jnp.where(first_head, zero, value)], 0)

    def side(value):
        return jnp.concatenate([value[0:TILE], value[TILE : 2 * TILE]], 1)

    def attend(t, carry):
        whole = split_ref[first_tile + t] == 0
        allowed = jnp.logical_or(same_half, whole)
        span = pl.ds(pl.multiple_of(t * TILE, TILE), TILE)
        for p in range(HEADS // 2):
            cols = slice(p * TILE, (p + 1) * TILE)
            score = dot_nt(both(qkv[0, span, cols]), qkv[1, span, cols]) * score_scale
            score = jnp.where(allowed, score, masked_score)
            exponent = jnp.exp(score - jnp.max(score, -1, keepdims=True))
            weight = (exponent * (1.0 / jnp.sum(exponent, -1, keepdims=True))).astype(BF16)
            prob[t, p] = weight
            mixed[span, cols] = dot_nn(side(weight), both(qkv[2, span, cols])).astype(BF16)
        return carry

    lax.fori_loop(0, tiles, attend, 0)

    for m in range(row_tiles):
        span = slice(m * ROWS, (m + 1) * ROWS)
        value = h0[span, :] + (dot_nn(mixed[span, :], w_out[...]) + param(6))
        h1[span, :] = value
        hat, _ = normalised(value)
        c[span, :] = (hat * param(1) + param(3)).astype(BF16)
        acc_o[span, :] = value + param(7)
        acc_d[span, :] = jnp.zeros_like(value)

    def feed(part, carry):
        settle(0)
        assemble(0, w_up)

        @pl.when(part < 3)
        def _():
            fetch(0, functools.partial(up_block, part + 1))

        settle(1)
        assemble(1, w_down)

        @pl.when(part < 3)
        def _():
            fetch(1, functools.partial(down_block, part + 1))

        bias = par[pl.ds(8 + part, 1), :]
        bias_grad = jnp.zeros((1, D), F32)
        for m in range(row_tiles):
            span = slice(m * ROWS, (m + 1) * ROWS)
            upper = dot_nn(c[span, :], w_up[...]) + bias
            back = dot_nt(grad_ref[span, :], w_down[...])
            below = 0.5 + 0.5 * lax.erf(upper * 0.7071067811865476)
            density = jnp.exp(upper * upper * -0.5) * 0.3989422804014327
            active = (upper * below).astype(BF16)
            grad_upper = (back * (below + upper * density)).astype(BF16)
            r[span, :] = active
            du[span, :] = grad_upper
            bias_grad = bias_grad + col_sum(grad_upper)
            acc_o[span, :] = acc_o[span, :] + dot_nn(active, w_down[...])
            acc_d[span, :] = acc_d[span, :] + dot_nt(grad_upper, w_up[...])
        dpar[pl.ds(8 + part, 1), :] = bias_grad

        @pl.when(part > 0)
        def _():
            emit_wait(0)
            emit_wait(1)

        weight_grad(0, r[...], grad_ref[...], functools.partial(down_block, part))
        weight_grad(1, c[...], du[...], functools.partial(up_block, part))
        return carry

    lax.fori_loop(0, 4, feed, 0)

    for m in range(row_tiles):
        span = slice(m * ROWS, (m + 1) * ROWS)
        out_ref[span, :] = acc_o[span, :].astype(BF16)
        hat, scale = normalised(h1[span, :])
        cotangent = acc_d[span, :]
        upstream = grad_ref[span, :].astype(F32)
        add_grad(1, col_sum(cotangent * hat))
        add_grad(3, col_sum(cotangent))
        add_grad(7, col_sum(upstream))
        value = upstream + norm_back(cotangent, hat, scale, param(1))
        acc_d[span, :] = value
        rounded = value.astype(BF16)
        c[span, :] = rounded
        add_grad(6, col_sum(rounded))
        r[span, :] = dot_nt(rounded, w_out[...]).astype(BF16)
    emit_wait(0)
    weight_grad(0, mixed[...], c[...], functools.partial(block_of, 3))

    def attend_back(t, carry):
        span = pl.ds(pl.multiple_of(t * TILE, TILE), TILE)
        for p in range(HEADS // 2):
            cols = slice(p * TILE, (p + 1) * TILE)
            cotangent = both(r[span, cols])
            weight = prob[t, p]
            wide = weight.astype(F32)
            back = dot_nt(cotangent, qkv[2, span, cols])
            score_grad = (wide * (back - jnp.sum(wide * back, -1, keepdims=True))).astype(BF16)
            dqkv[0, span, cols] = (dot_nn(side(score_grad), both(qkv[1, span, cols])) * score_scale).astype(BF16)
            dqkv[1, span, cols] = (dot_tn(score_grad, both(qkv[0, span, cols])) * score_scale).astype(BF16)
            dqkv[2, span, cols] = dot_tn(weight, cotangent).astype(BF16)
        return carry

    lax.fori_loop(0, tiles, attend_back, 0)

    for n in range(3):
        emit_wait((n + 1) % 2)
        weight_grad((n + 1) % 2, a[...], dqkv[n], functools.partial(block_of, n))
    add_grad(4, col_sum(dqkv[0]))
    add_grad(5, col_sum(dqkv[2]))
    for m in range(row_tiles):
        span = slice(m * ROWS, (m + 1) * ROWS)
        cotangent = dot_nt(dqkv[0, span, :], w_qkv[0]) + dot_nt(dqkv[1, span, :], w_qkv[1]) + dot_nt(dqkv[2, span, :], w_qkv[2])
        hat, scale = normalised(h0[span, :])
        add_grad(0, col_sum(cotangent * hat))
        add_grad(2, col_sum(cotangent))
        in_grad_ref[span, :] = (acc_d[span, :] + norm_back(cotangent, hat, scale, param(0))).astype(BF16)
    if len(dvec_ref.shape) == 3:
        dvec_ref[...] = jnp.zeros_like(dvec_ref)
        for owner in range(dvec_ref.shape[0]):
            dvec_ref[owner, 0:12, 0:96] = dpar[0:12, owner * 96 : (owner + 1) * 96]
    else:
        dvec_ref[...] = dpar[0:12, :]
    emit_wait(0)
    emit_wait(1)


def run_layer(tokens, out_grad, table, time_step, tile_split, block_slot, blocks, vecs):
    tok_rows = tokens.shape[0]
    tiles = tok_rows // TILE
    smem = pl.BlockSpec(memory_space=pltpu.SMEM)
    vmem = pl.BlockSpec(memory_space=pltpu.VMEM)
    hbm = pl.BlockSpec(memory_space=pl.ANY)
    dvec_shape = vecs.shape
    return pl.pallas_call(
        layer_kernel,
        out_shape=(
            jax.ShapeDtypeStruct((tok_rows, D), BF16),
            jax.ShapeDtypeStruct((tok_rows, D), BF16),
            jax.ShapeDtypeStruct((NBLK, HALF, WIDE), BF16),
            jax.ShapeDtypeStruct(dvec_shape, F32),
        ),
        in_specs=[smem, smem, smem, vmem, vmem, hbm, hbm, vmem],
        out_specs=(vmem, vmem, hbm, vmem),
        scratch_shapes=[
            pltpu.VMEM((16, D), F32),
            pltpu.VMEM((16, D), F32),
            pltpu.VMEM((2 * tiles, 16, D), BF16),
            pltpu.VMEM((tok_rows, D), F32),
            pltpu.VMEM((tok_rows, D), BF16),
            pltpu.VMEM((3, tok_rows, D), BF16),
            pltpu.VMEM((tiles, HEADS // 2, 2 * TILE, TILE), BF16),
            pltpu.VMEM((tok_rows, D), BF16),
            pltpu.VMEM((tok_rows, D), F32),
            pltpu.VMEM((tok_rows, D), BF16),
            pltpu.VMEM((tok_rows, D), F32),
            pltpu.VMEM((tok_rows, D), F32),
            pltpu.VMEM((tok_rows, D), BF16),
            pltpu.VMEM((tok_rows, D), BF16),
            pltpu.VMEM((3, tok_rows, D), BF16),
            pltpu.VMEM((3, D, D), BF16),
            pltpu.VMEM((D, D), BF16),
            pltpu.VMEM((D, D), BF16),
            pltpu.VMEM((D, D), BF16),
            pltpu.VMEM((2, 16, HALF, WIDE), BF16),
            pltpu.VMEM((2, 16, HALF, WIDE), BF16),
            pltpu.SemaphoreType.DMA,
            pltpu.SemaphoreType.DMA((2,)),
            pltpu.SemaphoreType.DMA((2,)),
        ],
        compiler_params=pltpu.CompilerParams(vmem_limit_bytes=60 * MIB),
        name="layer",
    )(time_step, tile_split, block_slot, tokens, out_grad, table.reshape(-1, 16, D), blocks, vecs)


def step_kernel(
    items_count, sum_ref, vsum_ref, weight_ref, momentum_ref, left_ref, right_ref, root_l_ref, root_r_ref,
    vec_ref, first_ref, second_ref,
    grad_out, momentum_out, weight_out, left_out, right_out, vgrad_out, first_out, second_out, vec_out,
):
    inverse = 1.0 / items_count
    for s in range(sum_ref.shape[0]):
        packed = sum_ref[s]
        low = jnp.concatenate([packed[:, 0:BLK], packed[:, BLK:WIDE]], 0)
        grad = low.astype(F32) * inverse
        low = grad.astype(BF16)
        grad_out[s] = grad
        momentum = 0.9 * momentum_ref[s] + grad
        momentum_out[s] = momentum
        left_out[s] = 0.95 * left_ref[s] + 0.05 * dot_nt(low, low)
        right_out[s] = 0.95 * right_ref[s] + 0.05 * dot_tn(low, low)
        direction = jnp.dot(root_l_ref[s], momentum, precision=highest, preferred_element_type=F32)
        direction = jnp.dot(direction, root_r_ref[s], precision=highest, preferred_element_type=F32)
        weight = weight_ref[s]
        scale = jnp.sqrt(jnp.mean(weight * weight) + 1e-06) * lax.rsqrt(jnp.mean(direction * direction) + 1e-06)
        weight_out[s] = weight - (0.3 * scale) * direction

    @pl.when(pl.program_id(0) == 0)
    def _():
        rows, cols = vec_ref.shape
        grad = vsum_ref[0:rows, 0:cols] * inverse
        vgrad_out[...] = grad
        first = 0.9 * first_ref[...] + 0.1 * grad
        second = 0.999 * second_ref[...] + 0.001 * grad * grad
        first_out[...] = first
        second_out[...] = second
        vec_out[...] = vec_ref[...] - 0.1 * first / (jnp.sqrt(second) + 1e-08)


def run_step(items_count, sums, vsums, weights, momentum, left, right, root_l, root_r, vectors, first, second):
    count = weights.shape[0]
    per = 3
    block = pl.BlockSpec((per, BLK, BLK), lambda i: (i, 0, 0))
    packed = pl.BlockSpec((per, HALF, WIDE), lambda i: (i, 0, 0))
    small = pl.BlockSpec(vectors.shape, lambda i: (0, 0))
    vsum = pl.BlockSpec(vsums.shape, lambda i: (0, 0))
    slots = jax.ShapeDtypeStruct(weights.shape, F32)
    vec = jax.ShapeDtypeStruct(vectors.shape, F32)
    return pl.pallas_call(
        functools.partial(step_kernel, items_count),
        grid=(count // per,),
        out_shape=(slots,) * 5 + (vec,) * 4,
        in_specs=[packed, vsum] + [block] * 6 + [small] * 3,
        out_specs=[block] * 5 + [small] * 4,
        compiler_params=pltpu.CompilerParams(vmem_limit_bytes=40 * MIB),
        name="step",
    )(sums, vsums, weights, momentum, left, right, root_l, root_r, vectors, first, second)


def body(
    tokens, out_grad, time_table, time_step, tile_split, block_slot, weight_slots, momentum_slots,
    stat_left, stat_right, root_left, root_right, vectors, vector_first, vector_second,
):
    items_count = lax.axis_size("items")
    known = items_count == 8 and lax.axis_size("seq") == 4
    if known:
        blocks, vecs = gather_weights(weight_slots, vectors)
        blocks = blocks.reshape(NBLK, HALF, WIDE)
    else:
        low = weight_slots.astype(BF16)
        blocks = lax.all_gather(jnp.concatenate([low[:, :HALF], low[:, HALF:]], 2), "items", axis=0, tiled=True)
        vecs = lax.all_gather(vectors, "items", axis=1, tiled=True)
    output, input_grad, parts, dvec = run_layer(
        tokens, out_grad, time_table, time_step, tile_split, block_slot, blocks, vecs
    )
    if known:
        sums, vsums = scatter_sums(parts.reshape(8, 24, HALF, WIDE), dvec)
    else:
        sums = lax.psum_scatter(parts.astype(F32), "items", scatter_dimension=0, tiled=True)
        vsums = lax.psum_scatter(dvec, "items", scatter_dimension=1, tiled=True)
        sums, vsums = lax.psum((sums, vsums), "seq")
    stepped = run_step(
        items_count, sums, vsums, weight_slots, momentum_slots, stat_left, stat_right, root_left, root_right,
        vectors, vector_first, vector_second,
    )
    grad, momentum, weights, left, right, vgrad, first, second, vecs_new = stepped
    return output, input_grad, grad, momentum, weights, left, right, vgrad, first, second, vecs_new


def solution(mesh):
    return jax.shard_map(
        body,
        mesh=mesh,
        in_specs=(
            P(("items", "seq"), None),
            P(("items", "seq"), None),
            P(),
            P("items", None),
            P("items"),
            P(),
            P("items", None, None),
            P("items", None, None),
            P("items", None, None),
            P("items", None, None),
            P("items", None, None),
            P("items", None, None),
            P(None, "items"),
            P(None, "items"),
            P(None, "items"),
        ),
        out_specs=(
            P(("items", "seq"), None),
            P(("items", "seq"), None),
            P("items", None, None),
            P("items", None, None),
            P("items", None, None),
            P("items", None, None),
            P("items", None, None),
            P(None, "items"),
            P(None, "items"),
            P(None, "items"),
            P(None, "items"),
        ),
        check_vma=False,
    )
```

```python
import functools
import jax
import jax.numpy as jnp
from jax import lax
from jax.experimental import pallas as pl
from jax.experimental.pallas import tpu as pltpu
from jax.sharding import PartitionSpec as P

D = 768
HEADS = 12
HD = 64
TILE = 128
BLK = 192
NBLK = 192
HALF = 96
WIDE = 384
MESH = pl.DeviceIdType.MESH
BF16 = jnp.bfloat16
F32 = jnp.float32
MIB = 2 ** 20
highest = lax.Precision.HIGHEST
masked_score = -1000000000.0
norm_epsilon = 1e-05
score_scale = HD ** (-0.5)


def place():
    it = lax.axis_index("items")
    sq = lax.axis_index("seq")
    return it // 2, it % 2, sq // 2, sq % 2


def greet(partners):
    barrier = pltpu.get_barrier_semaphore()
    for partner in partners:
        pl.semaphore_signal(barrier, inc=1, device_id=partner, device_id_type=MESH)
    pl.semaphore_wait(barrier, len(partners))


class Copies:
    def __init__(self, send_sem, recv_sem):
        self.send_sem, self.recv_sem = send_sem, recv_sem
        self.sent = []

    def start(self, index, src, dst, device):
        made = pltpu.make_async_remote_copy(
            src_ref=src, dst_ref=dst,
            send_sem=self.send_sem.at[index], recv_sem=self.recv_sem.at[index],
            device_id=device, device_id_type=MESH,
        )
        made.start()
        self.sent.append(made)

    def wait(self, index, dst, device):
        pltpu.make_async_remote_copy(
            src_ref=dst, dst_ref=dst,
            send_sem=self.send_sem.at[index], recv_sem=self.recv_sem.at[index],
            device_id=device, device_id_type=MESH,
        ).wait_recv()

    def finish(self):
        for made in self.sent:
            made.wait_send()


GATHER_X_FIRST = (True, False, True, False, True, False)


def gather_kernel(slots_ref, vec_ref, blocks_ref, vecs_ref, raw, own, vec_own, raw_sem, own_sem, vec_sem, send_sem, recv_sem, vsend, vrecv):
    z, x, y, c = place()
    me = z * 2 + x
    quarter = y * 2 + c
    across_x = (z * 2 + (1 - x), quarter)
    across_y = (me, (1 - y) * 2 + c)
    across_c = (me, y * 2 + (1 - c))
    far = [(z + d) % 4 for d in (1, 2, 3)]
    along_z = [(f * 2 + x, quarter) for f in far]
    others = along_z + [(f * 2 + (1 - x), quarter) for f in far] + [across_x]

    def loads(j):
        slot = (quarter * 6 + j * 6) % 24
        return pltpu.make_async_copy(slots_ref.at[pl.ds(slot, 6)], raw.at[pl.ds(slot, 6)], raw_sem.at[j])

    for j in range(4):
        loads(j).start()
    greet(others + [across_y, across_c])
    copies = Copies(send_sem, recv_sem)
    vcopies = Copies(vsend, vrecv)
    vec_own[...] = jnp.zeros_like(vec_own)
    vec_own[0:12, 0:96] = vec_ref[...]
    for i, d in enumerate((1, 2, 3)):
        vcopies.start(i, vec_own, vecs_ref.at[me], along_z[i])
        vcopies.start(3 + i, vec_own, vecs_ref.at[me], (far[i] * 2 + (1 - x), quarter))
    vcopies.start(6, vec_own, vecs_ref.at[me], across_x)

    def cast(slot):
        own[slot, :, 0:192] = raw[slot, 0:HALF, :].astype(BF16)
        own[slot, :, 192:384] = raw[slot, HALF:BLK, :].astype(BF16)

    base = quarter * 6
    base_y = ((1 - y) * 2 + c) * 6
    def send_z(k):
        slot = base + k
        for i in range(3):
            copies.start((k, i), own.at[slot], blocks_ref.at[me, slot], along_z[i])

    def core(k, index, owner, slot):
        copies.start((k, index), blocks_ref.at[owner, slot], blocks_ref.at[owner, slot], across_c)

    def phase_two(k):
        slot = base + k
        for i in range(3):
            owner = ((z - (i + 1)) % 4) * 2 + x
            ref = blocks_ref.at[owner, slot]
            copies.wait((k, i), ref, along_z[i])
            if GATHER_X_FIRST[k]:
                copies.start((k, 4 + i), ref, ref, across_x)
                copies.start((k, 7 + i), ref, ref, across_y)
            else:
                copies.start((k, 3 + i), ref, ref, across_y)
                copies.start((k, 8 + i), ref, ref, across_x)
            core(k, 14 + i, owner, slot)

    def early(k):
        slot = base + k
        if GATHER_X_FIRST[k]:
            copies.start((k, 3), own.at[slot], blocks_ref.at[me, slot], across_x)
        else:
            copies.start((k, 6), own.at[slot], blocks_ref.at[me, slot], across_x)
            slot_y = base_y + k
            copies.start((k, 7), own.at[slot_y], blocks_ref.at[me, slot_y], across_x)

    def phase_three(k):
        slot = base + k
        slot_y = base_y + k
        if GATHER_X_FIRST[k]:
            for p in range(4):
                owner = ((z - p) % 4) * 2 + (1 - x)
                ref = blocks_ref.at[owner, slot]
                copies.wait((k, 3 + p), ref, across_x)
                copies.start((k, 10 + p), ref, ref, across_y)
                core(k, 17 + p, owner, slot)
        else:
            for i in range(3):
                owner = ((z - (i + 1)) % 4) * 2 + x
                ref = blocks_ref.at[owner, slot_y]
                copies.wait((k, 3 + i), ref, across_y)
                copies.start((k, 11 + i), ref, ref, across_x)
                core(k, 17 + i, owner, slot_y)

    def phase_four(k):
        slot = base + k
        slot_y = base_y + k
        if GATHER_X_FIRST[k]:
            for i in range(3):
                owner = ((z - (i + 1)) % 4) * 2 + x
                copies.wait((k, 7 + i), blocks_ref.at[owner, slot_y], across_y)
                core(k, 21 + i, owner, slot_y)
            for p in range(4):
                owner = ((z - p) % 4) * 2 + (1 - x)
                copies.wait((k, 10 + p), blocks_ref.at[owner, slot_y], across_y)
                core(k, 24 + p, owner, slot_y)
        else:
            mine = z * 2 + (1 - x)
            copies.wait((k, 6), blocks_ref.at[mine, slot], across_x)
            core(k, 20, mine, slot)
            copies.wait((k, 7), blocks_ref.at[mine, slot_y], across_x)
            core(k, 21, mine, slot_y)
            for i in range(3):
                owner = ((z - (i + 1)) % 4) * 2 + (1 - x)
                copies.wait((k, 8 + i), blocks_ref.at[owner, slot], across_x)
                core(k, 22 + i, owner, slot)
            for i in range(3):
                owner = ((z - (i + 1)) % 4) * 2 + (1 - x)
                copies.wait((k, 11 + i), blocks_ref.at[owner, slot_y], across_x)
                core(k, 25 + i, owner, slot_y)

    base_c = (y * 2 + (1 - c)) * 6
    base_yc = ((1 - y) * 2 + (1 - c)) * 6

    def core_waits(k):
        slot_c = base_c + k
        slot_yc = base_yc + k
        def w(index, owner, slot):
            copies.wait((k, index), blocks_ref.at[owner, slot], across_c)
        same = [((z - (i + 1)) % 4) * 2 + x for i in range(3)]
        cross = [((z - p) % 4) * 2 + (1 - x) for p in range(4)]
        for i in range(3):
            w(14 + i, same[i], slot_c)
        if GATHER_X_FIRST[k]:
            for p in range(4):
                w(17 + p, cross[p], slot_c)
            for i in range(3):
                w(21 + i, same[i], slot_yc)
            for p in range(4):
                w(24 + p, cross[p], slot_yc)
        else:
            for i in range(3):
                w(17 + i, same[i], slot_yc)
            w(20, cross[0], slot_c)
            w(21, cross[0], slot_yc)
            for i in range(3):
                w(22 + i, cross[1 + i], slot_c)
            for i in range(3):
                w(25 + i, cross[1 + i], slot_yc)

    steps = 6
    loads(0).wait()
    for k in range(2):
        cast(base + k)
        send_z(k)
    for k in range(2, steps):
        cast(base + k)
    loads(2).wait()
    for k in range(steps):
        cast(base_y + k)
    for k in range(steps):
        early(k)
    for t in range(steps + 2):
        if t < steps:
            phase_two(t)
            if t + 2 < steps:
                send_z(t + 2)
        if 1 <= t <= steps:
            phase_three(t - 1)
        if t == 0:
            loads(1).wait()
            loads(3).wait()
            lax.fori_loop(0, 6, lambda k, carry: (cast(base_c + k), cast(base_yc + k), carry)[2], 0)
            local = pltpu.make_async_copy(own, blocks_ref.at[me], own_sem)
            local.start()
            local_vec = pltpu.make_async_copy(vec_own, vecs_ref.at[me], vec_sem)
            local_vec.start()
        if t >= 2:
            phase_four(t - 2)
    for k in range(steps):
        core_waits(k)
    local.wait()
    local_vec.wait()
    for i in range(3):
        vcopies.wait(i, vecs_ref.at[((z - (i + 1)) % 4) * 2 + x], along_z[i])
        vcopies.wait(3 + i, vecs_ref.at[((z - (i + 1)) % 4) * 2 + (1 - x)], along_z[i])
    vcopies.wait(6, vecs_ref.at[z * 2 + (1 - x)], across_x)
    copies.finish()
    vcopies.finish()


def gather_weights(slots, vectors):
    return pl.pallas_call(
        gather_kernel,
        out_shape=(
            jax.ShapeDtypeStruct((8, 24, HALF, WIDE), BF16),
            jax.ShapeDtypeStruct((8, 16, 128), F32),
        ),
        in_specs=[pl.BlockSpec(memory_space=pl.ANY), pl.BlockSpec(memory_space=pltpu.VMEM)],
        out_specs=(pl.BlockSpec(memory_space=pl.ANY), pl.BlockSpec(memory_space=pl.ANY)),
        scratch_shapes=[
            pltpu.VMEM((24, BLK, BLK), F32),
            pltpu.VMEM((24, HALF, WIDE), BF16),
            pltpu.VMEM((16, 128), F32),
            pltpu.SemaphoreType.DMA((4,)),
            pltpu.SemaphoreType.DMA,
            pltpu.SemaphoreType.DMA,
            pltpu.SemaphoreType.DMA((6, 28)),
            pltpu.SemaphoreType.DMA((6, 28)),
            pltpu.SemaphoreType.DMA((7,)),
            pltpu.SemaphoreType.DMA((7,)),
        ],
        compiler_params=pltpu.CompilerParams(collective_id=0, has_side_effects=True, vmem_limit_bytes=60 * MIB),
        name="gather_weights",
    )(slots, vectors)


UNIT = 48
UNITS = 12
SCATTER_Y_FIRST = (True, False) * 6
SCATTER_AHEAD = 4
SCATTER_LOOK = 1


def scatter_kernel(part_ref, vec_ref, sum_ref, vsum_ref, acc, from_c, from_y, from_x, from_z, fin, va, vb, vz, vload_sem, load_sem, out_sem, send_sem, recv_sem, vsend, vrecv):
    z, x, y, c = place()
    me = z * 2 + x
    quarter = y * 2 + c
    across_x = (z * 2 + (1 - x), quarter)
    across_y = (me, (1 - y) * 2 + c)
    across_c = (me, y * 2 + (1 - c))
    far = [(z + d) % 4 for d in (1, 2, 3)]
    along_z = [(f * 2 + x, quarter) for f in far]
    steps = UNITS

    def rows(k):
        return pl.ds(k % 2 * UNIT, UNIT)

    def load(k, yy):
        slot = (yy * 2 + c) * 6 + k // 2
        return pltpu.make_async_copy(part_ref.at[:, slot, rows(k)], acc.at[k, yy], load_sem.at[k, yy])

    for k in range(steps):
        for yy in range(2):
            load(k, yy).start()
    greet([across_x, across_y, across_c] + along_z)
    copies = Copies(send_sem, recv_sem)
    vcopies = Copies(vsend, vrecv)

    def core_send(k):
        for yy in range(2):
            slot = (yy * 2 + (1 - c)) * 6 + k // 2
            copies.start((k, yy), part_ref.at[:, slot, rows(k)], from_c.at[k, yy], across_c)

    for k in range(SCATTER_AHEAD):
        core_send(k)
    vec_load = pltpu.make_async_copy(vec_ref, vb.at[0], vload_sem)
    vec_load.start()
    vcopies.start(0, vec_ref, va, across_c)

    def core_add(k):
        for yy in range(2):
            load(k, yy).wait()
            copies.wait((k, yy), from_c.at[k, yy], across_c)

        def owner_add(o, carry):
            for yy in range(2):
                acc[k, yy, o] = acc[k, yy, o] + from_c[k, yy, o]
            return carry

        lax.fori_loop(0, 8, owner_add, 0)
        if SCATTER_Y_FIRST[k]:
            copies.start((k, 2), acc.at[k, 1 - y], from_y.at[k], across_y)
        else:
            for yy in range(2):
                for zz in range(4):
                    copies.start((k, 2 + yy * 4 + zz), acc.at[k, yy, zz * 2 + (1 - x)], from_x.at[k, yy, zz], across_x)

    def second_add(k):
        if SCATTER_Y_FIRST[k]:
            copies.wait((k, 2), from_y.at[k], across_y)

            def owner_add(o, carry):
                acc[k, y, o] = acc[k, y, o] + from_y[k, o]
                return carry

            lax.fori_loop(0, 8, owner_add, 0)
            for zz in range(4):
                copies.start((k, 3 + zz), acc.at[k, y, zz * 2 + (1 - x)], from_x.at[k, 0, zz], across_x)
        else:
            for yy in range(2):
                for zz in range(4):
                    copies.wait((k, 2 + yy * 4 + zz), from_x.at[k, yy, zz], across_x)

            def z_add(zz, carry):
                for yy in range(2):
                    acc[k, yy, zz * 2 + x] = acc[k, yy, zz * 2 + x] + from_x[k, yy, zz]
                return carry

            lax.fori_loop(0, 4, z_add, 0)
            for zz in range(4):
                copies.start((k, 10 + zz), acc.at[k, 1 - y, zz * 2 + x], from_y.at[k, zz], across_y)

    def third_add(k):
        if SCATTER_Y_FIRST[k]:
            for zz in range(4):
                copies.wait((k, 3 + zz), from_x.at[k, 0, zz], across_x)

            def z_add(zz, carry):
                acc[k, y, zz * 2 + x] = acc[k, y, zz * 2 + x] + from_x[k, 0, zz]
                return carry
        else:
            for zz in range(4):
                copies.wait((k, 10 + zz), from_y.at[k, zz], across_y)

            def z_add(zz, carry):
                acc[k, y, zz * 2 + x] = acc[k, y, zz * 2 + x] + from_y[k, zz]
                return carry

        lax.fori_loop(0, 4, z_add, 0)
        for i in range(3):
            copies.start((k, 14 + i), acc.at[k, y, far[i] * 2 + x], from_z.at[k, i], along_z[i])

    def last_add(k):
        for i in range(3):
            copies.wait((k, 14 + i), from_z.at[k, i], along_z[i])
        total = acc[k, y, me].astype(F32)
        for i in range(3):
            total = total + from_z[k, i].astype(F32)
        slot = quarter * 6 + k // 2
        fin[slot, rows(k)] = total.astype(BF16)
        copies.start((k, 17), fin.at[slot, rows(k)], fin.at[slot, rows(k)], across_y)
        copies.start((k, 18), fin.at[slot, rows(k)], fin.at[slot, rows(k)], across_c)
        pltpu.make_async_copy(fin.at[slot, rows(k)], sum_ref.at[slot, rows(k)], out_sem.at[k, 0]).start()

    def spread(k):
        slot_y = ((1 - y) * 2 + c) * 6 + k // 2
        copies.wait((k, 17), fin.at[slot_y, rows(k)], across_y)
        copies.start((k, 19), fin.at[slot_y, rows(k)], fin.at[slot_y, rows(k)], across_c)
        pltpu.make_async_copy(fin.at[slot_y, rows(k)], sum_ref.at[slot_y, rows(k)], out_sem.at[k, 1]).start()

    def spread_core(k):
        for j, (yy, index) in enumerate(((y, 18), (1 - y, 19))):
            slot = (yy * 2 + (1 - c)) * 6 + k // 2
            copies.wait((k, index), fin.at[slot, rows(k)], across_c)
            pltpu.make_async_copy(fin.at[slot, rows(k)], sum_ref.at[slot, rows(k)], out_sem.at[k, 2 + j]).start()

    def vec_step(t):
        if t == 0:
            vcopies.wait(0, va, across_c)
            vec_load.wait()
            va[...] = va[...] + vb[0]
            vcopies.start(1, va, vb.at[1], across_y)
        elif t == 1:
            vcopies.wait(1, vb.at[1], across_y)
            vb[1] = va[...] + vb[1]
            vcopies.start(2, vb.at[1], vb.at[2], across_x)
        elif t == 2:
            vcopies.wait(2, vb.at[2], across_x)
            vb[3] = vb[1] + vb[2]
            for i in range(3):
                vcopies.start(3 + i, vb.at[3, far[i] * 2 + x], vz.at[i], along_z[i])
        elif t == 3:
            for i in range(3):
                vcopies.wait(3 + i, vz.at[i], along_z[i])
            vsum_ref[...] = vb[3, me] + vz[0] + vz[1] + vz[2]

    def core_step(k):
        core_add(k)
        if k + SCATTER_AHEAD < steps:
            core_send(k + SCATTER_AHEAD)

    for t in range(SCATTER_LOOK):
        core_step(t)
    for t in range(steps + 5):
        if t + SCATTER_LOOK < steps:
            core_step(t + SCATTER_LOOK)
        if 1 <= t <= steps:
            second_add(t - 1)
        if 2 <= t <= steps + 1:
            third_add(t - 2)
        if 3 <= t <= steps + 2:
            last_add(t - 3)
        if 4 <= t <= steps + 3:
            spread(t - 4)
        if 5 <= t:
            spread_core(t - 5)
        vec_step(t)
    for k in range(steps):
        for j in range(4):
            pltpu.make_async_copy(fin.at[0, rows(k)], sum_ref.at[0, rows(k)], out_sem.at[k, j]).wait()
    copies.finish()
    vcopies.finish()


def scatter_sums(parts, vecs):
    return pl.pallas_call(
        scatter_kernel,
        out_shape=(
            jax.ShapeDtypeStruct((24, HALF, WIDE), BF16),
            jax.ShapeDtypeStruct((16, 128), F32),
        ),
        in_specs=[pl.BlockSpec(memory_space=pltpu.HBM), pl.BlockSpec(memory_space=pltpu.HBM)],
        out_specs=(pl.BlockSpec(memory_space=pl.ANY), pl.BlockSpec(memory_space=pltpu.VMEM)),
        scratch_shapes=[
            pltpu.VMEM((UNITS, 2, 8, UNIT, WIDE), BF16),
            pltpu.VMEM((UNITS, 2, 8, UNIT, WIDE), BF16),
            pltpu.VMEM((UNITS, 8, UNIT, WIDE), BF16),
            pltpu.VMEM((UNITS, 2, 4, UNIT, WIDE), BF16),
            pltpu.VMEM((UNITS, 3, UNIT, WIDE), BF16),
            pltpu.VMEM((24, HALF, WIDE), BF16),
            pltpu.VMEM((8, 16, 128), F32),
            pltpu.VMEM((4, 8, 16, 128), F32),
            pltpu.VMEM((3, 16, 128), F32),
            pltpu.SemaphoreType.DMA,
            pltpu.SemaphoreType.DMA((UNITS, 2)),
            pltpu.SemaphoreType.DMA((UNITS, 4)),
            pltpu.SemaphoreType.DMA((UNITS, 20)),
            pltpu.SemaphoreType.DMA((UNITS, 20)),
            pltpu.SemaphoreType.DMA((6,)),
            pltpu.SemaphoreType.DMA((6,)),
        ],
        compiler_params=pltpu.CompilerParams(collective_id=1, has_side_effects=True, vmem_limit_bytes=50 * MIB),
        name="scatter_sums",
    )(parts, vecs)


def dot_nn(left, right):
    return jnp.dot(left, right, preferred_element_type=F32)


def dot_nt(left, right):
    return lax.dot_general(left, right, (((1,), (1,)), ((), ())), preferred_element_type=F32)


def dot_tn(left, right):
    return lax.dot_general(left, right, (((0,), (0,)), ((), ())), preferred_element_type=F32)


def normalised(values):
    average = jnp.mean(values, -1, keepdims=True)
    centred = values - average
    spread = jnp.mean(centred * centred, -1, keepdims=True)
    scale = lax.rsqrt(spread + norm_epsilon)
    return centred * scale, scale


def norm_back(cotangent, hat, scale, gain):
    inner = cotangent * gain
    first = jnp.mean(inner, -1, keepdims=True)
    second = jnp.mean(inner * hat, -1, keepdims=True)
    return scale * (inner - first - hat * second)


ROWS = 256
TOK_TILES_MAX = 8


def layer_kernel(
    time_ref, split_ref, slot_ref, tok_ref, grad_ref, table_ref, blocks_ref, vec_ref,
    out_ref, in_grad_ref, parts_ref, dvec_ref,
    step_ref, par, dpar, table_rows, h0, a, qkv, prob, mixed, h1, c, acc_o, acc_d, r, du, dqkv,
    w_qkv, w_out, w_up, w_down, stage, emit, step_sem, table_sem, stage_sem, emit_sem,
):
    tok_rows = tok_ref.shape[0]
    tiles = tok_rows // TILE
    row_tiles = tok_rows // ROWS
    first_tile = lax.axis_index("seq") * tiles

    def block_of(chunk, i, j):
        if isinstance(chunk, int) and chunk < 3:
            return i * 12 + chunk * 4 + j
        if isinstance(chunk, int) and chunk == 3:
            return 48 + i * 4 + j
        raise ValueError

    def up_block(part, i, j):
        return 64 + i * 16 + part * 4 + j

    def down_block(part, i, j):
        return 128 + part * 16 + i * 4 + j

    def fetch(buffer, block):
        for i in range(4):
            for j in range(4):
                pltpu.make_async_copy(
                    blocks_ref.at[slot_ref[block(i, j)]], stage.at[buffer, i * 4 + j], stage_sem.at[buffer]
                ).start()

    def settle(buffer):
        pltpu.make_async_copy(stage.at[buffer], stage.at[buffer], stage_sem.at[buffer]).wait()

    def assemble(buffer, dst):
        def row_block(i, carry):
            for j in range(4):
                tile = i * 4 + j
                top = pl.ds(pl.multiple_of(i * BLK, 64), HALF)
                low = pl.ds(pl.multiple_of(i * BLK + HALF, 32), HALF)
                dst[top, j * BLK : (j + 1) * BLK] = stage[buffer, tile, :, 0:BLK]
                dst[low, j * BLK : (j + 1) * BLK] = stage[buffer, tile, :, BLK:WIDE]
            return carry

        lax.fori_loop(0, 4, row_block, 0)

    def emit_wait(buffer):
        pltpu.make_async_copy(emit.at[buffer], emit.at[buffer], emit_sem.at[buffer]).wait()

    def emit_rows(buffer, i, value):
        low = value.astype(BF16)
        for j in range(4):
            emit[buffer, i * 4 + j, :, 0:BLK] = low[0:HALF, j * BLK : (j + 1) * BLK]
            emit[buffer, i * 4 + j, :, BLK:WIDE] = low[HALF:BLK, j * BLK : (j + 1) * BLK]

    def emit_send(buffer, block):
        for i in range(4):
            for j in range(4):
                pltpu.make_async_copy(
                    emit.at[buffer, i * 4 + j], parts_ref.at[slot_ref[block(i, j)]], emit_sem.at[buffer]
                ).start()

    def weight_grad(buffer, left, right, block):
        total = dot_tn(left, right)
        for i in range(4):
            emit_rows(buffer, i, total[i * BLK : (i + 1) * BLK])
        emit_send(buffer, block)

    steps_in = pltpu.make_async_copy(time_ref, step_ref, step_sem)
    steps_in.start()
    fetch(0, functools.partial(block_of, 0))
    fetch(1, functools.partial(block_of, 1))
    steps_in.wait()
    for t in range(tiles):
        for e in range(2):
            step = step_ref[0, first_tile + t] if e == 0 else step_ref[split_ref[first_tile + t], first_tile + t]
            pltpu.make_async_copy(table_ref.at[step // 16], table_rows.at[t * 2 + e], table_sem).start()

    if len(vec_ref.shape) == 3:
        for owner in range(vec_ref.shape[0]):
            par[0:12, owner * 96 : (owner + 1) * 96] = vec_ref[owner, 0:12, 0:96].astype(BF16).astype(F32)
    else:
        par[0:12, :] = vec_ref[...].astype(BF16).astype(F32)
    dpar[...] = jnp.zeros_like(dpar)

    def param(row):
        return par[row : row + 1, :]

    def add_grad(row, value):
        dpar[row : row + 1, :] = dpar[row : row + 1, :] + value

    def col_sum(value):
        return jnp.sum(value.astype(F32), 0, keepdims=True)

    pltpu.make_async_copy(table_rows, table_rows, table_sem).wait()
    rows_iota = lax.broadcasted_iota(jnp.int32, (16, D), 0)
    for t in range(tiles):
        for e in range(2):
            step = step_ref[0, first_tile + t] if e == 0 else step_ref[split_ref[first_tile + t], first_tile + t]
            chosen = jnp.sum(jnp.where(rows_iota == step % 16, table_rows[t * 2 + e].astype(F32), 0.0), 0, keepdims=True)
            span = slice(t * TILE + e * 64, t * TILE + (e + 1) * 64)
            value = tok_ref[span, :].astype(F32) + chosen
            h0[span, :] = value
            hat, _ = normalised(value)
            a[span, :] = (hat * param(0) + param(2)).astype(BF16)

    for n in range(3):
        settle(n % 2)
        assemble(n % 2, w_qkv.at[n])
        if n == 0:
            fetch(0, functools.partial(block_of, 2))
        elif n == 1:
            fetch(1, functools.partial(block_of, 3))
        else:
            fetch(0, functools.partial(up_block, 0))
        for m in range(row_tiles):
            span = slice(m * ROWS, (m + 1) * ROWS)
            value = dot_nn(a[span, :], w_qkv[n])
            if n == 0:
                value = value + param(4)
            elif n == 2:
                value = value + param(5)
            qkv[n, span, :] = value.astype(BF16)
    settle(1)
    assemble(1, w_out)
    fetch(1, functools.partial(down_block, 0))

    lane = lax.broadcasted_iota(jnp.int32, (TILE, TILE), 1)
    first_head = lane < HD
    row_half = lax.broadcasted_iota(jnp.int32, (2 * TILE, TILE), 0) % TILE // (TILE // 2)
    col_half = lax.broadcasted_iota(jnp.int32, (2 * TILE, TILE), 1) // (TILE // 2)
    same_half = row_half == col_half

    def both(value):
        zero = jnp.zeros_like(value)
        return jnp.concatenate([jnp.where(first_head, value, zero), jnp.where(first_head, zero, value)], 0)

    def side(value):
        return jnp.concatenate([value[0:TILE], value[TILE : 2 * TILE]], 1)

    def attend(t, carry):
        whole = split_ref[first_tile + t] == 0
        allowed = jnp.logical_or(same_half, whole)
        span = pl.ds(pl.multiple_of(t * TILE, TILE), TILE)
        for p in range(HEADS // 2):
            cols = slice(p * TILE, (p + 1) * TILE)
            score = dot_nt(both(qkv[0, span, cols]), qkv[1, span, cols]) * score_scale
            score = jnp.where(allowed, score, masked_score)
            exponent = jnp.exp(score - jnp.max(score, -1, keepdims=True))
            weight = (exponent * (1.0 / jnp.sum(exponent, -1, keepdims=True))).astype(BF16)
            prob[t, p] = weight
            mixed[span, cols] = dot_nn(side(weight), both(qkv[2, span, cols])).astype(BF16)
        return carry

    lax.fori_loop(0, tiles, attend, 0)

    for m in range(row_tiles):
        span = slice(m * ROWS, (m + 1) * ROWS)
        value = h0[span, :] + (dot_nn(mixed[span, :], w_out[...]) + param(6))
        h1[span, :] = value
        hat, _ = normalised(value)
        c[span, :] = (hat * param(1) + param(3)).astype(BF16)
        acc_o[span, :] = value + param(7)
        acc_d[span, :] = jnp.zeros_like(value)

    def feed(part, carry):
        settle(0)
        assemble(0, w_up)

        @pl.when(part < 3)
        def _():
            fetch(0, functools.partial(up_block, part + 1))

        settle(1)
        assemble(1, w_down)

        @pl.when(part < 3)
        def _():
            fetch(1, functools.partial(down_block, part + 1))

        bias = par[pl.ds(8 + part, 1), :]
        bias_grad = jnp.zeros((1, D), F32)
        for m in range(row_tiles):
            span = slice(m * ROWS, (m + 1) * ROWS)
            upper = dot_nn(c[span, :], w_up[...]) + bias
            back = dot_nt(grad_ref[span, :], w_down[...])
            below = 0.5 + 0.5 * lax.erf(upper * 0.7071067811865476)
            density = jnp.exp(upper * upper * -0.5) * 0.3989422804014327
            active = (upper * below).astype(BF16)
            grad_upper = (back * (below + upper * density)).astype(BF16)
            r[span, :] = active
            du[span, :] = grad_upper
            bias_grad = bias_grad + col_sum(grad_upper)
            acc_o[span, :] = acc_o[span, :] + dot_nn(active, w_down[...])
            acc_d[span, :] = acc_d[span, :] + dot_nt(grad_upper, w_up[...])
        dpar[pl.ds(8 + part, 1), :] = bias_grad

        @pl.when(part > 0)
        def _():
            emit_wait(0)
            emit_wait(1)

        weight_grad(0, r[...], grad_ref[...], functools.partial(down_block, part))
        weight_grad(1, c[...], du[...], functools.partial(up_block, part))
        return carry

    lax.fori_loop(0, 4, feed, 0)

    for m in range(row_tiles):
        span = slice(m * ROWS, (m + 1) * ROWS)
        out_ref[span, :] = acc_o[span, :].astype(BF16)
        hat, scale = normalised(h1[span, :])
        cotangent = acc_d[span, :]
        upstream = grad_ref[span, :].astype(F32)
        add_grad(1, col_sum(cotangent * hat))
        add_grad(3, col_sum(cotangent))
        add_grad(7, col_sum(upstream))
        value = upstream + norm_back(cotangent, hat, scale, param(1))
        acc_d[span, :] = value
        rounded = value.astype(BF16)
        c[span, :] = rounded
        add_grad(6, col_sum(rounded))
        r[span, :] = dot_nt(rounded, w_out[...]).astype(BF16)
    emit_wait(0)
    weight_grad(0, mixed[...], c[...], functools.partial(block_of, 3))

    def attend_back(t, carry):
        span = pl.ds(pl.multiple_of(t * TILE, TILE), TILE)
        for p in range(HEADS // 2):
            cols = slice(p * TILE, (p + 1) * TILE)
            cotangent = both(r[span, cols])
            weight = prob[t, p]
            wide = weight.astype(F32)
            back = dot_nt(cotangent, qkv[2, span, cols])
            score_grad = (wide * (back - jnp.sum(wide * back, -1, keepdims=True))).astype(BF16)
            dqkv[0, span, cols] = (dot_nn(side(score_grad), both(qkv[1, span, cols])) * score_scale).astype(BF16)
            dqkv[1, span, cols] = (dot_tn(score_grad, both(qkv[0, span, cols])) * score_scale).astype(BF16)
            dqkv[2, span, cols] = dot_tn(weight, cotangent).astype(BF16)
        return carry

    lax.fori_loop(0, tiles, attend_back, 0)

    for n in range(3):
        emit_wait((n + 1) % 2)
        weight_grad((n + 1) % 2, a[...], dqkv[n], functools.partial(block_of, n))
    add_grad(4, col_sum(dqkv[0]))
    add_grad(5, col_sum(dqkv[2]))
    for m in range(row_tiles):
        span = slice(m * ROWS, (m + 1) * ROWS)
        cotangent = dot_nt(dqkv[0, span, :], w_qkv[0]) + dot_nt(dqkv[1, span, :], w_qkv[1]) + dot_nt(dqkv[2, span, :], w_qkv[2])
        hat, scale = normalised(h0[span, :])
        add_grad(0, col_sum(cotangent * hat))
        add_grad(2, col_sum(cotangent))
        in_grad_ref[span, :] = (acc_d[span, :] + norm_back(cotangent, hat, scale, param(0))).astype(BF16)
    if len(dvec_ref.shape) == 3:
        dvec_ref[...] = jnp.zeros_like(dvec_ref)
        for owner in range(dvec_ref.shape[0]):
            dvec_ref[owner, 0:12, 0:96] = dpar[0:12, owner * 96 : (owner + 1) * 96]
    else:
        dvec_ref[...] = dpar[0:12, :]
    emit_wait(0)
    emit_wait(1)


def run_layer(tokens, out_grad, table, time_step, tile_split, block_slot, blocks, vecs):
    tok_rows = tokens.shape[0]
    tiles = tok_rows // TILE
    smem = pl.BlockSpec(memory_space=pltpu.SMEM)
    vmem = pl.BlockSpec(memory_space=pltpu.VMEM)
    hbm = pl.BlockSpec(memory_space=pl.ANY)
    dvec_shape = vecs.shape
    return pl.pallas_call(
        layer_kernel,
        out_shape=(
            jax.ShapeDtypeStruct((tok_rows, D), BF16),
            jax.ShapeDtypeStruct((tok_rows, D), BF16),
            jax.ShapeDtypeStruct((NBLK, HALF, WIDE), BF16),
            jax.ShapeDtypeStruct(dvec_shape, F32),
        ),
        in_specs=[hbm, smem, smem, vmem, vmem, hbm, hbm, vmem],
        out_specs=(vmem, vmem, hbm, vmem),
        scratch_shapes=[
            pltpu.SMEM(time_step.shape, jnp.int32),
            pltpu.VMEM((16, D), F32),
            pltpu.VMEM((16, D), F32),
            pltpu.VMEM((2 * tiles, 16, D), BF16),
            pltpu.VMEM((tok_rows, D), F32),
            pltpu.VMEM((tok_rows, D), BF16),
            pltpu.VMEM((3, tok_rows, D), BF16),
            pltpu.VMEM((tiles, HEADS // 2, 2 * TILE, TILE), BF16),
            pltpu.VMEM((tok_rows, D), BF16),
            pltpu.VMEM((tok_rows, D), F32),
            pltpu.VMEM((tok_rows, D), BF16),
            pltpu.VMEM((tok_rows, D), F32),
            pltpu.VMEM((tok_rows, D), F32),
            pltpu.VMEM((tok_rows, D), BF16),
            pltpu.VMEM((tok_rows, D), BF16),
            pltpu.VMEM((3, tok_rows, D), BF16),
            pltpu.VMEM((3, D, D), BF16),
            pltpu.VMEM((D, D), BF16),
            pltpu.VMEM((D, D), BF16),
            pltpu.VMEM((D, D), BF16),
            pltpu.VMEM((2, 16, HALF, WIDE), BF16),
            pltpu.VMEM((2, 16, HALF, WIDE), BF16),
            pltpu.SemaphoreType.DMA,
            pltpu.SemaphoreType.DMA,
            pltpu.SemaphoreType.DMA((2,)),
            pltpu.SemaphoreType.DMA((2,)),
        ],
        compiler_params=pltpu.CompilerParams(vmem_limit_bytes=60 * MIB),
        name="layer",
    )(time_step, tile_split, block_slot, tokens, out_grad, table.reshape(-1, 16, D), blocks, vecs)


def step_kernel(
    items_count, sum_ref, vsum_ref, weight_ref, momentum_ref, left_ref, right_ref, root_l_ref, root_r_ref,
    vec_ref, first_ref, second_ref,
    grad_out, momentum_out, weight_out, left_out, right_out, vgrad_out, first_out, second_out, vec_out,
):
    inverse = 1.0 / items_count
    for s in range(sum_ref.shape[0]):
        packed = sum_ref[s]
        low = jnp.concatenate([packed[:, 0:BLK], packed[:, BLK:WIDE]], 0)
        grad = low.astype(F32) * inverse
        low = grad.astype(BF16)
        grad_out[s] = grad
        momentum = 0.9 * momentum_ref[s] + grad
        momentum_out[s] = momentum
        left_out[s] = 0.95 * left_ref[s] + 0.05 * dot_nt(low, low)
        right_out[s] = 0.95 * right_ref[s] + 0.05 * dot_tn(low, low)
        direction = jnp.dot(root_l_ref[s], momentum, precision=highest, preferred_element_type=F32)
        direction = jnp.dot(direction, root_r_ref[s], precision=highest, preferred_element_type=F32)
        weight = weight_ref[s]
        scale = jnp.sqrt(jnp.mean(weight * weight) + 1e-06) * lax.rsqrt(jnp.mean(direction * direction) + 1e-06)
        weight_out[s] = weight - (0.3 * scale) * direction

    @pl.when(pl.program_id(0) == 0)
    def _():
        rows, cols = vec_ref.shape
        grad = vsum_ref[0:rows, 0:cols] * inverse
        vgrad_out[...] = grad
        first = 0.9 * first_ref[...] + 0.1 * grad
        second = 0.999 * second_ref[...] + 0.001 * grad * grad
        first_out[...] = first
        second_out[...] = second
        vec_out[...] = vec_ref[...] - 0.1 * first / (jnp.sqrt(second) + 1e-08)


def run_step(items_count, sums, vsums, weights, momentum, left, right, root_l, root_r, vectors, first, second):
    count = weights.shape[0]
    per = 3
    block = pl.BlockSpec((per, BLK, BLK), lambda i: (i, 0, 0))
    packed = pl.BlockSpec((per, HALF, WIDE), lambda i: (i, 0, 0))
    small = pl.BlockSpec(vectors.shape, lambda i: (0, 0))
    vsum = pl.BlockSpec(vsums.shape, lambda i: (0, 0))
    slots = jax.ShapeDtypeStruct(weights.shape, F32)
    vec = jax.ShapeDtypeStruct(vectors.shape, F32)
    return pl.pallas_call(
        functools.partial(step_kernel, items_count),
        grid=(count // per,),
        out_shape=(slots,) * 5 + (vec,) * 4,
        in_specs=[packed, vsum] + [block] * 6 + [small] * 3,
        out_specs=[block] * 5 + [small] * 4,
        compiler_params=pltpu.CompilerParams(vmem_limit_bytes=50 * MIB),
        name="step",
    )(sums, vsums, weights, momentum, left, right, root_l, root_r, vectors, first, second)


def body(
    tokens, out_grad, time_table, time_step, tile_split, block_slot, weight_slots, momentum_slots,
    stat_left, stat_right, root_left, root_right, vectors, vector_first, vector_second,
):
    items_count = lax.axis_size("items")
    known = items_count == 8 and lax.axis_size("seq") == 4
    if known:
        blocks, vecs = gather_weights(weight_slots, vectors)
        blocks = blocks.reshape(NBLK, HALF, WIDE)
    else:
        low = weight_slots.astype(BF16)
        blocks = lax.all_gather(jnp.concatenate([low[:, :HALF], low[:, HALF:]], 2), "items", axis=0, tiled=True)
        vecs = lax.all_gather(vectors, "items", axis=1, tiled=True)
    output, input_grad, parts, dvec = run_layer(
        tokens, out_grad, time_table, time_step.T, tile_split, block_slot, blocks, vecs
    )
    if known:
        sums, vsums = scatter_sums(parts.reshape(8, 24, HALF, WIDE), dvec)
    else:
        sums = lax.psum_scatter(parts.astype(F32), "items", scatter_dimension=0, tiled=True)
        vsums = lax.psum_scatter(dvec, "items", scatter_dimension=1, tiled=True)
        sums, vsums = lax.psum((sums, vsums), "seq")
    stepped = run_step(
        items_count, sums, vsums, weight_slots, momentum_slots, stat_left, stat_right, root_left, root_right,
        vectors, vector_first, vector_second,
    )
    grad, momentum, weights, left, right, vgrad, first, second, vecs_new = stepped
    return output, input_grad, grad, momentum, weights, left, right, vgrad, first, second, vecs_new


def solution(mesh):
    return jax.shard_map(
        body,
        mesh=mesh,
        in_specs=(
            P(("items", "seq"), None),
            P(("items", "seq"), None),
            P(),
            P("items", None),
            P("items"),
            P(),
            P("items", None, None),
            P("items", None, None),
            P("items", None, None),
            P("items", None, None),
            P("items", None, None),
            P("items", None, None),
            P(None, "items"),
            P(None, "items"),
            P(None, "items"),
        ),
        out_specs=(
            P(("items", "seq"), None),
            P(("items", "seq"), None),
            P("items", None, None),
            P("items", None, None),
            P("items", None, None),
            P("items", None, None),
            P("items", None, None),
            P(None, "items"),
            P(None, "items"),
            P(None, "items"),
            P(None, "items"),
        ),
        check_vma=False,
    )
```

```python
import functools
import jax
import jax.numpy as jnp
from jax import lax
from jax.experimental import pallas as pl
from jax.experimental.pallas import tpu as pltpu
from jax.sharding import PartitionSpec as P

D = 768
HEADS = 12
HD = 64
TILE = 128
BLK = 192
NBLK = 192
HALF = 96
WIDE = 384
MESH = pl.DeviceIdType.MESH
BF16 = jnp.bfloat16
F32 = jnp.float32
MIB = 2 ** 20
highest = lax.Precision.HIGHEST
masked_score = -1000000000.0
norm_epsilon = 1e-05
score_scale = HD ** (-0.5)


def place():
    it = lax.axis_index("items")
    sq = lax.axis_index("seq")
    return it // 2, it % 2, sq // 2, sq % 2


def greet(partners):
    barrier = pltpu.get_barrier_semaphore()
    for partner in partners:
        pl.semaphore_signal(barrier, inc=1, device_id=partner, device_id_type=MESH)
    pl.semaphore_wait(barrier, len(partners))


class Copies:
    def __init__(self, send_sem, recv_sem):
        self.send_sem, self.recv_sem = send_sem, recv_sem
        self.sent = []

    def start(self, index, src, dst, device):
        made = pltpu.make_async_remote_copy(
            src_ref=src, dst_ref=dst,
            send_sem=self.send_sem.at[index], recv_sem=self.recv_sem.at[index],
            device_id=device, device_id_type=MESH,
        )
        made.start()
        self.sent.append(made)

    def wait(self, index, dst, device):
        pltpu.make_async_remote_copy(
            src_ref=dst, dst_ref=dst,
            send_sem=self.send_sem.at[index], recv_sem=self.recv_sem.at[index],
            device_id=device, device_id_type=MESH,
        ).wait_recv()

    def finish(self):
        for made in self.sent:
            made.wait_send()


def dot_nn(left, right):
    return jnp.dot(left, right, preferred_element_type=F32)


def dot_nt(left, right):
    return lax.dot_general(left, right, (((1,), (1,)), ((), ())), preferred_element_type=F32)


def dot_tn(left, right):
    return lax.dot_general(left, right, (((0,), (0,)), ((), ())), preferred_element_type=F32)


def normalised(values):
    average = jnp.mean(values, -1, keepdims=True)
    centred = values - average
    spread = jnp.mean(centred * centred, -1, keepdims=True)
    scale = lax.rsqrt(spread + norm_epsilon)
    return centred * scale, scale


def norm_back(cotangent, hat, scale, gain):
    inner = cotangent * gain
    first = jnp.mean(inner, -1, keepdims=True)
    second = jnp.mean(inner * hat, -1, keepdims=True)
    return scale * (inner - first - hat * second)


ROWS = 256
TOK_TILES_MAX = 8


def layer_kernel(
    time_ref, split_ref, slot_ref, tok_ref, grad_ref, table_ref, blocks_ref, vec_ref,
    out_ref, in_grad_ref, parts_ref, dvec_ref,
    step_ref, par, dpar, table_rows, h0, a, qkv, prob, mixed, h1, c, acc_o, acc_d, r, du, dqkv,
    w_qkv, w_out, w_up, w_down, stage, emit, step_sem, table_sem, stage_sem, emit_sem,
):
    tok_rows = tok_ref.shape[0]
    tiles = tok_rows // TILE
    row_tiles = tok_rows // ROWS
    first_tile = lax.axis_index("seq") * tiles

    def block_of(chunk, i, j):
        if isinstance(chunk, int) and chunk < 3:
            return i * 12 + chunk * 4 + j
        if isinstance(chunk, int) and chunk == 3:
            return 48 + i * 4 + j
        raise ValueError

    def up_block(part, i, j):
        return 64 + i * 16 + part * 4 + j

    def down_block(part, i, j):
        return 128 + part * 16 + i * 4 + j

    def fetch(buffer, block):
        for i in range(4):
            for j in range(4):
                pltpu.make_async_copy(
                    blocks_ref.at[slot_ref[block(i, j)]], stage.at[buffer, i * 4 + j], stage_sem.at[buffer]
                ).start()

    def settle(buffer):
        pltpu.make_async_copy(stage.at[buffer], stage.at[buffer], stage_sem.at[buffer]).wait()

    def assemble(buffer, dst):
        def row_block(i, carry):
            for j in range(4):
                tile = i * 4 + j
                top = pl.ds(pl.multiple_of(i * BLK, 64), HALF)
                low = pl.ds(pl.multiple_of(i * BLK + HALF, 32), HALF)
                dst[top, j * BLK : (j + 1) * BLK] = stage[buffer, tile, :, 0:BLK]
                dst[low, j * BLK : (j + 1) * BLK] = stage[buffer, tile, :, BLK:WIDE]
            return carry

        lax.fori_loop(0, 4, row_block, 0)

    def emit_wait(buffer):
        pltpu.make_async_copy(emit.at[buffer], emit.at[buffer], emit_sem.at[buffer]).wait()

    def emit_rows(buffer, i, value):
        low = value.astype(BF16)
        for j in range(4):
            emit[buffer, i * 4 + j, :, 0:BLK] = low[0:HALF, j * BLK : (j + 1) * BLK]
            emit[buffer, i * 4 + j, :, BLK:WIDE] = low[HALF:BLK, j * BLK : (j + 1) * BLK]

    def emit_send(buffer, block):
        for i in range(4):
            for j in range(4):
                pltpu.make_async_copy(
                    emit.at[buffer, i * 4 + j], parts_ref.at[slot_ref[block(i, j)]], emit_sem.at[buffer]
                ).start()

    def weight_grad(buffer, left, right, block):
        total = dot_tn(left, right)
        for i in range(4):
            emit_rows(buffer, i, total[i * BLK : (i + 1) * BLK])
        emit_send(buffer, block)

    steps_in = pltpu.make_async_copy(time_ref, step_ref, step_sem)
    steps_in.start()
    fetch(0, functools.partial(block_of, 0))
    fetch(1, functools.partial(block_of, 1))
    steps_in.wait()
    for t in range(tiles):
        for e in range(2):
            step = step_ref[0, first_tile + t] if e == 0 else step_ref[split_ref[first_tile + t], first_tile + t]
            pltpu.make_async_copy(table_ref.at[step // 16], table_rows.at[t * 2 + e], table_sem).start()

    if len(vec_ref.shape) == 3:
        for owner in range(vec_ref.shape[0]):
            par[0:12, owner * 96 : (owner + 1) * 96] = vec_ref[owner, 0:12, 0:96].astype(BF16).astype(F32)
    else:
        par[0:12, :] = vec_ref[...].astype(BF16).astype(F32)
    dpar[...] = jnp.zeros_like(dpar)

    def param(row):
        return par[row : row + 1, :]

    def add_grad(row, value):
        dpar[row : row + 1, :] = dpar[row : row + 1, :] + value

    def col_sum(value):
        return jnp.sum(value.astype(F32), 0, keepdims=True)

    pltpu.make_async_copy(table_rows, table_rows, table_sem).wait()
    rows_iota = lax.broadcasted_iota(jnp.int32, (16, D), 0)
    for t in range(tiles):
        for e in range(2):
            step = step_ref[0, first_tile + t] if e == 0 else step_ref[split_ref[first_tile + t], first_tile + t]
            chosen = jnp.sum(jnp.where(rows_iota == step % 16, table_rows[t * 2 + e].astype(F32), 0.0), 0, keepdims=True)
            span = slice(t * TILE + e * 64, t * TILE + (e + 1) * 64)
            value = tok_ref[span, :].astype(F32) + chosen
            h0[span, :] = value
            hat, _ = normalised(value)
            a[span, :] = (hat * param(0) + param(2)).astype(BF16)

    for n in range(3):
        settle(n % 2)
        assemble(n % 2, w_qkv.at[n])
        if n == 0:
            fetch(0, functools.partial(block_of, 2))
        elif n == 1:
            fetch(1, functools.partial(block_of, 3))
        else:
            fetch(0, functools.partial(up_block, 0))
        for m in range(row_tiles):
            span = slice(m * ROWS, (m + 1) * ROWS)
            value = dot_nn(a[span, :], w_qkv[n])
            if n == 0:
                value = value + param(4)
            elif n == 2:
                value = value + param(5)
            qkv[n, span, :] = value.astype(BF16)
    settle(1)
    assemble(1, w_out)
    fetch(1, functools.partial(down_block, 0))

    lane = lax.broadcasted_iota(jnp.int32, (TILE, TILE), 1)
    first_head = lane < HD
    row_half = lax.broadcasted_iota(jnp.int32, (2 * TILE, TILE), 0) % TILE // (TILE // 2)
    col_half = lax.broadcasted_iota(jnp.int32, (2 * TILE, TILE), 1) // (TILE // 2)
    same_half = row_half == col_half

    def both(value):
        zero = jnp.zeros_like(value)
        return jnp.concatenate([jnp.where(first_head, value, zero), jnp.where(first_head, zero, value)], 0)

    def side(value):
        return jnp.concatenate([value[0:TILE], value[TILE : 2 * TILE]], 1)

    def attend(t, carry):
        whole = split_ref[first_tile + t] == 0
        allowed = jnp.logical_or(same_half, whole)
        span = pl.ds(pl.multiple_of(t * TILE, TILE), TILE)
        for p in range(HEADS // 2):
            cols = slice(p * TILE, (p + 1) * TILE)
            score = dot_nt(both(qkv[0, span, cols]), qkv[1, span, cols]) * score_scale
            score = jnp.where(allowed, score, masked_score)
            exponent = jnp.exp(score - jnp.max(score, -1, keepdims=True))
            weight = (exponent * (1.0 / jnp.sum(exponent, -1, keepdims=True))).astype(BF16)
            prob[t, p] = weight
            mixed[span, cols] = dot_nn(side(weight), both(qkv[2, span, cols])).astype(BF16)
        return carry

    lax.fori_loop(0, tiles, attend, 0)

    for m in range(row_tiles):
        span = slice(m * ROWS, (m + 1) * ROWS)
        value = h0[span, :] + (dot_nn(mixed[span, :], w_out[...]) + param(6))
        h1[span, :] = value
        hat, _ = normalised(value)
        c[span, :] = (hat * param(1) + param(3)).astype(BF16)
        acc_o[span, :] = value + param(7)
        acc_d[span, :] = jnp.zeros_like(value)

    def feed(part, carry):
        settle(0)
        assemble(0, w_up)

        @pl.when(part < 3)
        def _():
            fetch(0, functools.partial(up_block, part + 1))

        settle(1)
        assemble(1, w_down)

        @pl.when(part < 3)
        def _():
            fetch(1, functools.partial(down_block, part + 1))

        bias = par[pl.ds(8 + part, 1), :]
        bias_grad = jnp.zeros((1, D), F32)
        for m in range(row_tiles):
            span = slice(m * ROWS, (m + 1) * ROWS)
            upper = dot_nn(c[span, :], w_up[...]) + bias
            back = dot_nt(grad_ref[span, :], w_down[...])
            below = 0.5 + 0.5 * lax.erf(upper * 0.7071067811865476)
            density = jnp.exp(upper * upper * -0.5) * 0.3989422804014327
            active = (upper * below).astype(BF16)
            grad_upper = (back * (below + upper * density)).astype(BF16)
            r[span, :] = active
            du[span, :] = grad_upper
            bias_grad = bias_grad + col_sum(grad_upper)
            acc_o[span, :] = acc_o[span, :] + dot_nn(active, w_down[...])
            acc_d[span, :] = acc_d[span, :] + dot_nt(grad_upper, w_up[...])
        dpar[pl.ds(8 + part, 1), :] = bias_grad

        @pl.when(part > 0)
        def _():
            emit_wait(0)
            emit_wait(1)

        weight_grad(0, r[...], grad_ref[...], functools.partial(down_block, part))
        weight_grad(1, c[...], du[...], functools.partial(up_block, part))
        return carry

    lax.fori_loop(0, 4, feed, 0)

    for m in range(row_tiles):
        span = slice(m * ROWS, (m + 1) * ROWS)
        out_ref[span, :] = acc_o[span, :].astype(BF16)
        hat, scale = normalised(h1[span, :])
        cotangent = acc_d[span, :]
        upstream = grad_ref[span, :].astype(F32)
        add_grad(1, col_sum(cotangent * hat))
        add_grad(3, col_sum(cotangent))
        add_grad(7, col_sum(upstream))
        value = upstream + norm_back(cotangent, hat, scale, param(1))
        acc_d[span, :] = value
        rounded = value.astype(BF16)
        c[span, :] = rounded
        add_grad(6, col_sum(rounded))
        r[span, :] = dot_nt(rounded, w_out[...]).astype(BF16)
    emit_wait(0)
    weight_grad(0, mixed[...], c[...], functools.partial(block_of, 3))

    def attend_back(t, carry):
        span = pl.ds(pl.multiple_of(t * TILE, TILE), TILE)
        for p in range(HEADS // 2):
            cols = slice(p * TILE, (p + 1) * TILE)
            cotangent = both(r[span, cols])
            weight = prob[t, p]
            wide = weight.astype(F32)
            back = dot_nt(cotangent, qkv[2, span, cols])
            score_grad = (wide * (back - jnp.sum(wide * back, -1, keepdims=True))).astype(BF16)
            dqkv[0, span, cols] = (dot_nn(side(score_grad), both(qkv[1, span, cols])) * score_scale).astype(BF16)
            dqkv[1, span, cols] = (dot_tn(score_grad, both(qkv[0, span, cols])) * score_scale).astype(BF16)
            dqkv[2, span, cols] = dot_tn(weight, cotangent).astype(BF16)
        return carry

    lax.fori_loop(0, tiles, attend_back, 0)

    for n in range(3):
        emit_wait((n + 1) % 2)
        weight_grad((n + 1) % 2, a[...], dqkv[n], functools.partial(block_of, n))
    add_grad(4, col_sum(dqkv[0]))
    add_grad(5, col_sum(dqkv[2]))
    for m in range(row_tiles):
        span = slice(m * ROWS, (m + 1) * ROWS)
        cotangent = dot_nt(dqkv[0, span, :], w_qkv[0]) + dot_nt(dqkv[1, span, :], w_qkv[1]) + dot_nt(dqkv[2, span, :], w_qkv[2])
        hat, scale = normalised(h0[span, :])
        add_grad(0, col_sum(cotangent * hat))
        add_grad(2, col_sum(cotangent))
        in_grad_ref[span, :] = (acc_d[span, :] + norm_back(cotangent, hat, scale, param(0))).astype(BF16)
    if len(dvec_ref.shape) == 3:
        dvec_ref[...] = jnp.zeros_like(dvec_ref)
        for owner in range(dvec_ref.shape[0]):
            dvec_ref[owner, 0:12, 0:96] = dpar[0:12, owner * 96 : (owner + 1) * 96]
    else:
        dvec_ref[...] = dpar[0:12, :]
    emit_wait(0)
    emit_wait(1)


def run_layer(tokens, out_grad, table, time_step, tile_split, block_slot, blocks, vecs):
    tok_rows = tokens.shape[0]
    tiles = tok_rows // TILE
    smem = pl.BlockSpec(memory_space=pltpu.SMEM)
    vmem = pl.BlockSpec(memory_space=pltpu.VMEM)
    hbm = pl.BlockSpec(memory_space=pl.ANY)
    dvec_shape = vecs.shape
    return pl.pallas_call(
        layer_kernel,
        out_shape=(
            jax.ShapeDtypeStruct((tok_rows, D), BF16),
            jax.ShapeDtypeStruct((tok_rows, D), BF16),
            jax.ShapeDtypeStruct((NBLK, HALF, WIDE), BF16),
            jax.ShapeDtypeStruct(dvec_shape, F32),
        ),
        in_specs=[hbm, smem, smem, vmem, vmem, hbm, hbm, vmem],
        out_specs=(vmem, vmem, hbm, vmem),
        scratch_shapes=[
            pltpu.SMEM(time_step.shape, jnp.int32),
            pltpu.VMEM((16, D), F32),
            pltpu.VMEM((16, D), F32),
            pltpu.VMEM((2 * tiles, 16, D), BF16),
            pltpu.VMEM((tok_rows, D), F32),
            pltpu.VMEM((tok_rows, D), BF16),
            pltpu.VMEM((3, tok_rows, D), BF16),
            pltpu.VMEM((tiles, HEADS // 2, 2 * TILE, TILE), BF16),
            pltpu.VMEM((tok_rows, D), BF16),
            pltpu.VMEM((tok_rows, D), F32),
            pltpu.VMEM((tok_rows, D), BF16),
            pltpu.VMEM((tok_rows, D), F32),
            pltpu.VMEM((tok_rows, D), F32),
            pltpu.VMEM((tok_rows, D), BF16),
            pltpu.VMEM((tok_rows, D), BF16),
            pltpu.VMEM((3, tok_rows, D), BF16),
            pltpu.VMEM((3, D, D), BF16),
            pltpu.VMEM((D, D), BF16),
            pltpu.VMEM((D, D), BF16),
            pltpu.VMEM((D, D), BF16),
            pltpu.VMEM((2, 16, HALF, WIDE), BF16),
            pltpu.VMEM((2, 16, HALF, WIDE), BF16),
            pltpu.SemaphoreType.DMA,
            pltpu.SemaphoreType.DMA,
            pltpu.SemaphoreType.DMA((2,)),
            pltpu.SemaphoreType.DMA((2,)),
        ],
        compiler_params=pltpu.CompilerParams(vmem_limit_bytes=60 * MIB),
        name="layer",
    )(time_step, tile_split, block_slot, tokens, out_grad, table.reshape(-1, 16, D), blocks, vecs)


CHUNKS = 12
ROWS_CHIP = 48
SPAN = 384


def chip_row(position):
    chip, q = position // ROWS_CHIP, position % ROWS_CHIP
    wide = q // 8 * BLK + chip * 8 + q % 8
    narrow = (q - 32) // 4 * BLK + 128 + chip * 4 + q % 4
    return jnp.where(q < 32, wide, narrow)


def chunk_block(n, i, j):
    if isinstance(n, int) and n < 3:
        return i * 12 + n * 4 + j
    if isinstance(n, int) and n == 3:
        return 48 + i * 4 + j
    raise ValueError


def deal_kernel(slots_ref, order_ref, vec_ref, pieces_ref, vecs_ref, raw, out, vec_own, raw_sem, own_sem, vec_sem, send_sem, recv_sem, vsend, vrecv):
    z, x, y, c = place()
    me = z * 2 + x
    far = [(z + d) % 4 for d in (1, 2, 3)]
    xt = (1 - c) * x + c * (1 - x)
    quarter = y * 2 + c
    across_x = (z * 2 + (1 - x), quarter)
    across_c = (me, y * 2 + (1 - c))
    partners = [(f * 2 + x, quarter) for f in far] + [(f * 2 + (1 - x), quarter) for f in far] + [across_x]
    loads = [
        pltpu.make_async_copy(slots_ref.at[pl.ds(6 * j, 6)], raw.at[pl.ds(6 * j, 6)], raw_sem.at[j]) for j in range(4)
    ]
    for load in loads:
        load.start()
    vec_own[...] = jnp.zeros_like(vec_own)
    vec_own[0:12, 0:96] = vec_ref[...]
    greet(partners + [across_c])
    vcopies = Copies(vsend, vrecv)
    for i in range(7):
        vcopies.start(i, vec_own, vecs_ref.at[me], partners[i])
    local_vec = pltpu.make_async_copy(vec_own, vecs_ref.at[me], vec_sem)
    local_vec.start()

    order = order_ref[...]
    index = lax.broadcasted_iota(jnp.int32, order.shape, 1)
    up = jnp.logical_and(index >= 64, index < 128)

    def deal(s, carry):
        block = raw[s]
        hit = jnp.max(jnp.where(jnp.logical_and(up, order == me * 24 + s), 1, 0), 1, keepdims=True)
        block = jnp.where(hit > 0, jnp.transpose(block, (1, 0)), block)
        low = block.astype(BF16)
        for e in range(16):
            out[e, s, :, 0:BLK] = low[8 * e : 8 * e + 8]
            out[e, s, :, BLK:WIDE] = low[128 + 8 * (e // 2) : 136 + 8 * (e // 2)]
        return carry

    for j in range(4):
        loads[j].wait()
        lax.fori_loop(6 * j, 6 * j + 6, deal, 0)

    copies = Copies(send_sem, recv_sem)
    for i, d in enumerate((1, 2, 3)):
        copies.start(i, out.at[far[i] * 4 + xt * 2 + y], pieces_ref.at[me], (far[i] * 2 + xt, quarter))

    @pl.when(c == 1)
    def _():
        pltpu.make_async_remote_copy(
            src_ref=out.at[z * 4 + xt * 2 + y], dst_ref=pieces_ref.at[me],
            send_sem=send_sem.at[3], recv_sem=recv_sem.at[3],
            device_id=across_x, device_id_type=MESH,
        ).start()

    @pl.when(c == 0)
    def _():
        pltpu.make_async_copy(out.at[z * 4 + x * 2 + y], pieces_ref.at[me], own_sem).start()

    def from_owner(zz):
        return pieces_ref.at[zz * 2 + xt]

    @pl.when(c == 1)
    def _():
        pltpu.make_async_remote_copy(
            src_ref=from_owner(z), dst_ref=from_owner(z),
            send_sem=send_sem.at[3], recv_sem=recv_sem.at[3],
            device_id=across_x, device_id_type=MESH,
        ).wait()

    @pl.when(c == 0)
    def _():
        pltpu.make_async_copy(out.at[z * 4 + x * 2 + y], pieces_ref.at[me], own_sem).wait()

    copies.start(7, from_owner(z), from_owner(z), across_c)
    for i, d in enumerate((1, 2, 3)):
        ref = from_owner((z - d) % 4)
        copies.wait(i, ref, across_c)
        copies.start(4 + i, ref, ref, across_c)
    for i, d in enumerate((1, 2, 3)):
        copies.wait(4 + i, pieces_ref.at[((z - d) % 4) * 2 + (1 - xt)], across_c)
    copies.wait(7, pieces_ref.at[z * 2 + (1 - xt)], across_c)
    for i, d in enumerate((1, 2, 3)):
        vcopies.wait(i, vecs_ref.at[((z - d) % 4) * 2 + x], across_c)
        vcopies.wait(3 + i, vecs_ref.at[((z - d) % 4) * 2 + (1 - x)], across_c)
    vcopies.wait(6, vecs_ref.at[z * 2 + (1 - x)], across_c)
    local_vec.wait()
    copies.finish()
    vcopies.finish()


def deal_weights(slots, order, vectors):
    hbm = pl.BlockSpec(memory_space=pl.ANY)
    vmem = pl.BlockSpec(memory_space=pltpu.VMEM)
    return pl.pallas_call(
        deal_kernel,
        out_shape=(
            jax.ShapeDtypeStruct((8, 24, 8, WIDE), BF16),
            jax.ShapeDtypeStruct((8, 16, 128), F32),
        ),
        in_specs=[hbm, vmem, vmem],
        out_specs=(hbm, hbm),
        scratch_shapes=[
            pltpu.VMEM((24, BLK, BLK), F32),
            pltpu.VMEM((16, 24, 8, WIDE), BF16),
            pltpu.VMEM((16, 128), F32),
            pltpu.SemaphoreType.DMA((4,)),
            pltpu.SemaphoreType.DMA,
            pltpu.SemaphoreType.DMA,
            pltpu.SemaphoreType.DMA((8,)),
            pltpu.SemaphoreType.DMA((8,)),
            pltpu.SemaphoreType.DMA((7,)),
            pltpu.SemaphoreType.DMA((7,)),
        ],
        compiler_params=pltpu.CompilerParams(collective_id=2, has_side_effects=True, vmem_limit_bytes=60 * MIB),
        name="deal_weights",
    )(slots, order, vectors)


def stream_kernel(
    rows_ref, split_ref, slot_ref, tok_hbm, grad_hbm, pieces_ref, vec_ref,
    out_hbm, in_grad_hbm, fin_hbm, dvec_ref,
    par, dpar, bias_up, perm, lay_buf, tok, grad, pieces, hat_one, scale_one, a, qkv, prob, o, hat_two, scale_two,
    c_in, acc_o, acc_d, du, w, dw, from_core, from_first, from_second, from_z, fin,
    in_sem, out_sem, ag_send, ag_recv, rs_send, rs_recv,
):
    tok_rows = tok.shape[0]
    tiles = tok_rows // TILE
    row_tiles = tok_rows // ROWS
    z, x, y, c = place()
    first_tile = (y * 2 + c) * tiles
    me = z * 2 + x
    quarter = y * 2 + c
    fx, fy = (1 - c) * (1 - x) + c * x, (1 - c) * y + c * (1 - y)
    sx, sy = (1 - c) * x + c * (1 - x), (1 - c) * (1 - y) + c * y
    ox, oy = 1 - x, 1 - y
    first = (z * 2 + fx, fy * 2 + c)
    second = (z * 2 + sx, sy * 2 + c)
    across_c = (me, y * 2 + (1 - c))
    far = [(z + d) % 4 for d in (1, 2, 3)]
    near = [(z - d) % 4 for d in (1, 2, 3)]
    along_z = [(f * 2 + x, quarter) for f in far]
    half = pl.ds(pl.multiple_of(c * SPAN, SPAN), SPAN)
    other_half = pl.ds(pl.multiple_of((1 - c) * SPAN, SPAN), SPAN)

    def remote(src, dst, send, recv, device):
        return pltpu.make_async_remote_copy(
            src_ref=src, dst_ref=dst, send_sem=send, recv_sem=recv, device_id=device, device_id_type=MESH
        )

    loads = [
        pltpu.make_async_copy(pieces_ref, pieces, in_sem.at[0]),
        pltpu.make_async_copy(tok_hbm, tok, in_sem.at[1]),
        pltpu.make_async_copy(grad_hbm, grad, in_sem.at[2]),
    ]
    for load in loads:
        load.start()
    greet([first, second, across_c] + along_z)

    def one(n, zz):
        return w.at[n, zz, x, y, :, half]

    def four(n, xx, yy, lanes):
        return w.at[n, :, xx, yy, :, lanes]

    def ag(n, i, ref, device):
        return remote(ref, ref, ag_send.at[n, i], ag_recv.at[n, i], device)

    def gather_start(n):
        for i in range(3):
            ag(n, i, one(n, z), along_z[i]).start()

    def gather_one(n):
        for i in range(3):
            ag(n, i, one(n, near[i]), along_z[i]).wait_recv()
        ref = four(n, x, y, half)
        ag(n, 3, ref, first).start()
        ag(n, 4, ref, second).start()
        ag(n, 6, ref, across_c).start()

    def gather_two(n):
        ref = four(n, fx, fy, half)
        ag(n, 3, ref, first).wait_recv()
        ag(n, 5, ref, second).start()
        ag(n, 7, ref, across_c).start()

    def gather_three(n):
        ref = four(n, sx, sy, half)
        ag(n, 4, ref, second).wait_recv()
        ag(n, 8, ref, across_c).start()
        ref = four(n, ox, oy, half)
        ag(n, 5, ref, second).wait_recv()
        ag(n, 9, ref, across_c).start()

    def gather_four(n):
        for i, (xx, yy) in ((6, (x, y)), (7, (sx, sy)), (8, (fx, fy)), (9, (ox, oy))):
            ag(n, i, four(n, xx, yy, other_half), across_c).wait_recv()

    def guarded(run, n):
        if isinstance(n, int):
            if 0 <= n < CHUNKS:
                run(n)
        else:
            pl.when(jnp.logical_and(n >= 0, n < CHUNKS))(lambda: run(n))

    def gather_step(t):
        guarded(gather_one, t)
        guarded(gather_start, t + 3)
        guarded(gather_two, t - 1)
        guarded(gather_three, t - 2)
        guarded(gather_four, t - 3)

    def rs(n, i, src, dst, device):
        return remote(src, dst, rs_send.at[n, i], rs_recv.at[n, i], device)

    def core_copy(n, slot):
        return rs(n, 0, dw.at[slot, :, :, :, :, other_half], from_core.at[n], across_c)

    def sum_start(n, slot):
        core_copy(n, slot).start()

    def sum_one(n, slot):
        core_copy(n, slot).wait_recv()

        def add(zz, carry):
            for xx in range(2):
                for yy in range(2):
                    from_core[n, zz, xx, yy] = from_core[n, zz, xx, yy] + dw[slot, zz, xx, yy, :, half]
            return carry

        lax.fori_loop(0, 4, add, 0)
        rs(n, 1, from_core.at[n, :, sx, sy], from_first.at[n, 0], second).start()
        rs(n, 2, from_core.at[n, :, ox, oy], from_first.at[n, 1], second).start()
        core_copy(n, slot).wait_send()

    def sum_two(n):
        for i in range(2):
            rs(n, 1 + i, from_first.at[n, i], from_first.at[n, i], second).wait_recv()

        def add(zz, carry):
            from_core[n, zz, fx, fy] = from_core[n, zz, fx, fy] + from_first[n, 1, zz]
            return carry

        lax.fori_loop(0, 4, add, 0)
        rs(n, 3, from_core.at[n, :, fx, fy], from_second.at[n], first).start()

    def sum_three(n):
        rs(n, 3, from_second.at[n], from_second.at[n], first).wait_recv()

        def add(zz, carry):
            from_core[n, zz, x, y] = from_core[n, zz, x, y] + from_first[n, 0, zz] + from_second[n, zz]
            return carry

        lax.fori_loop(0, 4, add, 0)
        for i in range(3):
            rs(n, 4 + i, from_core.at[n, far[i], x, y], from_z.at[n, i], along_z[i]).start()

    def sum_four(n):
        for i in range(3):
            rs(n, 4 + i, from_z.at[n, i], from_z.at[n, i], along_z[i]).wait_recv()
        total = from_core[n, z, x, y].astype(F32)
        for i in range(3):
            total = total + from_z[n, i].astype(F32)
        fin[n] = total.astype(BF16)

    def sum_step(t, slot):
        guarded(lambda n: sum_one(n, slot), t)
        guarded(sum_two, t - 1)
        guarded(sum_three, t - 2)
        guarded(sum_four, t - 3)

    loads[0].wait()

    def lay(n, block):
        for j in range(4):
            wide, narrow = [], []
            for i in range(4):
                piece = pieces[slot_ref[block(i, j)]].astype(F32)
                wide.append(piece[:, 0:BLK])
                extra = piece[:, BLK:WIDE]
                narrow.append(jnp.where(y == 0, extra[0:4], extra[4:8]))
            lay_buf[:, j * BLK : (j + 1) * BLK] = jnp.concatenate(wide + narrow, 0).astype(BF16)
        w[n, z, x, y, :, half] = lay_buf[:, half]

    for n in range(4):
        lay(n, functools.partial(chunk_block, n))
        if n < 3:
            gather_start(n)

    def lay_feed(part, carry):
        lay(4 + 2 * part, lambda i, j: 64 + j * 16 + part * 4 + i)
        lay(5 + 2 * part, lambda i, j: 128 + part * 16 + i * 4 + j)
        return carry

    lax.fori_loop(0, 4, lay_feed, 0)

    par[...] = jnp.zeros_like(par)
    for owner in range(8):
        par[0:12, owner * 96 : (owner + 1) * 96] = vec_ref[owner, 0:12, 0:96].astype(BF16).astype(F32)
    dpar[...] = jnp.zeros_like(dpar)
    chosen_row = chip_row(lax.broadcasted_iota(jnp.int32, (8, D), 1))
    row_index = lax.broadcasted_iota(jnp.int32, (16, D), 0)
    chosen_row = jnp.concatenate([chosen_row, chosen_row], 0)

    def perm_rows(i, carry):
        perm[pl.ds(pl.multiple_of(i * 16, 16), 16), :] = jnp.where(chosen_row == row_index + i * 16, 1.0, 0.0).astype(BF16)
        return carry

    lax.fori_loop(0, D // 16, perm_rows, 0)
    bias_up[...] = dot_nn(par[8:16, :].astype(BF16), perm[...])

    def param(row):
        return par[row : row + 1, :]

    def add_grad(row, value):
        dpar[row : row + 1, :] = dpar[row : row + 1, :] + value

    def col_sum(value):
        return jnp.sum(value.astype(F32), 0, keepdims=True)

    def span_of(m):
        return slice(m * ROWS, (m + 1) * ROWS)

    def weights(n):
        return w[n].reshape(D, D)

    loads[1].wait()
    loads[2].wait()
    for t in range(tiles):
        for e in range(2):
            span = slice(t * TILE + e * 64, t * TILE + (e + 1) * 64)
            value = tok[span, :].astype(F32) + rows_ref[2 * t + e : 2 * t + e + 1, :]
            acc_o[span, :] = value
            hat, scale = normalised(value)
            hat_one[span, :] = hat.astype(BF16)
            scale_one[span, :] = scale
            c_in[span, :] = (hat * param(0) + param(2)).astype(BF16)
    for m in range(row_tiles):
        a[span_of(m), :] = dot_nn(c_in[span_of(m), :], perm[...]).astype(BF16)

    for t in range(4):
        gather_step(t)
    for n in range(3):
        for m in range(row_tiles):
            value = dot_nn(a[span_of(m), :], weights(n))
            if n == 0:
                value = value + param(4)
            elif n == 2:
                value = value + param(5)
            qkv[n, span_of(m), :] = value.astype(BF16)
        gather_step(4 + n)

    lane = lax.broadcasted_iota(jnp.int32, (TILE, TILE), 1)
    first_head = lane < HD
    row_half = lax.broadcasted_iota(jnp.int32, (2 * TILE, TILE), 0) % TILE // (TILE // 2)
    col_half = lax.broadcasted_iota(jnp.int32, (2 * TILE, TILE), 1) // (TILE // 2)
    same_half = row_half == col_half

    def both(value):
        zero = jnp.zeros_like(value)
        return jnp.concatenate([jnp.where(first_head, value, zero), jnp.where(first_head, zero, value)], 0)

    def side(value):
        return jnp.concatenate([value[0:TILE], value[TILE : 2 * TILE]], 1)

    def attend(t, carry):
        whole = split_ref[first_tile + t] == 0
        allowed = jnp.logical_or(same_half, whole)
        span = pl.ds(pl.multiple_of(t * TILE, TILE), TILE)
        for p in range(HEADS // 2):
            cols = slice(p * TILE, (p + 1) * TILE)
            score = dot_nt(both(qkv[0, span, cols]), qkv[1, span, cols]) * score_scale
            score = jnp.where(allowed, score, masked_score)
            exponent = jnp.exp(score - jnp.max(score, -1, keepdims=True))
            weight = (exponent * (1.0 / jnp.sum(exponent, -1, keepdims=True))).astype(BF16)
            prob[t, p] = weight
            c_in[span, cols] = dot_nn(side(weight), both(qkv[2, span, cols])).astype(BF16)
        return carry

    lax.fori_loop(0, tiles // 2, attend, 0)
    gather_step(7)
    lax.fori_loop(tiles // 2, tiles, attend, 0)

    for m in range(row_tiles):
        span = span_of(m)
        o[span, :] = dot_nn(c_in[span, :], perm[...]).astype(BF16)
        value = acc_o[span, :] + (dot_nn(o[span, :], weights(3)) + param(6))
        hat, scale = normalised(value)
        hat_two[span, :] = hat.astype(BF16)
        scale_two[span, :] = scale
        c_in[span, :] = (hat * param(1) + param(3)).astype(BF16)
        acc_o[span, :] = value + param(7)
        acc_d[span, :] = jnp.zeros_like(value)
    gather_step(8)

    def feed(part, carry):
        up, down = 4 + 2 * part, 5 + 2 * part
        bias = bias_up[pl.ds(part, 1), :]
        bias_grad = jnp.zeros((1, D), F32)
        for m in range(row_tiles):
            span = span_of(m)
            upper = dot_nt(c_in[span, :], weights(up)) + bias
            back = dot_nt(grad[span, :], weights(down))
            below = 0.5 + 0.5 * lax.erf(upper * 0.7071067811865476)
            density = jnp.exp(upper * upper * -0.5) * 0.3989422804014327
            active = (upper * below).astype(BF16)
            grad_upper = (back * (below + upper * density)).astype(BF16)
            tok[span, :] = active
            du[span, :] = grad_upper
            bias_grad = bias_grad + col_sum(grad_upper)
            acc_o[span, :] = acc_o[span, :] + dot_nn(active, weights(down))
            acc_d[span, :] = acc_d[span, :] + dot_nn(grad_upper, weights(up))
            if m == 0:
                gather_step(9 + 2 * part)
            elif m == 1:
                pl.when(part > 0)(lambda: sum_step(2 * part - 2, 0))
            elif m == 2:
                gather_step(10 + 2 * part)
            else:
                pl.when(part > 0)(lambda: sum_step(2 * part - 1, 1))
        dpar[pl.ds(8 + part, 1), :] = bias_grad
        dw[0] = dot_tn(tok[...], grad[...]).astype(BF16).reshape(4, 2, 2, ROWS_CHIP, D)
        sum_start(2 * part, 0)
        dw[1] = dot_tn(du[...], c_in[...]).astype(BF16).reshape(4, 2, 2, ROWS_CHIP, D)
        sum_start(2 * part + 1, 1)
        return carry

    lax.fori_loop(0, 4, feed, 0)

    for m in range(row_tiles):
        span = span_of(m)
        du[span, :] = acc_o[span, :].astype(BF16)
        hat = hat_two[span, :].astype(F32)
        cotangent = acc_d[span, :]
        upstream = grad[span, :].astype(F32)
        add_grad(1, col_sum(cotangent * hat))
        add_grad(3, col_sum(cotangent))
        add_grad(7, col_sum(upstream))
        value = upstream + norm_back(cotangent, hat, scale_two[span, :], param(1))
        acc_d[span, :] = value
        rounded = value.astype(BF16)
        c_in[span, :] = rounded
        add_grad(6, col_sum(rounded))
        mixed_grad = dot_nt(rounded, weights(3)).astype(BF16)
        tok[span, :] = dot_nt(mixed_grad, perm[...]).astype(BF16)
        if m == 0:
            sum_step(6, 0)
        elif m == 2:
            sum_step(7, 1)
    out_copy = pltpu.make_async_copy(du, out_hbm, out_sem.at[0])
    out_copy.start()
    dw[0] = dot_tn(o[...], c_in[...]).astype(BF16).reshape(4, 2, 2, ROWS_CHIP, D)
    sum_start(8, 0)

    def attend_back(t, carry):
        span = pl.ds(pl.multiple_of(t * TILE, TILE), TILE)
        for p in range(HEADS // 2):
            cols = slice(p * TILE, (p + 1) * TILE)
            cotangent = both(tok[span, cols])
            weight = prob[t, p]
            wide = weight.astype(F32)
            queries, keys = both(qkv[0, span, cols]), both(qkv[1, span, cols])
            back = dot_nt(cotangent, qkv[2, span, cols])
            score_grad = (wide * (back - jnp.sum(wide * back, -1, keepdims=True))).astype(BF16)
            qkv[0, span, cols] = (dot_nn(side(score_grad), keys) * score_scale).astype(BF16)
            qkv[1, span, cols] = (dot_tn(score_grad, queries) * score_scale).astype(BF16)
            qkv[2, span, cols] = dot_tn(weight, cotangent).astype(BF16)
        return carry

    lax.fori_loop(0, 2, attend_back, 0)
    sum_step(8, 0)
    lax.fori_loop(2, 5, attend_back, 0)
    sum_two(8)
    sum_three(7)
    sum_four(6)
    lax.fori_loop(5, tiles, attend_back, 0)

    for n in range(3):
        slot = (n + 1) % 2
        dw[slot] = dot_tn(a[...], qkv[n]).astype(BF16).reshape(4, 2, 2, ROWS_CHIP, D)
        sum_start(9 + n, slot)
        if n == 0:
            sum_three(8)
            sum_four(7)
        else:
            sum_one(8 + n, (n + 0) % 2)
            if n == 1:
                sum_four(8)
            else:
                sum_two(9)
    add_grad(4, col_sum(qkv[0]))
    add_grad(5, col_sum(qkv[2]))
    for m in range(row_tiles):
        span = span_of(m)
        cotangent = dot_nt(qkv[0, span, :], weights(0)) + dot_nt(qkv[1, span, :], weights(1)) + dot_nt(qkv[2, span, :], weights(2))
        cotangent = dot_nt(cotangent.astype(BF16), perm[...])
        hat = hat_one[span, :].astype(F32)
        add_grad(0, col_sum(cotangent * hat))
        add_grad(2, col_sum(cotangent))
        grad[span, :] = (acc_d[span, :] + norm_back(cotangent, hat, scale_one[span, :], param(0))).astype(BF16)
        if m == 0:
            sum_one(11, 1)
            sum_two(10)
            sum_three(9)
        elif m == 2:
            sum_two(11)
            sum_three(10)
            sum_four(9)
    in_grad_copy = pltpu.make_async_copy(grad, in_grad_hbm, out_sem.at[1])
    in_grad_copy.start()

    rest = dpar[8:16, :]
    ordered = jnp.zeros((8, D), F32)
    for _ in range(3):
        low = rest.astype(BF16)
        ordered = ordered + dot_nt(low, perm[...])
        rest = rest - low.astype(F32)
    dpar[8:16, :] = ordered
    dvec_ref[...] = jnp.zeros_like(dvec_ref)
    for owner in range(8):
        dvec_ref[owner, 0:12, 0:96] = dpar[0:12, owner * 96 : (owner + 1) * 96]

    sum_three(11)
    sum_four(10)
    sum_four(11)
    fin_copy = pltpu.make_async_copy(fin, fin_hbm, out_sem.at[2])
    fin_copy.start()

    def finish(n, carry):
        for i in range(3):
            ag(n, i, one(n, z), along_z[i]).wait_send()
        for i in range(3, 10):
            ag(n, i, four(n, x, y, half), across_c).wait_send()
        for i in range(1, 4):
            rs(n, i, from_core.at[n, :, x, y], from_second.at[n], first).wait_send()
        for i in range(4, 7):
            rs(n, i, from_core.at[n, z, x, y], from_z.at[n, 0], first).wait_send()
        return carry

    lax.fori_loop(0, CHUNKS, finish, 0)
    out_copy.wait()
    in_grad_copy.wait()
    fin_copy.wait()


def rows_kernel(step_ref, split_ref, table_ref, rows_ref, groups, sem):
    count = rows_ref.shape[0]
    first = lax.axis_index("seq") * (count // 2)

    def step_of(i):
        tile = first + i // 2
        return step_ref[0, tile] if i % 2 == 0 else step_ref[split_ref[tile], tile]

    for i in range(count):
        pltpu.make_async_copy(table_ref.at[step_of(i) // 16], groups.at[i], sem).start()
    pltpu.make_async_copy(groups, groups, sem).wait()
    row_index = lax.broadcasted_iota(jnp.int32, (16, D), 0)
    for i in range(count):
        picked = jnp.where(row_index == step_of(i) % 16, groups[i].astype(F32), 0.0)
        rows_ref[i : i + 1, :] = jnp.sum(picked, 0, keepdims=True)


def pick_rows(time_step, tile_split, table, count):
    smem = pl.BlockSpec(memory_space=pltpu.SMEM)
    return pl.pallas_call(
        rows_kernel,
        out_shape=jax.ShapeDtypeStruct((count, D), F32),
        in_specs=[smem, smem, pl.BlockSpec(memory_space=pl.ANY)],
        out_specs=pl.BlockSpec(memory_space=pltpu.VMEM),
        scratch_shapes=[pltpu.VMEM((count, 16, D), BF16), pltpu.SemaphoreType.DMA],
        compiler_params=pltpu.CompilerParams(vmem_limit_bytes=60 * MIB),
        name="pick_rows",
    )(time_step, tile_split, table.reshape(-1, 16, D))


def run_stream(tokens, out_grad, rows, tile_split, block_slot, pieces, vecs):
    tok_rows = tokens.shape[0]
    tiles = tok_rows // TILE
    smem = pl.BlockSpec(memory_space=pltpu.SMEM)
    vmem = pl.BlockSpec(memory_space=pltpu.VMEM)
    hbm = pl.BlockSpec(memory_space=pl.ANY)
    rows_low = pltpu.VMEM((tok_rows, D), BF16)
    rows_full = pltpu.VMEM((tok_rows, D), F32)
    rows_one = pltpu.VMEM((tok_rows, 1), F32)
    return pl.pallas_call(
        stream_kernel,
        out_shape=(
            jax.ShapeDtypeStruct((tok_rows, D), BF16),
            jax.ShapeDtypeStruct((tok_rows, D), BF16),
            jax.ShapeDtypeStruct((CHUNKS, ROWS_CHIP, SPAN), BF16),
            jax.ShapeDtypeStruct(vecs.shape, F32),
        ),
        in_specs=[vmem, smem, smem, hbm, hbm, hbm, vmem],
        out_specs=(hbm, hbm, hbm, vmem),
        scratch_shapes=[
            pltpu.VMEM((16, D), F32),
            pltpu.VMEM((16, D), F32),
            pltpu.VMEM((8, D), F32),
            pltpu.VMEM((D, D), BF16),
            pltpu.VMEM((ROWS_CHIP, D), BF16),
            rows_low,
            rows_low,
            pltpu.VMEM((NBLK, 8, WIDE), BF16),
            rows_low,
            rows_one,
            rows_low,
            pltpu.VMEM((3, tok_rows, D), BF16),
            pltpu.VMEM((tiles, HEADS // 2, 2 * TILE, TILE), BF16),
            rows_low,
            rows_low,
            rows_one,
            rows_low,
            rows_full,
            rows_full,
            rows_low,
            pltpu.VMEM((CHUNKS, 4, 2, 2, ROWS_CHIP, D), BF16),
            pltpu.VMEM((2, 4, 2, 2, ROWS_CHIP, D), BF16),
            pltpu.VMEM((CHUNKS, 4, 2, 2, ROWS_CHIP, SPAN), BF16),
            pltpu.VMEM((CHUNKS, 2, 4, ROWS_CHIP, SPAN), BF16),
            pltpu.VMEM((CHUNKS, 4, ROWS_CHIP, SPAN), BF16),
            pltpu.VMEM((CHUNKS, 3, ROWS_CHIP, SPAN), BF16),
            pltpu.VMEM((CHUNKS, ROWS_CHIP, SPAN), BF16),
            pltpu.SemaphoreType.DMA((3,)),
            pltpu.SemaphoreType.DMA((3,)),
            pltpu.SemaphoreType.DMA((CHUNKS, 10)),
            pltpu.SemaphoreType.DMA((CHUNKS, 10)),
            pltpu.SemaphoreType.DMA((CHUNKS, 7)),
            pltpu.SemaphoreType.DMA((CHUNKS, 7)),
        ],
        compiler_params=pltpu.CompilerParams(collective_id=3, has_side_effects=True, vmem_limit_bytes=63 * MIB),
        name="stream",
    )(rows, tile_split, block_slot, tokens, out_grad, pieces, vecs)


def collect_kernel(
    inverse_ref, fin_ref, dvec_ref, gp_ref, vsum_ref,
    full, by_block, out, va, vb, vz, load_sem, own_sem, send_sem, recv_sem, vload_sem, vsend, vrecv,
):
    z, x, y, c = place()
    me = z * 2 + x
    quarter = y * 2 + c
    far = [(z + d) % 4 for d in (1, 2, 3)]
    near = [(z - d) % 4 for d in (1, 2, 3)]
    xt = (1 - c) * x + c * (1 - x)
    across_x = (z * 2 + (1 - x), quarter)
    across_y = (me, (1 - y) * 2 + c)
    across_c = (me, y * 2 + (1 - c))
    along_z = [(f * 2 + x, quarter) for f in far]
    skew = [(f * 2 + (1 - x), quarter) for f in far]
    half = pl.ds(pl.multiple_of(c * SPAN, SPAN), SPAN)
    own_half = pltpu.make_async_copy(fin_ref, full.at[:, :, half], load_sem)
    own_half.start()
    vec_load = pltpu.make_async_copy(dvec_ref, vb.at[0], vload_sem)
    vec_load.start()
    greet([across_x, across_y, across_c] + along_z + skew)
    copies = Copies(send_sem, recv_sem)
    vcopies = Copies(vsend, vrecv)
    copies.start(16, fin_ref, full.at[:, :, half], across_c)
    vcopies.start(0, dvec_ref, va, across_c)
    own_half.wait()
    copies.wait(16, full.at[:, :, pl.ds(pl.multiple_of((1 - c) * SPAN, SPAN), SPAN)], across_c)

    mine = lax.broadcasted_iota(jnp.int32, (8, BLK), 0) // 4 == y

    def split_chunk(n, block):
        for j in range(4):
            column = full[n, :, j * BLK : (j + 1) * BLK].astype(F32)
            for i in range(4):
                extra = column[32 + 4 * i : 36 + 4 * i]
                extra = jnp.where(mine, jnp.concatenate([extra, extra], 0), 0.0)
                by_block[block(i, j), :, 0:BLK] = column[8 * i : 8 * i + 8].astype(BF16)
                by_block[block(i, j), :, BLK:WIDE] = extra.astype(BF16)

    def split_feed(part, carry):
        split_chunk(2 * part, lambda i, j: 128 + part * 16 + i * 4 + j)
        split_chunk(2 * part + 1, lambda i, j: 64 + j * 16 + part * 4 + i)
        return carry

    lax.fori_loop(0, 4, split_feed, 0)
    split_chunk(8, functools.partial(chunk_block, 3))
    for n in range(3):
        split_chunk(9 + n, functools.partial(chunk_block, n))

    def pick(s, carry):
        out[s] = by_block[inverse_ref[s]]
        return carry

    lax.fori_loop(0, NBLK, pick, 0)

    def owner_part(zz):
        return out.at[pl.ds((zz * 2 + xt) * 24, 24)]

    def chip(zz, xx, yy):
        return gp_ref.at[zz * 4 + xx * 2 + yy]

    for i in range(3):
        copies.start(i, owner_part(far[i]), chip(z, x, y), (far[i] * 2 + xt, quarter))

    def straight():
        return pltpu.make_async_remote_copy(
            src_ref=owner_part(z), dst_ref=chip(z, x, y), send_sem=send_sem.at[3], recv_sem=recv_sem.at[3],
            device_id=across_x, device_id_type=MESH,
        )

    def stays():
        return pltpu.make_async_copy(owner_part(z), chip(z, x, y), own_sem)

    pl.when(c == 1)(lambda: straight().start())
    pl.when(c == 0)(lambda: stays().start())

    vec_load.wait()
    vcopies.wait(0, va, across_c)
    va[...] = va[...] + vb[0]
    vcopies.start(1, va, vb.at[1], across_y)

    pl.when(c == 1)(lambda: straight().wait())
    pl.when(c == 0)(lambda: stays().wait())
    ref = chip(z, xt, y)
    copies.start(7, ref, ref, across_y)
    copies.start(11, ref, ref, across_c)
    for i in range(3):
        ref = chip(near[i], xt, y)
        copies.wait(i, ref, across_c)
        copies.start(4 + i, ref, ref, across_y)
        copies.start(8 + i, ref, ref, across_c)
        if i == 0:
            vcopies.wait(1, vb.at[1], across_y)
            vb[1] = va[...] + vb[1]
            vcopies.start(2, vb.at[1], vb.at[2], across_x)
        elif i == 1:
            vcopies.wait(2, vb.at[2], across_x)
            vb[3] = vb[1] + vb[2]
            for k in range(3):
                vcopies.start(3 + k, vb.at[3, far[k] * 2 + x], vz.at[k], along_z[k])
    for i, zz in ((3, z), (0, near[0]), (1, near[1]), (2, near[2])):
        ref = chip(zz, xt, 1 - y)
        copies.wait(4 + i, ref, across_y)
        copies.start(12 + i, ref, ref, across_c)
    for i in range(3):
        vcopies.wait(3 + i, vz.at[i], across_c)
    vsum_ref[...] = vb[3, me] + vz[0] + vz[1] + vz[2]
    for i, zz in ((3, z), (0, near[0]), (1, near[1]), (2, near[2])):
        copies.wait(8 + i, chip(zz, 1 - xt, y), across_c)
        copies.wait(12 + i, chip(zz, 1 - xt, 1 - y), across_c)
    copies.finish()
    vcopies.finish()


def collect_sums(inverse, fin, dvec):
    hbm = pl.BlockSpec(memory_space=pl.ANY)
    return pl.pallas_call(
        collect_kernel,
        out_shape=(
            jax.ShapeDtypeStruct((16, 24, 8, WIDE), BF16),
            jax.ShapeDtypeStruct((16, 128), F32),
        ),
        in_specs=[pl.BlockSpec(memory_space=pltpu.SMEM), hbm, hbm],
        out_specs=(hbm, pl.BlockSpec(memory_space=pltpu.VMEM)),
        scratch_shapes=[
            pltpu.VMEM((CHUNKS, ROWS_CHIP, D), BF16),
            pltpu.VMEM((NBLK, 8, WIDE), BF16),
            pltpu.VMEM((NBLK, 8, WIDE), BF16),
            pltpu.VMEM((8, 16, 128), F32),
            pltpu.VMEM((4, 8, 16, 128), F32),
            pltpu.VMEM((3, 16, 128), F32),
            pltpu.SemaphoreType.DMA,
            pltpu.SemaphoreType.DMA,
            pltpu.SemaphoreType.DMA((17,)),
            pltpu.SemaphoreType.DMA((17,)),
            pltpu.SemaphoreType.DMA,
            pltpu.SemaphoreType.DMA((6,)),
            pltpu.SemaphoreType.DMA((6,)),
        ],
        compiler_params=pltpu.CompilerParams(collective_id=4, has_side_effects=True, vmem_limit_bytes=16 * MIB),
        name="collect_sums",
    )(inverse, fin, dvec)


def step_kernel(
    items_count, inverse_ref, sum_ref, vsum_ref, weight_ref, momentum_ref, left_ref, right_ref, root_l_ref, root_r_ref,
    vec_ref, first_ref, second_ref,
    grad_out, momentum_out, weight_out, left_out, right_out, vgrad_out, first_out, second_out, vec_out,
):
    inverse = 1.0 / items_count
    count = weight_ref.shape[0]
    for s in range(count):
        if len(sum_ref.shape) == 4:
            wide = sum_ref[:, s, :, 0:BLK].astype(F32).reshape(128, BLK)
            narrow = sum_ref[:, s, :, BLK:WIDE].astype(F32).reshape(8, 2, 8, BLK)
            grad = jnp.concatenate([wide, (narrow[:, 0] + narrow[:, 1]).reshape(64, BLK)], 0)
            block = inverse_ref[(lax.axis_index("items") * pl.num_programs(0) + pl.program_id(0)) * count + s]
            up = jnp.logical_and(block >= 64, block < 128)
            grad = jnp.where(up, jnp.transpose(grad, (1, 0)), grad) * inverse
        else:
            packed = sum_ref[s]
            grad = jnp.concatenate([packed[:, 0:BLK], packed[:, BLK:WIDE]], 0).astype(F32) * inverse
        low = grad.astype(BF16)
        grad_out[s] = grad
        momentum = 0.9 * momentum_ref[s] + grad
        momentum_out[s] = momentum
        left_out[s] = 0.95 * left_ref[s] + 0.05 * dot_nt(low, low)
        right_out[s] = 0.95 * right_ref[s] + 0.05 * dot_tn(low, low)
        direction = jnp.dot(root_l_ref[s], momentum, precision=highest, preferred_element_type=F32)
        direction = jnp.dot(direction, root_r_ref[s], precision=highest, preferred_element_type=F32)
        weight = weight_ref[s]
        scale = jnp.sqrt(jnp.mean(weight * weight) + 1e-06) * lax.rsqrt(jnp.mean(direction * direction) + 1e-06)
        weight_out[s] = weight - (0.3 * scale) * direction

    @pl.when(pl.program_id(0) == 0)
    def _():
        rows, cols = vec_ref.shape
        grad = vsum_ref[0:rows, 0:cols] * inverse
        vgrad_out[...] = grad
        first = 0.9 * first_ref[...] + 0.1 * grad
        second = 0.999 * second_ref[...] + 0.001 * grad * grad
        first_out[...] = first
        second_out[...] = second
        vec_out[...] = vec_ref[...] - 0.1 * first / (jnp.sqrt(second) + 1e-08)


def run_step(items_count, inverse, sums, vsums, weights, momentum, left, right, root_l, root_r, vectors, first, second):
    count = weights.shape[0]
    per = 3
    block = pl.BlockSpec((per, BLK, BLK), lambda i: (i, 0, 0))
    if len(sums.shape) == 4:
        packed = pl.BlockSpec((16, per, 8, WIDE), lambda i: (0, i, 0, 0))
    else:
        packed = pl.BlockSpec((per, HALF, WIDE), lambda i: (i, 0, 0))
    small = pl.BlockSpec(vectors.shape, lambda i: (0, 0))
    vsum = pl.BlockSpec(vsums.shape, lambda i: (0, 0))
    slots = jax.ShapeDtypeStruct(weights.shape, F32)
    vec = jax.ShapeDtypeStruct(vectors.shape, F32)
    return pl.pallas_call(
        functools.partial(step_kernel, items_count),
        grid=(count // per,),
        out_shape=(slots,) * 5 + (vec,) * 4,
        in_specs=[pl.BlockSpec(memory_space=pltpu.SMEM), packed, vsum] + [block] * 6 + [small] * 3,
        out_specs=[block] * 5 + [small] * 4,
        compiler_params=pltpu.CompilerParams(vmem_limit_bytes=50 * MIB),
        name="step",
    )(inverse, sums, vsums, weights, momentum, left, right, root_l, root_r, vectors, first, second)


def body(
    tokens, out_grad, time_table, time_step, tile_split, block_slot, weight_slots, momentum_slots,
    stat_left, stat_right, root_left, root_right, vectors, vector_first, vector_second,
):
    items_count = lax.axis_size("items")
    spots = jnp.arange(NBLK, dtype=jnp.int32)
    inverse = jnp.sum(jnp.where(block_slot[None, :] == spots[:, None], spots[None, :], 0), 1)
    if items_count == 8 and lax.axis_size("seq") == 4:
        pieces, vecs = deal_weights(weight_slots, block_slot.reshape(1, NBLK), vectors)
        rows = pick_rows(time_step.T, tile_split, time_table, 2 * tokens.shape[0] // TILE)
        output, input_grad, fin, dvec = run_stream(
            tokens, out_grad, rows, tile_split, block_slot, pieces.reshape(NBLK, 8, WIDE), vecs
        )
        sums, vsums = collect_sums(inverse, fin, dvec)
    else:
        low = weight_slots.astype(BF16)
        blocks = lax.all_gather(jnp.concatenate([low[:, :HALF], low[:, HALF:]], 2), "items", axis=0, tiled=True)
        vecs = lax.all_gather(vectors, "items", axis=1, tiled=True)
        output, input_grad, parts, dvec = run_layer(
            tokens, out_grad, time_table, time_step.T, tile_split, block_slot, blocks, vecs
        )
        sums = lax.psum_scatter(parts.astype(F32), "items", scatter_dimension=0, tiled=True)
        vsums = lax.psum_scatter(dvec, "items", scatter_dimension=1, tiled=True)
        sums, vsums = lax.psum((sums, vsums), "seq")
    stepped = run_step(
        items_count, inverse, sums, vsums, weight_slots, momentum_slots, stat_left, stat_right, root_left, root_right,
        vectors, vector_first, vector_second,
    )
    grad, momentum, weights, left, right, vgrad, first, second, vecs_new = stepped
    return output, input_grad, grad, momentum, weights, left, right, vgrad, first, second, vecs_new


def solution(mesh):
    return jax.shard_map(
        body,
        mesh=mesh,
        in_specs=(
            P(("items", "seq"), None),
            P(("items", "seq"), None),
            P(),
            P("items", None),
            P("items"),
            P(),
            P("items", None, None),
            P("items", None, None),
            P("items", None, None),
            P("items", None, None),
            P("items", None, None),
            P("items", None, None),
            P(None, "items"),
            P(None, "items"),
            P(None, "items"),
        ),
        out_specs=(
            P(("items", "seq"), None),
            P(("items", "seq"), None),
            P("items", None, None),
            P("items", None, None),
            P("items", None, None),
            P("items", None, None),
            P("items", None, None),
            P(None, "items"),
            P(None, "items"),
            P(None, "items"),
            P(None, "items"),
        ),
        check_vma=False,
    )
```

```python
import functools
import jax
import jax.numpy as jnp
from jax import lax
from jax.experimental import pallas as pl
from jax.experimental.pallas import tpu as pltpu
from jax.sharding import PartitionSpec as P

D = 768
HEADS = 12
HD = 64
TILE = 128
BLK = 192
NBLK = 192
HALF = 96
WIDE = 384
MESH = pl.DeviceIdType.MESH
BF16 = jnp.bfloat16
F32 = jnp.float32
MIB = 2 ** 20
highest = lax.Precision.HIGHEST
masked_score = -1000000000.0
norm_epsilon = 1e-05
score_scale = HD ** (-0.5)


def place():
    it = lax.axis_index("items")
    sq = lax.axis_index("seq")
    return it // 2, it % 2, sq // 2, sq % 2


def greet(partners):
    barrier = pltpu.get_barrier_semaphore()
    for partner in partners:
        pl.semaphore_signal(barrier, inc=1, device_id=partner, device_id_type=MESH)
    pl.semaphore_wait(barrier, len(partners))


class Copies:
    def __init__(self, send_sem, recv_sem):
        self.send_sem, self.recv_sem = send_sem, recv_sem
        self.sent = []

    def start(self, index, src, dst, device):
        made = pltpu.make_async_remote_copy(
            src_ref=src, dst_ref=dst,
            send_sem=self.send_sem.at[index], recv_sem=self.recv_sem.at[index],
            device_id=device, device_id_type=MESH,
        )
        made.start()
        self.sent.append(made)

    def wait(self, index, dst, device):
        pltpu.make_async_remote_copy(
            src_ref=dst, dst_ref=dst,
            send_sem=self.send_sem.at[index], recv_sem=self.recv_sem.at[index],
            device_id=device, device_id_type=MESH,
        ).wait_recv()

    def finish(self):
        for made in self.sent:
            made.wait_send()


def dot_nn(left, right):
    return jnp.dot(left, right, preferred_element_type=F32)


def dot_nt(left, right):
    return lax.dot_general(left, right, (((1,), (1,)), ((), ())), preferred_element_type=F32)


def dot_tn(left, right):
    return lax.dot_general(left, right, (((0,), (0,)), ((), ())), preferred_element_type=F32)


def normalised(values):
    average = jnp.mean(values, -1, keepdims=True)
    centred = values - average
    spread = jnp.mean(centred * centred, -1, keepdims=True)
    scale = lax.rsqrt(spread + norm_epsilon)
    return centred * scale, scale


def norm_back(cotangent, hat, scale, gain):
    inner = cotangent * gain
    first = jnp.mean(inner, -1, keepdims=True)
    second = jnp.mean(inner * hat, -1, keepdims=True)
    return scale * (inner - first - hat * second)


ROWS = 256
TOK_TILES_MAX = 8


def layer_kernel(
    time_ref, split_ref, slot_ref, tok_ref, grad_ref, table_ref, blocks_ref, vec_ref,
    out_ref, in_grad_ref, parts_ref, dvec_ref,
    step_ref, par, dpar, table_rows, h0, a, qkv, prob, mixed, h1, c, acc_o, acc_d, r, du, dqkv,
    w_qkv, w_out, w_up, w_down, stage, emit, step_sem, table_sem, stage_sem, emit_sem,
):
    tok_rows = tok_ref.shape[0]
    tiles = tok_rows // TILE
    row_tiles = tok_rows // ROWS
    first_tile = lax.axis_index("seq") * tiles

    def block_of(chunk, i, j):
        if isinstance(chunk, int) and chunk < 3:
            return i * 12 + chunk * 4 + j
        if isinstance(chunk, int) and chunk == 3:
            return 48 + i * 4 + j
        raise ValueError

    def up_block(part, i, j):
        return 64 + i * 16 + part * 4 + j

    def down_block(part, i, j):
        return 128 + part * 16 + i * 4 + j

    def fetch(buffer, block):
        for i in range(4):
            for j in range(4):
                pltpu.make_async_copy(
                    blocks_ref.at[slot_ref[block(i, j)]], stage.at[buffer, i * 4 + j], stage_sem.at[buffer]
                ).start()

    def settle(buffer):
        pltpu.make_async_copy(stage.at[buffer], stage.at[buffer], stage_sem.at[buffer]).wait()

    def assemble(buffer, dst):
        def row_block(i, carry):
            for j in range(4):
                tile = i * 4 + j
                top = pl.ds(pl.multiple_of(i * BLK, 64), HALF)
                low = pl.ds(pl.multiple_of(i * BLK + HALF, 32), HALF)
                dst[top, j * BLK : (j + 1) * BLK] = stage[buffer, tile, :, 0:BLK]
                dst[low, j * BLK : (j + 1) * BLK] = stage[buffer, tile, :, BLK:WIDE]
            return carry

        lax.fori_loop(0, 4, row_block, 0)

    def emit_wait(buffer):
        pltpu.make_async_copy(emit.at[buffer], emit.at[buffer], emit_sem.at[buffer]).wait()

    def emit_rows(buffer, i, value):
        low = value.astype(BF16)
        for j in range(4):
            emit[buffer, i * 4 + j, :, 0:BLK] = low[0:HALF, j * BLK : (j + 1) * BLK]
            emit[buffer, i * 4 + j, :, BLK:WIDE] = low[HALF:BLK, j * BLK : (j + 1) * BLK]

    def emit_send(buffer, block):
        for i in range(4):
            for j in range(4):
                pltpu.make_async_copy(
                    emit.at[buffer, i * 4 + j], parts_ref.at[slot_ref[block(i, j)]], emit_sem.at[buffer]
                ).start()

    def weight_grad(buffer, left, right, block):
        total = dot_tn(left, right)
        for i in range(4):
            emit_rows(buffer, i, total[i * BLK : (i + 1) * BLK])
        emit_send(buffer, block)

    steps_in = pltpu.make_async_copy(time_ref, step_ref, step_sem)
    steps_in.start()
    fetch(0, functools.partial(block_of, 0))
    fetch(1, functools.partial(block_of, 1))
    steps_in.wait()
    for t in range(tiles):
        for e in range(2):
            step = step_ref[0, first_tile + t] if e == 0 else step_ref[split_ref[first_tile + t], first_tile + t]
            pltpu.make_async_copy(table_ref.at[step // 16], table_rows.at[t * 2 + e], table_sem).start()

    if len(vec_ref.shape) == 3:
        for owner in range(vec_ref.shape[0]):
            par[0:12, owner * 96 : (owner + 1) * 96] = vec_ref[owner, 0:12, 0:96].astype(BF16).astype(F32)
    else:
        par[0:12, :] = vec_ref[...].astype(BF16).astype(F32)
    dpar[...] = jnp.zeros_like(dpar)

    def param(row):
        return par[row : row + 1, :]

    def add_grad(row, value):
        dpar[row : row + 1, :] = dpar[row : row + 1, :] + value

    def col_sum(value):
        return jnp.sum(value.astype(F32), 0, keepdims=True)

    pltpu.make_async_copy(table_rows, table_rows, table_sem).wait()
    rows_iota = lax.broadcasted_iota(jnp.int32, (16, D), 0)
    for t in range(tiles):
        for e in range(2):
            step = step_ref[0, first_tile + t] if e == 0 else step_ref[split_ref[first_tile + t], first_tile + t]
            chosen = jnp.sum(jnp.where(rows_iota == step % 16, table_rows[t * 2 + e].astype(F32), 0.0), 0, keepdims=True)
            span = slice(t * TILE + e * 64, t * TILE + (e + 1) * 64)
            value = tok_ref[span, :].astype(F32) + chosen
            h0[span, :] = value
            hat, _ = normalised(value)
            a[span, :] = (hat * param(0) + param(2)).astype(BF16)

    for n in range(3):
        settle(n % 2)
        assemble(n % 2, w_qkv.at[n])
        if n == 0:
            fetch(0, functools.partial(block_of, 2))
        elif n == 1:
            fetch(1, functools.partial(block_of, 3))
        else:
            fetch(0, functools.partial(up_block, 0))
        for m in range(row_tiles):
            span = slice(m * ROWS, (m + 1) * ROWS)
            value = dot_nn(a[span, :], w_qkv[n])
            if n == 0:
                value = value + param(4)
            elif n == 2:
                value = value + param(5)
            qkv[n, span, :] = value.astype(BF16)
    settle(1)
    assemble(1, w_out)
    fetch(1, functools.partial(down_block, 0))

    lane = lax.broadcasted_iota(jnp.int32, (TILE, TILE), 1)
    first_head = lane < HD
    row_half = lax.broadcasted_iota(jnp.int32, (2 * TILE, TILE), 0) % TILE // (TILE // 2)
    col_half = lax.broadcasted_iota(jnp.int32, (2 * TILE, TILE), 1) // (TILE // 2)
    same_half = row_half == col_half

    def both(value):
        zero = jnp.zeros_like(value)
        return jnp.concatenate([jnp.where(first_head, value, zero), jnp.where(first_head, zero, value)], 0)

    def side(value):
        return jnp.concatenate([value[0:TILE], value[TILE : 2 * TILE]], 1)

    def attend(t, carry):
        whole = split_ref[first_tile + t] == 0
        allowed = jnp.logical_or(same_half, whole)
        span = pl.ds(pl.multiple_of(t * TILE, TILE), TILE)
        for p in range(HEADS // 2):
            cols = slice(p * TILE, (p + 1) * TILE)
            score = dot_nt(both(qkv[0, span, cols]), qkv[1, span, cols]) * score_scale
            score = jnp.where(allowed, score, masked_score)
            exponent = jnp.exp(score - jnp.max(score, -1, keepdims=True))
            weight = (exponent * (1.0 / jnp.sum(exponent, -1, keepdims=True))).astype(BF16)
            prob[t, p] = weight
            mixed[span, cols] = dot_nn(side(weight), both(qkv[2, span, cols])).astype(BF16)
        return carry

    lax.fori_loop(0, tiles, attend, 0)

    for m in range(row_tiles):
        span = slice(m * ROWS, (m + 1) * ROWS)
        value = h0[span, :] + (dot_nn(mixed[span, :], w_out[...]) + param(6))
        h1[span, :] = value
        hat, _ = normalised(value)
        c[span, :] = (hat * param(1) + param(3)).astype(BF16)
        acc_o[span, :] = value + param(7)
        acc_d[span, :] = jnp.zeros_like(value)

    def feed(part, carry):
        settle(0)
        assemble(0, w_up)

        @pl.when(part < 3)
        def _():
            fetch(0, functools.partial(up_block, part + 1))

        settle(1)
        assemble(1, w_down)

        @pl.when(part < 3)
        def _():
            fetch(1, functools.partial(down_block, part + 1))

        bias = par[pl.ds(8 + part, 1), :]
        bias_grad = jnp.zeros((1, D), F32)
        for m in range(row_tiles):
            span = slice(m * ROWS, (m + 1) * ROWS)
            upper = dot_nn(c[span, :], w_up[...]) + bias
            back = dot_nt(grad_ref[span, :], w_down[...])
            below = 0.5 + 0.5 * lax.erf(upper * 0.7071067811865476)
            density = jnp.exp(upper * upper * -0.5) * 0.3989422804014327
            active = (upper * below).astype(BF16)
            grad_upper = (back * (below + upper * density)).astype(BF16)
            r[span, :] = active
            du[span, :] = grad_upper
            bias_grad = bias_grad + col_sum(grad_upper)
            acc_o[span, :] = acc_o[span, :] + dot_nn(active, w_down[...])
            acc_d[span, :] = acc_d[span, :] + dot_nt(grad_upper, w_up[...])
        dpar[pl.ds(8 + part, 1), :] = bias_grad

        @pl.when(part > 0)
        def _():
            emit_wait(0)
            emit_wait(1)

        weight_grad(0, r[...], grad_ref[...], functools.partial(down_block, part))
        weight_grad(1, c[...], du[...], functools.partial(up_block, part))
        return carry

    lax.fori_loop(0, 4, feed, 0)

    for m in range(row_tiles):
        span = slice(m * ROWS, (m + 1) * ROWS)
        out_ref[span, :] = acc_o[span, :].astype(BF16)
        hat, scale = normalised(h1[span, :])
        cotangent = acc_d[span, :]
        upstream = grad_ref[span, :].astype(F32)
        add_grad(1, col_sum(cotangent * hat))
        add_grad(3, col_sum(cotangent))
        add_grad(7, col_sum(upstream))
        value = upstream + norm_back(cotangent, hat, scale, param(1))
        acc_d[span, :] = value
        rounded = value.astype(BF16)
        c[span, :] = rounded
        add_grad(6, col_sum(rounded))
        r[span, :] = dot_nt(rounded, w_out[...]).astype(BF16)
    emit_wait(0)
    weight_grad(0, mixed[...], c[...], functools.partial(block_of, 3))

    def attend_back(t, carry):
        span = pl.ds(pl.multiple_of(t * TILE, TILE), TILE)
        for p in range(HEADS // 2):
            cols = slice(p * TILE, (p + 1) * TILE)
            cotangent = both(r[span, cols])
            weight = prob[t, p]
            wide = weight.astype(F32)
            back = dot_nt(cotangent, qkv[2, span, cols])
            score_grad = (wide * (back - jnp.sum(wide * back, -1, keepdims=True))).astype(BF16)
            dqkv[0, span, cols] = (dot_nn(side(score_grad), both(qkv[1, span, cols])) * score_scale).astype(BF16)
            dqkv[1, span, cols] = (dot_tn(score_grad, both(qkv[0, span, cols])) * score_scale).astype(BF16)
            dqkv[2, span, cols] = dot_tn(weight, cotangent).astype(BF16)
        return carry

    lax.fori_loop(0, tiles, attend_back, 0)

    for n in range(3):
        emit_wait((n + 1) % 2)
        weight_grad((n + 1) % 2, a[...], dqkv[n], functools.partial(block_of, n))
    add_grad(4, col_sum(dqkv[0]))
    add_grad(5, col_sum(dqkv[2]))
    for m in range(row_tiles):
        span = slice(m * ROWS, (m + 1) * ROWS)
        cotangent = dot_nt(dqkv[0, span, :], w_qkv[0]) + dot_nt(dqkv[1, span, :], w_qkv[1]) + dot_nt(dqkv[2, span, :], w_qkv[2])
        hat, scale = normalised(h0[span, :])
        add_grad(0, col_sum(cotangent * hat))
        add_grad(2, col_sum(cotangent))
        in_grad_ref[span, :] = (acc_d[span, :] + norm_back(cotangent, hat, scale, param(0))).astype(BF16)
    if len(dvec_ref.shape) == 3:
        dvec_ref[...] = jnp.zeros_like(dvec_ref)
        for owner in range(dvec_ref.shape[0]):
            dvec_ref[owner, 0:12, 0:96] = dpar[0:12, owner * 96 : (owner + 1) * 96]
    else:
        dvec_ref[...] = dpar[0:12, :]
    emit_wait(0)
    emit_wait(1)


def run_layer(tokens, out_grad, table, time_step, tile_split, block_slot, blocks, vecs):
    tok_rows = tokens.shape[0]
    tiles = tok_rows // TILE
    smem = pl.BlockSpec(memory_space=pltpu.SMEM)
    vmem = pl.BlockSpec(memory_space=pltpu.VMEM)
    hbm = pl.BlockSpec(memory_space=pl.ANY)
    dvec_shape = vecs.shape
    return pl.pallas_call(
        layer_kernel,
        out_shape=(
            jax.ShapeDtypeStruct((tok_rows, D), BF16),
            jax.ShapeDtypeStruct((tok_rows, D), BF16),
            jax.ShapeDtypeStruct((NBLK, HALF, WIDE), BF16),
            jax.ShapeDtypeStruct(dvec_shape, F32),
        ),
        in_specs=[hbm, smem, smem, vmem, vmem, hbm, hbm, vmem],
        out_specs=(vmem, vmem, hbm, vmem),
        scratch_shapes=[
            pltpu.SMEM(time_step.shape, jnp.int32),
            pltpu.VMEM((16, D), F32),
            pltpu.VMEM((16, D), F32),
            pltpu.VMEM((2 * tiles, 16, D), BF16),
            pltpu.VMEM((tok_rows, D), F32),
            pltpu.VMEM((tok_rows, D), BF16),
            pltpu.VMEM((3, tok_rows, D), BF16),
            pltpu.VMEM((tiles, HEADS // 2, 2 * TILE, TILE), BF16),
            pltpu.VMEM((tok_rows, D), BF16),
            pltpu.VMEM((tok_rows, D), F32),
            pltpu.VMEM((tok_rows, D), BF16),
            pltpu.VMEM((tok_rows, D), F32),
            pltpu.VMEM((tok_rows, D), F32),
            pltpu.VMEM((tok_rows, D), BF16),
            pltpu.VMEM((tok_rows, D), BF16),
            pltpu.VMEM((3, tok_rows, D), BF16),
            pltpu.VMEM((3, D, D), BF16),
            pltpu.VMEM((D, D), BF16),
            pltpu.VMEM((D, D), BF16),
            pltpu.VMEM((D, D), BF16),
            pltpu.VMEM((2, 16, HALF, WIDE), BF16),
            pltpu.VMEM((2, 16, HALF, WIDE), BF16),
            pltpu.SemaphoreType.DMA,
            pltpu.SemaphoreType.DMA,
            pltpu.SemaphoreType.DMA((2,)),
            pltpu.SemaphoreType.DMA((2,)),
        ],
        compiler_params=pltpu.CompilerParams(vmem_limit_bytes=60 * MIB),
        name="layer",
    )(time_step, tile_split, block_slot, tokens, out_grad, table.reshape(-1, 16, D), blocks, vecs)


CHUNKS = 12
ROWS_CHIP = 48
SPAN = 384


def chip_row(position):
    chip, q = position // ROWS_CHIP, position % ROWS_CHIP
    wide = q // 8 * BLK + chip * 8 + q % 8
    narrow = (q - 32) // 4 * BLK + 128 + chip * 4 + q % 4
    return jnp.where(q < 32, wide, narrow)


def chunk_block(n, i, j):
    if isinstance(n, int) and n < 3:
        return i * 12 + n * 4 + j
    if isinstance(n, int) and n == 3:
        return 48 + i * 4 + j
    raise ValueError


def deal_kernel(slots_ref, order_ref, vec_ref, pieces_ref, vecs_ref, raw, out, vec_own, raw_sem, own_sem, vec_sem, send_sem, recv_sem, vsend, vrecv):
    z, x, y, c = place()
    me = z * 2 + x
    far = [(z + d) % 4 for d in (1, 2, 3)]
    xt = (1 - c) * x + c * (1 - x)
    quarter = y * 2 + c
    across_x = (z * 2 + (1 - x), quarter)
    across_c = (me, y * 2 + (1 - c))
    partners = [(f * 2 + x, quarter) for f in far] + [(f * 2 + (1 - x), quarter) for f in far] + [across_x]
    loads = [
        pltpu.make_async_copy(slots_ref.at[pl.ds(8 * j, 8)], raw.at[pl.ds(8 * j, 8)], raw_sem.at[j]) for j in range(3)
    ]
    for load in loads:
        load.start()
    vec_own[...] = jnp.zeros_like(vec_own)
    vec_own[0:12, 0:96] = vec_ref[...]
    greet(partners + [across_c])
    vcopies = Copies(vsend, vrecv)
    for i in range(7):
        vcopies.start(i, vec_own, vecs_ref.at[me], partners[i])
    local_vec = pltpu.make_async_copy(vec_own, vecs_ref.at[me], vec_sem)
    local_vec.start()

    order = order_ref[...]
    index = lax.broadcasted_iota(jnp.int32, order.shape, 1)
    up = jnp.logical_and(index >= 64, index < 128)

    def deal(s, carry):
        block = raw[s]
        hit = jnp.max(jnp.where(jnp.logical_and(up, order == me * 24 + s), 1, 0), 1, keepdims=True)
        block = jnp.where(hit > 0, jnp.transpose(block, (1, 0)), block)
        for e in range(16):
            out[e, s, :, 0:BLK] = block[8 * e : 8 * e + 8].astype(BF16)
            out[e, s, :, BLK:WIDE] = block[128 + 8 * (e // 2) : 136 + 8 * (e // 2)].astype(BF16)
        return carry

    copies = Copies(send_sem, recv_sem)

    def part_of(ref, j):
        return ref.at[pl.ds(8 * j, 8)]

    def straight(j):
        return pltpu.make_async_remote_copy(
            src_ref=part_of(out.at[z * 4 + xt * 2 + y], j), dst_ref=part_of(pieces_ref.at[me], j),
            send_sem=send_sem.at[j, 3], recv_sem=recv_sem.at[j, 3],
            device_id=across_x, device_id_type=MESH,
        )

    def stays(j):
        return pltpu.make_async_copy(part_of(out.at[z * 4 + x * 2 + y], j), part_of(pieces_ref.at[me], j), own_sem.at[j])

    def from_owner(zz, j):
        return part_of(pieces_ref.at[zz * 2 + xt], j)

    def pass_on(j):
        pl.when(c == 1)(lambda: straight(j).wait())
        pl.when(c == 0)(lambda: stays(j).wait())
        copies.start((j, 7), from_owner(z, j), from_owner(z, j), across_c)
        for i, d in enumerate((1, 2, 3)):
            ref = from_owner((z - d) % 4, j)
            copies.wait((j, i), ref, across_c)
            copies.start((j, 4 + i), ref, ref, across_c)

    for j in range(3):
        loads[j].wait()
        lax.fori_loop(8 * j, 8 * j + 8, deal, 0)
        for i in range(3):
            copies.start((j, i), part_of(out.at[far[i] * 4 + xt * 2 + y], j), part_of(pieces_ref.at[me], j), (far[i] * 2 + xt, quarter))
        pl.when(c == 1)(lambda: straight(j).start())
        pl.when(c == 0)(lambda: stays(j).start())
    for j in range(3):
        pass_on(j)
    for j in range(3):
        for i, d in enumerate((1, 2, 3)):
            copies.wait((j, 4 + i), part_of(pieces_ref.at[((z - d) % 4) * 2 + (1 - xt)], j), across_c)
        copies.wait((j, 7), part_of(pieces_ref.at[z * 2 + (1 - xt)], j), across_c)
    for i, d in enumerate((1, 2, 3)):
        vcopies.wait(i, vecs_ref.at[((z - d) % 4) * 2 + x], across_c)
        vcopies.wait(3 + i, vecs_ref.at[((z - d) % 4) * 2 + (1 - x)], across_c)
    vcopies.wait(6, vecs_ref.at[z * 2 + (1 - x)], across_c)
    local_vec.wait()
    copies.finish()
    vcopies.finish()


def deal_weights(slots, order, vectors):
    hbm = pl.BlockSpec(memory_space=pl.ANY)
    vmem = pl.BlockSpec(memory_space=pltpu.VMEM)
    return pl.pallas_call(
        deal_kernel,
        out_shape=(
            jax.ShapeDtypeStruct((8, 24, 8, WIDE), BF16),
            jax.ShapeDtypeStruct((8, 16, 128), F32),
        ),
        in_specs=[hbm, vmem, vmem],
        out_specs=(hbm, hbm),
        scratch_shapes=[
            pltpu.VMEM((24, BLK, BLK), F32),
            pltpu.VMEM((16, 24, 8, WIDE), BF16),
            pltpu.VMEM((16, 128), F32),
            pltpu.SemaphoreType.DMA((3,)),
            pltpu.SemaphoreType.DMA((3,)),
            pltpu.SemaphoreType.DMA,
            pltpu.SemaphoreType.DMA((3, 8)),
            pltpu.SemaphoreType.DMA((3, 8)),
            pltpu.SemaphoreType.DMA((7,)),
            pltpu.SemaphoreType.DMA((7,)),
        ],
        compiler_params=pltpu.CompilerParams(collective_id=2, has_side_effects=True, vmem_limit_bytes=60 * MIB),
        name="deal_weights",
    )(slots, order, vectors)


def stream_kernel(
    rows_ref, split_ref, slot_ref, tok_hbm, grad_hbm, pieces_ref, vec_ref,
    out_hbm, in_grad_hbm, fin_hbm, dvec_ref,
    par, dpar, bias_up, perm, lay_buf, tok, grad, pieces, hat_one, scale_one, a, qkv, prob, o, hat_two, scale_two,
    c_in, acc_o, acc_d, du, w, dw, from_core, from_first, from_second, from_z, fin,
    in_sem, out_sem, ag_send, ag_recv, rs_send, rs_recv,
):
    tok_rows = tok.shape[0]
    tiles = tok_rows // TILE
    row_tiles = tok_rows // ROWS
    z, x, y, c = place()
    first_tile = (y * 2 + c) * tiles
    me = z * 2 + x
    quarter = y * 2 + c
    fx, fy = (1 - c) * (1 - x) + c * x, (1 - c) * y + c * (1 - y)
    sx, sy = (1 - c) * x + c * (1 - x), (1 - c) * (1 - y) + c * y
    ox, oy = 1 - x, 1 - y
    first = (z * 2 + fx, fy * 2 + c)
    second = (z * 2 + sx, sy * 2 + c)
    across_c = (me, y * 2 + (1 - c))
    far = [(z + d) % 4 for d in (1, 2, 3)]
    near = [(z - d) % 4 for d in (1, 2, 3)]
    along_z = [(f * 2 + x, quarter) for f in far]
    half = pl.ds(pl.multiple_of(c * SPAN, SPAN), SPAN)
    other_half = pl.ds(pl.multiple_of((1 - c) * SPAN, SPAN), SPAN)

    def remote(src, dst, send, recv, device):
        return pltpu.make_async_remote_copy(
            src_ref=src, dst_ref=dst, send_sem=send, recv_sem=recv, device_id=device, device_id_type=MESH
        )

    loads = [
        pltpu.make_async_copy(pieces_ref, pieces, in_sem.at[0]),
        pltpu.make_async_copy(tok_hbm, tok, in_sem.at[1]),
        pltpu.make_async_copy(grad_hbm, grad, in_sem.at[2]),
    ]
    for load in loads:
        load.start()
    greet([first, second, across_c] + along_z)

    def one(n, zz):
        return w.at[n, zz, x, y, :, half]

    def four(n, xx, yy, lanes):
        return w.at[n, :, xx, yy, :, lanes]

    def ag(n, i, ref, device):
        return remote(ref, ref, ag_send.at[n, i], ag_recv.at[n, i], device)

    def gather_start(n):
        for i in range(3):
            ag(n, i, one(n, z), along_z[i]).start()

    def gather_one(n):
        for i in range(3):
            ag(n, i, one(n, near[i]), along_z[i]).wait_recv()
        ref = four(n, x, y, half)
        ag(n, 3, ref, first).start()
        ag(n, 4, ref, second).start()
        ag(n, 6, ref, across_c).start()

    def gather_two(n):
        ref = four(n, fx, fy, half)
        ag(n, 3, ref, first).wait_recv()
        ag(n, 5, ref, second).start()
        ag(n, 7, ref, across_c).start()

    def gather_three(n):
        ref = four(n, sx, sy, half)
        ag(n, 4, ref, second).wait_recv()
        ag(n, 8, ref, across_c).start()
        ref = four(n, ox, oy, half)
        ag(n, 5, ref, second).wait_recv()
        ag(n, 9, ref, across_c).start()

    def gather_four(n):
        for i, (xx, yy) in ((6, (x, y)), (7, (sx, sy)), (8, (fx, fy)), (9, (ox, oy))):
            ag(n, i, four(n, xx, yy, other_half), across_c).wait_recv()

    def guarded(run, n):
        if isinstance(n, int):
            if 0 <= n < CHUNKS:
                run(n)
        else:
            pl.when(jnp.logical_and(n >= 0, n < CHUNKS))(lambda: run(n))

    def gather_step(t):
        guarded(gather_one, t)
        guarded(gather_start, t + 3)
        guarded(gather_two, t - 1)
        guarded(gather_three, t - 2)
        guarded(gather_four, t - 3)

    def rs(n, i, src, dst, device):
        return remote(src, dst, rs_send.at[n, i], rs_recv.at[n, i], device)

    def core_copy(n, slot):
        return rs(n, 0, dw.at[slot, :, :, :, :, other_half], from_core.at[n], across_c)

    def sum_start(n, slot):
        core_copy(n, slot).start()

    def sum_one(n, slot):
        core_copy(n, slot).wait_recv()

        def add(zz, carry):
            for xx in range(2):
                for yy in range(2):
                    from_core[n, zz, xx, yy] = from_core[n, zz, xx, yy] + dw[slot, zz, xx, yy, :, half]
            return carry

        lax.fori_loop(0, 4, add, 0)
        rs(n, 1, from_core.at[n, :, sx, sy], from_first.at[n, 0], second).start()
        rs(n, 2, from_core.at[n, :, ox, oy], from_first.at[n, 1], second).start()
        core_copy(n, slot).wait_send()

    def sum_two(n):
        for i in range(2):
            rs(n, 1 + i, from_first.at[n, i], from_first.at[n, i], second).wait_recv()

        def add(zz, carry):
            from_core[n, zz, fx, fy] = from_core[n, zz, fx, fy] + from_first[n, 1, zz]
            return carry

        lax.fori_loop(0, 4, add, 0)
        rs(n, 3, from_core.at[n, :, fx, fy], from_second.at[n], first).start()

    def sum_three(n):
        rs(n, 3, from_second.at[n], from_second.at[n], first).wait_recv()

        def add(zz, carry):
            from_core[n, zz, x, y] = from_core[n, zz, x, y] + from_first[n, 0, zz] + from_second[n, zz]
            return carry

        lax.fori_loop(0, 4, add, 0)
        for i in range(3):
            rs(n, 4 + i, from_core.at[n, far[i], x, y], from_z.at[n, i], along_z[i]).start()

    def sum_four(n):
        for i in range(3):
            rs(n, 4 + i, from_z.at[n, i], from_z.at[n, i], along_z[i]).wait_recv()
        total = from_core[n, z, x, y].astype(F32)
        for i in range(3):
            total = total + from_z[n, i].astype(F32)
        fin[n] = total.astype(BF16)

    def sum_step(t, slot):
        guarded(lambda n: sum_one(n, slot), t)
        guarded(sum_two, t - 1)
        guarded(sum_three, t - 2)
        guarded(sum_four, t - 3)

    loads[0].wait()

    def lay(n, block):
        for j in range(4):
            wide, narrow = [], []
            for i in range(4):
                piece = pieces[slot_ref[block(i, j)]].astype(F32)
                wide.append(piece[:, 0:BLK])
                extra = piece[:, BLK:WIDE]
                narrow.append(jnp.where(y == 0, extra[0:4], extra[4:8]))
            lay_buf[:, j * BLK : (j + 1) * BLK] = jnp.concatenate(wide + narrow, 0).astype(BF16)
        w[n, z, x, y, :, half] = lay_buf[:, half]

    for n in range(4):
        lay(n, functools.partial(chunk_block, n))
        if n < 3:
            gather_start(n)

    def lay_feed(part, carry):
        lay(4 + 2 * part, lambda i, j: 64 + j * 16 + part * 4 + i)
        lay(5 + 2 * part, lambda i, j: 128 + part * 16 + i * 4 + j)
        return carry

    lax.fori_loop(0, 4, lay_feed, 0)

    par[...] = jnp.zeros_like(par)
    for owner in range(8):
        par[0:12, owner * 96 : (owner + 1) * 96] = vec_ref[owner, 0:12, 0:96].astype(BF16).astype(F32)
    dpar[...] = jnp.zeros_like(dpar)
    chosen_row = chip_row(lax.broadcasted_iota(jnp.int32, (8, D), 1))
    row_index = lax.broadcasted_iota(jnp.int32, (16, D), 0)
    chosen_row = jnp.concatenate([chosen_row, chosen_row], 0)

    def perm_rows(i, carry):
        perm[pl.ds(pl.multiple_of(i * 16, 16), 16), :] = jnp.where(chosen_row == row_index + i * 16, 1.0, 0.0).astype(BF16)
        return carry

    lax.fori_loop(0, D // 16, perm_rows, 0)
    bias_up[...] = dot_nn(par[8:16, :].astype(BF16), perm[...])

    def param(row):
        return par[row : row + 1, :]

    def add_grad(row, value):
        dpar[row : row + 1, :] = dpar[row : row + 1, :] + value

    def col_sum(value):
        return jnp.sum(value.astype(F32), 0, keepdims=True)

    def span_of(m):
        return slice(m * ROWS, (m + 1) * ROWS)

    def weights(n):
        return w[n].reshape(D, D)

    loads[1].wait()
    loads[2].wait()
    for t in range(tiles):
        for e in range(2):
            span = slice(t * TILE + e * 64, t * TILE + (e + 1) * 64)
            value = tok[span, :].astype(F32) + rows_ref[2 * t + e : 2 * t + e + 1, :]
            acc_o[span, :] = value
            hat, scale = normalised(value)
            hat_one[span, :] = hat.astype(BF16)
            scale_one[span, :] = scale
            c_in[span, :] = (hat * param(0) + param(2)).astype(BF16)
    for m in range(row_tiles):
        a[span_of(m), :] = dot_nn(c_in[span_of(m), :], perm[...]).astype(BF16)

    for t in range(4):
        gather_step(t)
    for n in range(3):
        for m in range(row_tiles):
            value = dot_nn(a[span_of(m), :], weights(n))
            if n == 0:
                value = value + param(4)
            elif n == 2:
                value = value + param(5)
            qkv[n, span_of(m), :] = value.astype(BF16)
        gather_step(4 + n)

    lane = lax.broadcasted_iota(jnp.int32, (TILE, TILE), 1)
    first_head = lane < HD
    row_half = lax.broadcasted_iota(jnp.int32, (2 * TILE, TILE), 0) % TILE // (TILE // 2)
    col_half = lax.broadcasted_iota(jnp.int32, (2 * TILE, TILE), 1) // (TILE // 2)
    same_half = row_half == col_half

    def both(value):
        zero = jnp.zeros_like(value)
        return jnp.concatenate([jnp.where(first_head, value, zero), jnp.where(first_head, zero, value)], 0)

    def side(value):
        return jnp.concatenate([value[0:TILE], value[TILE : 2 * TILE]], 1)

    def attend(t, carry):
        whole = split_ref[first_tile + t] == 0
        allowed = jnp.logical_or(same_half, whole)
        span = pl.ds(pl.multiple_of(t * TILE, TILE), TILE)
        for p in range(HEADS // 2):
            cols = slice(p * TILE, (p + 1) * TILE)
            score = dot_nt(both(qkv[0, span, cols]), qkv[1, span, cols]) * score_scale
            score = jnp.where(allowed, score, masked_score)
            exponent = jnp.exp(score - jnp.max(score, -1, keepdims=True))
            weight = (exponent * (1.0 / jnp.sum(exponent, -1, keepdims=True))).astype(BF16)
            prob[t, p] = weight
            c_in[span, cols] = dot_nn(side(weight), both(qkv[2, span, cols])).astype(BF16)
        return carry

    def by_two(run):
        def two_tiles(t, carry):
            for e in range(2):
                run(2 * t + e, carry)
            return carry

        return two_tiles

    lax.fori_loop(0, tiles // 4, by_two(attend), 0)
    gather_step(7)
    lax.fori_loop(tiles // 4, tiles // 2, by_two(attend), 0)

    for m in range(row_tiles):
        span = span_of(m)
        o[span, :] = dot_nn(c_in[span, :], perm[...]).astype(BF16)
        value = acc_o[span, :] + (dot_nn(o[span, :], weights(3)) + param(6))
        hat, scale = normalised(value)
        hat_two[span, :] = hat.astype(BF16)
        scale_two[span, :] = scale
        c_in[span, :] = (hat * param(1) + param(3)).astype(BF16)
        acc_o[span, :] = value + param(7)
        acc_d[span, :] = jnp.zeros_like(value)
    gather_step(8)

    def feed(part, carry):
        up, down = 4 + 2 * part, 5 + 2 * part
        bias = bias_up[pl.ds(part, 1), :]
        bias_grad = jnp.zeros((1, D), F32)
        for m in range(row_tiles):
            span = span_of(m)
            upper = dot_nt(c_in[span, :], weights(up)) + bias
            back = dot_nt(grad[span, :], weights(down))
            below = 0.5 + 0.5 * lax.erf(upper * 0.7071067811865476)
            density = jnp.exp(upper * upper * -0.5) * 0.3989422804014327
            active = (upper * below).astype(BF16)
            grad_upper = (back * (below + upper * density)).astype(BF16)
            tok[span, :] = active
            du[span, :] = grad_upper
            bias_grad = bias_grad + col_sum(grad_upper)
            acc_o[span, :] = acc_o[span, :] + dot_nn(active, weights(down))
            acc_d[span, :] = acc_d[span, :] + dot_nn(grad_upper, weights(up))
            if m == 0:
                gather_step(9 + 2 * part)
            elif m == 1:
                pl.when(part > 0)(lambda: sum_step(2 * part - 2, 0))
            elif m == 2:
                gather_step(10 + 2 * part)
            else:
                pl.when(part > 0)(lambda: sum_step(2 * part - 1, 1))
        dpar[pl.ds(8 + part, 1), :] = bias_grad
        dw[0] = dot_tn(tok[...], grad[...]).astype(BF16).reshape(4, 2, 2, ROWS_CHIP, D)
        sum_start(2 * part, 0)
        dw[1] = dot_tn(du[...], c_in[...]).astype(BF16).reshape(4, 2, 2, ROWS_CHIP, D)
        sum_start(2 * part + 1, 1)
        return carry

    lax.fori_loop(0, 4, feed, 0)

    for m in range(row_tiles):
        span = span_of(m)
        du[span, :] = acc_o[span, :].astype(BF16)
        hat = hat_two[span, :].astype(F32)
        cotangent = acc_d[span, :]
        upstream = grad[span, :].astype(F32)
        add_grad(1, col_sum(cotangent * hat))
        add_grad(3, col_sum(cotangent))
        add_grad(7, col_sum(upstream))
        value = upstream + norm_back(cotangent, hat, scale_two[span, :], param(1))
        acc_d[span, :] = value
        rounded = value.astype(BF16)
        c_in[span, :] = rounded
        add_grad(6, col_sum(rounded))
        mixed_grad = dot_nt(rounded, weights(3)).astype(BF16)
        tok[span, :] = dot_nt(mixed_grad, perm[...]).astype(BF16)
        if m == 0:
            sum_step(6, 0)
        elif m == 2:
            sum_step(7, 1)
    out_copy = pltpu.make_async_copy(du, out_hbm, out_sem.at[0])
    out_copy.start()
    dw[0] = dot_tn(o[...], c_in[...]).astype(BF16).reshape(4, 2, 2, ROWS_CHIP, D)
    sum_start(8, 0)

    def attend_back(t, carry):
        span = pl.ds(pl.multiple_of(t * TILE, TILE), TILE)
        for p in range(HEADS // 2):
            cols = slice(p * TILE, (p + 1) * TILE)
            cotangent = both(tok[span, cols])
            weight = prob[t, p]
            wide = weight.astype(F32)
            queries, keys = both(qkv[0, span, cols]), both(qkv[1, span, cols])
            back = dot_nt(cotangent, qkv[2, span, cols])
            score_grad = (wide * (back - jnp.sum(wide * back, -1, keepdims=True))).astype(BF16)
            qkv[0, span, cols] = (dot_nn(side(score_grad), keys) * score_scale).astype(BF16)
            qkv[1, span, cols] = (dot_tn(score_grad, queries) * score_scale).astype(BF16)
            qkv[2, span, cols] = dot_tn(weight, cotangent).astype(BF16)
        return carry

    lax.fori_loop(0, 1, by_two(attend_back), 0)
    sum_step(8, 0)
    lax.fori_loop(1, 3, by_two(attend_back), 0)
    sum_two(8)
    sum_three(7)
    sum_four(6)
    lax.fori_loop(3, tiles // 2, by_two(attend_back), 0)

    for n in range(3):
        slot = (n + 1) % 2
        dw[slot] = dot_tn(a[...], qkv[n]).astype(BF16).reshape(4, 2, 2, ROWS_CHIP, D)
        sum_start(9 + n, slot)
        if n == 0:
            sum_three(8)
            sum_four(7)
        else:
            sum_one(8 + n, (n + 0) % 2)
            if n == 1:
                sum_four(8)
            else:
                sum_two(9)
    add_grad(4, col_sum(qkv[0]))
    add_grad(5, col_sum(qkv[2]))
    for m in range(row_tiles):
        span = span_of(m)
        cotangent = dot_nt(qkv[0, span, :], weights(0)) + dot_nt(qkv[1, span, :], weights(1)) + dot_nt(qkv[2, span, :], weights(2))
        cotangent = dot_nt(cotangent.astype(BF16), perm[...])
        hat = hat_one[span, :].astype(F32)
        add_grad(0, col_sum(cotangent * hat))
        add_grad(2, col_sum(cotangent))
        grad[span, :] = (acc_d[span, :] + norm_back(cotangent, hat, scale_one[span, :], param(0))).astype(BF16)
        if m == 0:
            sum_one(11, 1)
            sum_two(10)
            sum_three(9)
        elif m == 2:
            sum_two(11)
            sum_three(10)
            sum_four(9)
    in_grad_copy = pltpu.make_async_copy(grad, in_grad_hbm, out_sem.at[1])
    in_grad_copy.start()

    rest = dpar[8:16, :]
    ordered = jnp.zeros((8, D), F32)
    for _ in range(3):
        low = rest.astype(BF16)
        ordered = ordered + dot_nt(low, perm[...])
        rest = rest - low.astype(F32)
    dpar[8:16, :] = ordered
    dvec_ref[...] = jnp.zeros_like(dvec_ref)
    for owner in range(8):
        dvec_ref[owner, 0:12, 0:96] = dpar[0:12, owner * 96 : (owner + 1) * 96]

    sum_three(11)
    sum_four(10)
    sum_four(11)
    fin_copy = pltpu.make_async_copy(fin, fin_hbm, out_sem.at[2])
    fin_copy.start()

    def finish(n, carry):
        for i in range(3):
            ag(n, i, one(n, z), along_z[i]).wait_send()
        for i in range(3, 10):
            ag(n, i, four(n, x, y, half), across_c).wait_send()
        for i in range(1, 4):
            rs(n, i, from_core.at[n, :, x, y], from_second.at[n], first).wait_send()
        for i in range(4, 7):
            rs(n, i, from_core.at[n, z, x, y], from_z.at[n, 0], first).wait_send()
        return carry

    lax.fori_loop(0, CHUNKS, finish, 0)
    out_copy.wait()
    in_grad_copy.wait()
    fin_copy.wait()


def rows_kernel(step_ref, split_ref, table_ref, rows_ref, groups, sem):
    count = rows_ref.shape[0]
    first = lax.axis_index("seq") * (count // 2)

    def step_of(i):
        tile = first + i // 2
        return step_ref[0, tile] if i % 2 == 0 else step_ref[split_ref[tile], tile]

    for i in range(count):
        pltpu.make_async_copy(table_ref.at[step_of(i) // 16], groups.at[i], sem).start()
    pltpu.make_async_copy(groups, groups, sem).wait()
    row_index = lax.broadcasted_iota(jnp.int32, (16, D), 0)
    for i in range(count):
        picked = jnp.where(row_index == step_of(i) % 16, groups[i].astype(F32), 0.0)
        rows_ref[i : i + 1, :] = jnp.sum(picked, 0, keepdims=True)


def pick_rows(time_step, tile_split, table, count):
    smem = pl.BlockSpec(memory_space=pltpu.SMEM)
    return pl.pallas_call(
        rows_kernel,
        out_shape=jax.ShapeDtypeStruct((count, D), F32),
        in_specs=[smem, smem, pl.BlockSpec(memory_space=pl.ANY)],
        out_specs=pl.BlockSpec(memory_space=pltpu.VMEM),
        scratch_shapes=[pltpu.VMEM((count, 16, D), BF16), pltpu.SemaphoreType.DMA],
        compiler_params=pltpu.CompilerParams(vmem_limit_bytes=60 * MIB),
        name="pick_rows",
    )(time_step, tile_split, table.reshape(-1, 16, D))


def run_stream(tokens, out_grad, rows, tile_split, block_slot, pieces, vecs):
    tok_rows = tokens.shape[0]
    tiles = tok_rows // TILE
    smem = pl.BlockSpec(memory_space=pltpu.SMEM)
    vmem = pl.BlockSpec(memory_space=pltpu.VMEM)
    hbm = pl.BlockSpec(memory_space=pl.ANY)
    rows_low = pltpu.VMEM((tok_rows, D), BF16)
    rows_full = pltpu.VMEM((tok_rows, D), F32)
    rows_one = pltpu.VMEM((tok_rows, 1), F32)
    return pl.pallas_call(
        stream_kernel,
        out_shape=(
            jax.ShapeDtypeStruct((tok_rows, D), BF16),
            jax.ShapeDtypeStruct((tok_rows, D), BF16),
            jax.ShapeDtypeStruct((CHUNKS, ROWS_CHIP, SPAN), BF16),
            jax.ShapeDtypeStruct(vecs.shape, F32),
        ),
        in_specs=[vmem, smem, smem, hbm, hbm, hbm, vmem],
        out_specs=(hbm, hbm, hbm, vmem),
        scratch_shapes=[
            pltpu.VMEM((16, D), F32),
            pltpu.VMEM((16, D), F32),
            pltpu.VMEM((8, D), F32),
            pltpu.VMEM((D, D), BF16),
            pltpu.VMEM((ROWS_CHIP, D), BF16),
            rows_low,
            rows_low,
            pltpu.VMEM((NBLK, 8, WIDE), BF16),
            rows_low,
            rows_one,
            rows_low,
            pltpu.VMEM((3, tok_rows, D), BF16),
            pltpu.VMEM((tiles, HEADS // 2, 2 * TILE, TILE), BF16),
            rows_low,
            rows_low,
            rows_one,
            rows_low,
            rows_full,
            rows_full,
            rows_low,
            pltpu.VMEM((CHUNKS, 4, 2, 2, ROWS_CHIP, D), BF16),
            pltpu.VMEM((2, 4, 2, 2, ROWS_CHIP, D), BF16),
            pltpu.VMEM((CHUNKS, 4, 2, 2, ROWS_CHIP, SPAN), BF16),
            pltpu.VMEM((CHUNKS, 2, 4, ROWS_CHIP, SPAN), BF16),
            pltpu.VMEM((CHUNKS, 4, ROWS_CHIP, SPAN), BF16),
            pltpu.VMEM((CHUNKS, 3, ROWS_CHIP, SPAN), BF16),
            pltpu.VMEM((CHUNKS, ROWS_CHIP, SPAN), BF16),
            pltpu.SemaphoreType.DMA((3,)),
            pltpu.SemaphoreType.DMA((3,)),
            pltpu.SemaphoreType.DMA((CHUNKS, 10)),
            pltpu.SemaphoreType.DMA((CHUNKS, 10)),
            pltpu.SemaphoreType.DMA((CHUNKS, 7)),
            pltpu.SemaphoreType.DMA((CHUNKS, 7)),
        ],
        compiler_params=pltpu.CompilerParams(collective_id=3, has_side_effects=True, vmem_limit_bytes=63 * MIB),
        name="stream",
    )(rows, tile_split, block_slot, tokens, out_grad, pieces, vecs)


def collect_kernel(
    inverse_ref, fin_ref, dvec_ref, gp_ref, vsum_ref,
    full, by_block, out, va, vb, vz, load_sem, own_sem, send_sem, recv_sem, vload_sem, vsend, vrecv,
):
    z, x, y, c = place()
    me = z * 2 + x
    quarter = y * 2 + c
    far = [(z + d) % 4 for d in (1, 2, 3)]
    near = [(z - d) % 4 for d in (1, 2, 3)]
    xt = (1 - c) * x + c * (1 - x)
    across_x = (z * 2 + (1 - x), quarter)
    across_y = (me, (1 - y) * 2 + c)
    across_c = (me, y * 2 + (1 - c))
    along_z = [(f * 2 + x, quarter) for f in far]
    skew = [(f * 2 + (1 - x), quarter) for f in far]
    half = pl.ds(pl.multiple_of(c * SPAN, SPAN), SPAN)
    own_half = pltpu.make_async_copy(fin_ref, full.at[:, :, half], load_sem)
    own_half.start()
    vec_load = pltpu.make_async_copy(dvec_ref, vb.at[0], vload_sem)
    vec_load.start()
    greet([across_x, across_y, across_c] + along_z + skew)
    copies = Copies(send_sem, recv_sem)
    vcopies = Copies(vsend, vrecv)
    copies.start(16, fin_ref, full.at[:, :, half], across_c)
    vcopies.start(0, dvec_ref, va, across_c)
    own_half.wait()
    copies.wait(16, full.at[:, :, pl.ds(pl.multiple_of((1 - c) * SPAN, SPAN), SPAN)], across_c)

    mine = lax.broadcasted_iota(jnp.int32, (8, BLK), 0) // 4 == y

    def split_chunk(n, block):
        for j in range(4):
            column = full[n, :, j * BLK : (j + 1) * BLK].astype(F32)
            for i in range(4):
                extra = column[32 + 4 * i : 36 + 4 * i]
                extra = jnp.where(mine, jnp.concatenate([extra, extra], 0), 0.0)
                by_block[block(i, j), :, 0:BLK] = column[8 * i : 8 * i + 8].astype(BF16)
                by_block[block(i, j), :, BLK:WIDE] = extra.astype(BF16)

    def split_feed(part, carry):
        split_chunk(2 * part, lambda i, j: 128 + part * 16 + i * 4 + j)
        split_chunk(2 * part + 1, lambda i, j: 64 + j * 16 + part * 4 + i)
        return carry

    lax.fori_loop(0, 4, split_feed, 0)
    split_chunk(8, functools.partial(chunk_block, 3))
    for n in range(3):
        split_chunk(9 + n, functools.partial(chunk_block, n))

    def pick(s, carry):
        out[s] = by_block[inverse_ref[s]]
        return carry

    def owner_part(zz):
        return out.at[pl.ds((zz * 2 + xt) * 24, 24)]

    def pick_part(zz):
        lax.fori_loop((zz * 2 + xt) * 24, (zz * 2 + xt) * 24 + 24, pick, 0)

    def chip(zz, xx, yy):
        return gp_ref.at[zz * 4 + xx * 2 + yy]

    for i in (1, 0, 2):
        pick_part(far[i])
        copies.start(i, owner_part(far[i]), chip(z, x, y), (far[i] * 2 + xt, quarter))
    pick_part(z)

    def straight():
        return pltpu.make_async_remote_copy(
            src_ref=owner_part(z), dst_ref=chip(z, x, y), send_sem=send_sem.at[3], recv_sem=recv_sem.at[3],
            device_id=across_x, device_id_type=MESH,
        )

    def stays():
        return pltpu.make_async_copy(owner_part(z), chip(z, x, y), own_sem)

    pl.when(c == 1)(lambda: straight().start())
    pl.when(c == 0)(lambda: stays().start())

    vec_load.wait()
    vcopies.wait(0, va, across_c)
    va[...] = va[...] + vb[0]
    vcopies.start(1, va, vb.at[1], across_y)

    pl.when(c == 1)(lambda: straight().wait())
    pl.when(c == 0)(lambda: stays().wait())
    ref = chip(z, xt, y)
    copies.start(7, ref, ref, across_y)
    copies.start(11, ref, ref, across_c)
    for i in range(3):
        ref = chip(near[i], xt, y)
        copies.wait(i, ref, across_c)
        copies.start(4 + i, ref, ref, across_y)
        copies.start(8 + i, ref, ref, across_c)
        if i == 0:
            vcopies.wait(1, vb.at[1], across_y)
            vb[1] = va[...] + vb[1]
            vcopies.start(2, vb.at[1], vb.at[2], across_x)
        elif i == 1:
            vcopies.wait(2, vb.at[2], across_x)
            vb[3] = vb[1] + vb[2]
            for k in range(3):
                vcopies.start(3 + k, vb.at[3, far[k] * 2 + x], vz.at[k], along_z[k])
    for i, zz in ((3, z), (0, near[0]), (1, near[1]), (2, near[2])):
        ref = chip(zz, xt, 1 - y)
        copies.wait(4 + i, ref, across_y)
        copies.start(12 + i, ref, ref, across_c)
    for i in range(3):
        vcopies.wait(3 + i, vz.at[i], across_c)
    vsum_ref[...] = vb[3, me] + vz[0] + vz[1] + vz[2]
    for i, zz in ((3, z), (0, near[0]), (1, near[1]), (2, near[2])):
        copies.wait(8 + i, chip(zz, 1 - xt, y), across_c)
        copies.wait(12 + i, chip(zz, 1 - xt, 1 - y), across_c)
    copies.finish()
    vcopies.finish()


def collect_sums(inverse, fin, dvec):
    hbm = pl.BlockSpec(memory_space=pl.ANY)
    return pl.pallas_call(
        collect_kernel,
        out_shape=(
            jax.ShapeDtypeStruct((16, 24, 8, WIDE), BF16),
            jax.ShapeDtypeStruct((16, 128), F32),
        ),
        in_specs=[pl.BlockSpec(memory_space=pltpu.SMEM), hbm, hbm],
        out_specs=(hbm, pl.BlockSpec(memory_space=pltpu.VMEM)),
        scratch_shapes=[
            pltpu.VMEM((CHUNKS, ROWS_CHIP, D), BF16),
            pltpu.VMEM((NBLK, 8, WIDE), BF16),
            pltpu.VMEM((NBLK, 8, WIDE), BF16),
            pltpu.VMEM((8, 16, 128), F32),
            pltpu.VMEM((4, 8, 16, 128), F32),
            pltpu.VMEM((3, 16, 128), F32),
            pltpu.SemaphoreType.DMA,
            pltpu.SemaphoreType.DMA,
            pltpu.SemaphoreType.DMA((17,)),
            pltpu.SemaphoreType.DMA((17,)),
            pltpu.SemaphoreType.DMA,
            pltpu.SemaphoreType.DMA((6,)),
            pltpu.SemaphoreType.DMA((6,)),
        ],
        compiler_params=pltpu.CompilerParams(collective_id=4, has_side_effects=True, vmem_limit_bytes=16 * MIB),
        name="collect_sums",
    )(inverse, fin, dvec)


def dot_split(left, right):
    left_high, right_high = left.astype(BF16), right.astype(BF16)
    left_low = (left - left_high.astype(F32)).astype(BF16)
    right_low = (right - right_high.astype(F32)).astype(BF16)
    return dot_nn(left_high, right_high) + (dot_nn(left_low, right_high) + dot_nn(left_high, right_low))


def step_kernel(
    items_count, inverse_ref, sum_ref, vsum_ref, weight_ref, momentum_ref, left_ref, right_ref, root_l_ref, root_r_ref,
    vec_ref, first_ref, second_ref,
    grad_out, momentum_out, weight_out, left_out, right_out, vgrad_out, first_out, second_out, vec_out,
):
    inverse = 1.0 / items_count
    count = weight_ref.shape[0]
    for s in range(count):
        if len(sum_ref.shape) == 4:
            wide = sum_ref[:, s, :, 0:BLK].astype(F32).reshape(128, BLK)
            narrow = sum_ref[:, s, :, BLK:WIDE].astype(F32).reshape(8, 2, 8, BLK)
            grad = jnp.concatenate([wide, (narrow[:, 0] + narrow[:, 1]).reshape(64, BLK)], 0)
            block = inverse_ref[(lax.axis_index("items") * pl.num_programs(0) + pl.program_id(0)) * count + s]
            up = jnp.logical_and(block >= 64, block < 128)
            grad = jnp.where(up, jnp.transpose(grad, (1, 0)), grad) * inverse
        else:
            packed = sum_ref[s]
            grad = jnp.concatenate([packed[:, 0:BLK], packed[:, BLK:WIDE]], 0).astype(F32) * inverse
        low = grad.astype(BF16)
        grad_out[s] = grad
        momentum = 0.9 * momentum_ref[s] + grad
        momentum_out[s] = momentum
        left_out[s] = 0.95 * left_ref[s] + 0.05 * dot_nt(low, low)
        right_out[s] = 0.95 * right_ref[s] + 0.05 * dot_tn(low, low)
        direction = dot_split(dot_split(root_l_ref[s], momentum), root_r_ref[s])
        weight = weight_ref[s]
        scale = jnp.sqrt(jnp.mean(weight * weight) + 1e-06) * lax.rsqrt(jnp.mean(direction * direction) + 1e-06)
        weight_out[s] = weight - (0.3 * scale) * direction

    @pl.when(pl.program_id(0) == 0)
    def _():
        rows, cols = vec_ref.shape
        grad = vsum_ref[0:rows, 0:cols] * inverse
        vgrad_out[...] = grad
        first = 0.9 * first_ref[...] + 0.1 * grad
        second = 0.999 * second_ref[...] + 0.001 * grad * grad
        first_out[...] = first
        second_out[...] = second
        vec_out[...] = vec_ref[...] - 0.1 * first / (jnp.sqrt(second) + 1e-08)


def run_step(items_count, inverse, sums, vsums, weights, momentum, left, right, root_l, root_r, vectors, first, second):
    count = weights.shape[0]
    per = 6 if count % 6 == 0 else 3
    block = pl.BlockSpec((per, BLK, BLK), lambda i: (i, 0, 0))
    if len(sums.shape) == 4:
        packed = pl.BlockSpec((16, per, 8, WIDE), lambda i: (0, i, 0, 0))
    else:
        packed = pl.BlockSpec((per, HALF, WIDE), lambda i: (i, 0, 0))
    small = pl.BlockSpec(vectors.shape, lambda i: (0, 0))
    vsum = pl.BlockSpec(vsums.shape, lambda i: (0, 0))
    slots = jax.ShapeDtypeStruct(weights.shape, F32)
    vec = jax.ShapeDtypeStruct(vectors.shape, F32)
    return pl.pallas_call(
        functools.partial(step_kernel, items_count),
        grid=(count // per,),
        out_shape=(slots,) * 5 + (vec,) * 4,
        in_specs=[pl.BlockSpec(memory_space=pltpu.SMEM), packed, vsum] + [block] * 6 + [small] * 3,
        out_specs=[block] * 5 + [small] * 4,
        compiler_params=pltpu.CompilerParams(vmem_limit_bytes=50 * MIB),
        name="step",
    )(inverse, sums, vsums, weights, momentum, left, right, root_l, root_r, vectors, first, second)


def body(
    tokens, out_grad, time_table, time_step, tile_split, block_slot, weight_slots, momentum_slots,
    stat_left, stat_right, root_left, root_right, vectors, vector_first, vector_second,
):
    items_count = lax.axis_size("items")
    spots = jnp.arange(NBLK, dtype=jnp.int32)
    inverse = jnp.sum(jnp.where(block_slot[None, :] == spots[:, None], spots[None, :], 0), 1)
    if items_count == 8 and lax.axis_size("seq") == 4:
        pieces, vecs = deal_weights(weight_slots, block_slot.reshape(1, NBLK), vectors)
        rows = pick_rows(time_step.T, tile_split, time_table, 2 * tokens.shape[0] // TILE)
        output, input_grad, fin, dvec = run_stream(
            tokens, out_grad, rows, tile_split, block_slot, pieces.reshape(NBLK, 8, WIDE), vecs
        )
        sums, vsums = collect_sums(inverse, fin, dvec)
    else:
        low = weight_slots.astype(BF16)
        blocks = lax.all_gather(jnp.concatenate([low[:, :HALF], low[:, HALF:]], 2), "items", axis=0, tiled=True)
        vecs = lax.all_gather(vectors, "items", axis=1, tiled=True)
        output, input_grad, parts, dvec = run_layer(
            tokens, out_grad, time_table, time_step.T, tile_split, block_slot, blocks, vecs
        )
        sums = lax.psum_scatter(parts.astype(F32), "items", scatter_dimension=0, tiled=True)
        vsums = lax.psum_scatter(dvec, "items", scatter_dimension=1, tiled=True)
        sums, vsums = lax.psum((sums, vsums), "seq")
    stepped = run_step(
        items_count, inverse, sums, vsums, weight_slots, momentum_slots, stat_left, stat_right, root_left, root_right,
        vectors, vector_first, vector_second,
    )
    grad, momentum, weights, left, right, vgrad, first, second, vecs_new = stepped
    return output, input_grad, grad, momentum, weights, left, right, vgrad, first, second, vecs_new


def solution(mesh):
    return jax.shard_map(
        body,
        mesh=mesh,
        in_specs=(
            P(("items", "seq"), None),
            P(("items", "seq"), None),
            P(),
            P("items", None),
            P("items"),
            P(),
            P("items", None, None),
            P("items", None, None),
            P("items", None, None),
            P("items", None, None),
            P("items", None, None),
            P("items", None, None),
            P(None, "items"),
            P(None, "items"),
            P(None, "items"),
        ),
        out_specs=(
            P(("items", "seq"), None),
            P(("items", "seq"), None),
            P("items", None, None),
            P("items", None, None),
            P("items", None, None),
            P("items", None, None),
            P("items", None, None),
            P(None, "items"),
            P(None, "items"),
            P(None, "items"),
            P(None, "items"),
        ),
        check_vma=False,
    )
```

```python
import functools
import jax
import jax.numpy as jnp
from jax import lax
from jax.experimental import pallas as pl
from jax.experimental.pallas import tpu as pltpu
from jax.sharding import PartitionSpec as P

D = 768
HEADS = 12
HD = 64
TILE = 128
BLK = 192
NBLK = 192
HALF = 96
WIDE = 384
MESH = pl.DeviceIdType.MESH
BF16 = jnp.bfloat16
F32 = jnp.float32
MIB = 2 ** 20
highest = lax.Precision.HIGHEST
masked_score = -1000000000.0
norm_epsilon = 1e-05
score_scale = HD ** (-0.5)


def place():
    it = lax.axis_index("items")
    sq = lax.axis_index("seq")
    return it // 2, it % 2, sq // 2, sq % 2


def greet(partners):
    barrier = pltpu.get_barrier_semaphore()
    for partner in partners:
        pl.semaphore_signal(barrier, inc=1, device_id=partner, device_id_type=MESH)
    pl.semaphore_wait(barrier, len(partners))


class Copies:
    def __init__(self, send_sem, recv_sem):
        self.send_sem, self.recv_sem = send_sem, recv_sem
        self.sent = []

    def start(self, index, src, dst, device):
        made = pltpu.make_async_remote_copy(
            src_ref=src, dst_ref=dst,
            send_sem=self.send_sem.at[index], recv_sem=self.recv_sem.at[index],
            device_id=device, device_id_type=MESH,
        )
        made.start()
        self.sent.append(made)

    def wait(self, index, dst, device):
        pltpu.make_async_remote_copy(
            src_ref=dst, dst_ref=dst,
            send_sem=self.send_sem.at[index], recv_sem=self.recv_sem.at[index],
            device_id=device, device_id_type=MESH,
        ).wait_recv()

    def finish(self):
        for made in self.sent:
            made.wait_send()


def dot_nn(left, right):
    return jnp.dot(left, right, preferred_element_type=F32)


def dot_nt(left, right):
    return lax.dot_general(left, right, (((1,), (1,)), ((), ())), preferred_element_type=F32)


def dot_tn(left, right):
    return lax.dot_general(left, right, (((0,), (0,)), ((), ())), preferred_element_type=F32)


def normalised(values):
    average = jnp.mean(values, -1, keepdims=True)
    centred = values - average
    spread = jnp.mean(centred * centred, -1, keepdims=True)
    scale = lax.rsqrt(spread + norm_epsilon)
    return centred * scale, scale


def norm_back(cotangent, hat, scale, gain):
    inner = cotangent * gain
    first = jnp.mean(inner, -1, keepdims=True)
    second = jnp.mean(inner * hat, -1, keepdims=True)
    return scale * (inner - first - hat * second)


ROWS = 256
TOK_TILES_MAX = 8


def layer_kernel(
    time_ref, split_ref, slot_ref, tok_ref, grad_ref, table_ref, blocks_ref, vec_ref,
    out_ref, in_grad_ref, parts_ref, dvec_ref,
    step_ref, par, dpar, table_rows, h0, a, qkv, prob, mixed, h1, c, acc_o, acc_d, r, du, dqkv,
    w_qkv, w_out, w_up, w_down, stage, emit, step_sem, table_sem, stage_sem, emit_sem,
):
    tok_rows = tok_ref.shape[0]
    tiles = tok_rows // TILE
    row_tiles = tok_rows // ROWS
    first_tile = lax.axis_index("seq") * tiles

    def block_of(chunk, i, j):
        if isinstance(chunk, int) and chunk < 3:
            return i * 12 + chunk * 4 + j
        if isinstance(chunk, int) and chunk == 3:
            return 48 + i * 4 + j
        raise ValueError

    def up_block(part, i, j):
        return 64 + i * 16 + part * 4 + j

    def down_block(part, i, j):
        return 128 + part * 16 + i * 4 + j

    def fetch(buffer, block):
        for i in range(4):
            for j in range(4):
                pltpu.make_async_copy(
                    blocks_ref.at[slot_ref[block(i, j)]], stage.at[buffer, i * 4 + j], stage_sem.at[buffer]
                ).start()

    def settle(buffer):
        pltpu.make_async_copy(stage.at[buffer], stage.at[buffer], stage_sem.at[buffer]).wait()

    def assemble(buffer, dst):
        def row_block(i, carry):
            for j in range(4):
                tile = i * 4 + j
                top = pl.ds(pl.multiple_of(i * BLK, 64), HALF)
                low = pl.ds(pl.multiple_of(i * BLK + HALF, 32), HALF)
                dst[top, j * BLK : (j + 1) * BLK] = stage[buffer, tile, :, 0:BLK]
                dst[low, j * BLK : (j + 1) * BLK] = stage[buffer, tile, :, BLK:WIDE]
            return carry

        lax.fori_loop(0, 4, row_block, 0)

    def emit_wait(buffer):
        pltpu.make_async_copy(emit.at[buffer], emit.at[buffer], emit_sem.at[buffer]).wait()

    def emit_rows(buffer, i, value):
        low = value.astype(BF16)
        for j in range(4):
            emit[buffer, i * 4 + j, :, 0:BLK] = low[0:HALF, j * BLK : (j + 1) * BLK]
            emit[buffer, i * 4 + j, :, BLK:WIDE] = low[HALF:BLK, j * BLK : (j + 1) * BLK]

    def emit_send(buffer, block):
        for i in range(4):
            for j in range(4):
                pltpu.make_async_copy(
                    emit.at[buffer, i * 4 + j], parts_ref.at[slot_ref[block(i, j)]], emit_sem.at[buffer]
                ).start()

    def weight_grad(buffer, left, right, block):
        total = dot_tn(left, right)
        for i in range(4):
            emit_rows(buffer, i, total[i * BLK : (i + 1) * BLK])
        emit_send(buffer, block)

    steps_in = pltpu.make_async_copy(time_ref, step_ref, step_sem)
    steps_in.start()
    fetch(0, functools.partial(block_of, 0))
    fetch(1, functools.partial(block_of, 1))
    steps_in.wait()
    for t in range(tiles):
        for e in range(2):
            step = step_ref[0, first_tile + t] if e == 0 else step_ref[split_ref[first_tile + t], first_tile + t]
            pltpu.make_async_copy(table_ref.at[step // 16], table_rows.at[t * 2 + e], table_sem).start()

    if len(vec_ref.shape) == 3:
        for owner in range(vec_ref.shape[0]):
            par[0:12, owner * 96 : (owner + 1) * 96] = vec_ref[owner, 0:12, 0:96].astype(BF16).astype(F32)
    else:
        par[0:12, :] = vec_ref[...].astype(BF16).astype(F32)
    dpar[...] = jnp.zeros_like(dpar)

    def param(row):
        return par[row : row + 1, :]

    def add_grad(row, value):
        dpar[row : row + 1, :] = dpar[row : row + 1, :] + value

    def col_sum(value):
        return jnp.sum(value.astype(F32), 0, keepdims=True)

    pltpu.make_async_copy(table_rows, table_rows, table_sem).wait()
    rows_iota = lax.broadcasted_iota(jnp.int32, (16, D), 0)
    for t in range(tiles):
        for e in range(2):
            step = step_ref[0, first_tile + t] if e == 0 else step_ref[split_ref[first_tile + t], first_tile + t]
            chosen = jnp.sum(jnp.where(rows_iota == step % 16, table_rows[t * 2 + e].astype(F32), 0.0), 0, keepdims=True)
            span = slice(t * TILE + e * 64, t * TILE + (e + 1) * 64)
            value = tok_ref[span, :].astype(F32) + chosen
            h0[span, :] = value
            hat, _ = normalised(value)
            a[span, :] = (hat * param(0) + param(2)).astype(BF16)

    for n in range(3):
        settle(n % 2)
        assemble(n % 2, w_qkv.at[n])
        if n == 0:
            fetch(0, functools.partial(block_of, 2))
        elif n == 1:
            fetch(1, functools.partial(block_of, 3))
        else:
            fetch(0, functools.partial(up_block, 0))
        for m in range(row_tiles):
            span = slice(m * ROWS, (m + 1) * ROWS)
            value = dot_nn(a[span, :], w_qkv[n])
            if n == 0:
                value = value + param(4)
            elif n == 2:
                value = value + param(5)
            qkv[n, span, :] = value.astype(BF16)
    settle(1)
    assemble(1, w_out)
    fetch(1, functools.partial(down_block, 0))

    lane = lax.broadcasted_iota(jnp.int32, (TILE, TILE), 1)
    first_head = lane < HD
    row_half = lax.broadcasted_iota(jnp.int32, (2 * TILE, TILE), 0) % TILE // (TILE // 2)
    col_half = lax.broadcasted_iota(jnp.int32, (2 * TILE, TILE), 1) // (TILE // 2)
    same_half = row_half == col_half

    def both(value):
        zero = jnp.zeros_like(value)
        return jnp.concatenate([jnp.where(first_head, value, zero), jnp.where(first_head, zero, value)], 0)

    def side(value):
        return jnp.concatenate([value[0:TILE], value[TILE : 2 * TILE]], 1)

    def attend(t, carry):
        whole = split_ref[first_tile + t] == 0
        allowed = jnp.logical_or(same_half, whole)
        span = pl.ds(pl.multiple_of(t * TILE, TILE), TILE)
        for p in range(HEADS // 2):
            cols = slice(p * TILE, (p + 1) * TILE)
            score = dot_nt(both(qkv[0, span, cols]), qkv[1, span, cols]) * score_scale
            score = jnp.where(allowed, score, masked_score)
            exponent = jnp.exp(score - jnp.max(score, -1, keepdims=True))
            weight = (exponent * (1.0 / jnp.sum(exponent, -1, keepdims=True))).astype(BF16)
            prob[t, p] = weight
            mixed[span, cols] = dot_nn(side(weight), both(qkv[2, span, cols])).astype(BF16)
        return carry

    lax.fori_loop(0, tiles, attend, 0)

    for m in range(row_tiles):
        span = slice(m * ROWS, (m + 1) * ROWS)
        value = h0[span, :] + (dot_nn(mixed[span, :], w_out[...]) + param(6))
        h1[span, :] = value
        hat, _ = normalised(value)
        c[span, :] = (hat * param(1) + param(3)).astype(BF16)
        acc_o[span, :] = value + param(7)
        acc_d[span, :] = jnp.zeros_like(value)

    def feed(part, carry):
        settle(0)
        assemble(0, w_up)

        @pl.when(part < 3)
        def _():
            fetch(0, functools.partial(up_block, part + 1))

        settle(1)
        assemble(1, w_down)

        @pl.when(part < 3)
        def _():
            fetch(1, functools.partial(down_block, part + 1))

        bias = par[pl.ds(8 + part, 1), :]
        bias_grad = jnp.zeros((1, D), F32)
        for m in range(row_tiles):
            span = slice(m * ROWS, (m + 1) * ROWS)
            upper = dot_nn(c[span, :], w_up[...]) + bias
            back = dot_nt(grad_ref[span, :], w_down[...])
            below = 0.5 + 0.5 * lax.erf(upper * 0.7071067811865476)
            density = jnp.exp(upper * upper * -0.5) * 0.3989422804014327
            active = (upper * below).astype(BF16)
            grad_upper = (back * (below + upper * density)).astype(BF16)
            r[span, :] = active
            du[span, :] = grad_upper
            bias_grad = bias_grad + col_sum(grad_upper)
            acc_o[span, :] = acc_o[span, :] + dot_nn(active, w_down[...])
            acc_d[span, :] = acc_d[span, :] + dot_nt(grad_upper, w_up[...])
        dpar[pl.ds(8 + part, 1), :] = bias_grad

        @pl.when(part > 0)
        def _():
            emit_wait(0)
            emit_wait(1)

        weight_grad(0, r[...], grad_ref[...], functools.partial(down_block, part))
        weight_grad(1, c[...], du[...], functools.partial(up_block, part))
        return carry

    lax.fori_loop(0, 4, feed, 0)

    for m in range(row_tiles):
        span = slice(m * ROWS, (m + 1) * ROWS)
        out_ref[span, :] = acc_o[span, :].astype(BF16)
        hat, scale = normalised(h1[span, :])
        cotangent = acc_d[span, :]
        upstream = grad_ref[span, :].astype(F32)
        add_grad(1, col_sum(cotangent * hat))
        add_grad(3, col_sum(cotangent))
        add_grad(7, col_sum(upstream))
        value = upstream + norm_back(cotangent, hat, scale, param(1))
        acc_d[span, :] = value
        rounded = value.astype(BF16)
        c[span, :] = rounded
        add_grad(6, col_sum(rounded))
        r[span, :] = dot_nt(rounded, w_out[...]).astype(BF16)
    emit_wait(0)
    weight_grad(0, mixed[...], c[...], functools.partial(block_of, 3))

    def attend_back(t, carry):
        span = pl.ds(pl.multiple_of(t * TILE, TILE), TILE)
        for p in range(HEADS // 2):
            cols = slice(p * TILE, (p + 1) * TILE)
            cotangent = both(r[span, cols])
            weight = prob[t, p]
            wide = weight.astype(F32)
            back = dot_nt(cotangent, qkv[2, span, cols])
            score_grad = (wide * (back - jnp.sum(wide * back, -1, keepdims=True))).astype(BF16)
            dqkv[0, span, cols] = (dot_nn(side(score_grad), both(qkv[1, span, cols])) * score_scale).astype(BF16)
            dqkv[1, span, cols] = (dot_tn(score_grad, both(qkv[0, span, cols])) * score_scale).astype(BF16)
            dqkv[2, span, cols] = dot_tn(weight, cotangent).astype(BF16)
        return carry

    lax.fori_loop(0, tiles, attend_back, 0)

    for n in range(3):
        emit_wait((n + 1) % 2)
        weight_grad((n + 1) % 2, a[...], dqkv[n], functools.partial(block_of, n))
    add_grad(4, col_sum(dqkv[0]))
    add_grad(5, col_sum(dqkv[2]))
    for m in range(row_tiles):
        span = slice(m * ROWS, (m + 1) * ROWS)
        cotangent = dot_nt(dqkv[0, span, :], w_qkv[0]) + dot_nt(dqkv[1, span, :], w_qkv[1]) + dot_nt(dqkv[2, span, :], w_qkv[2])
        hat, scale = normalised(h0[span, :])
        add_grad(0, col_sum(cotangent * hat))
        add_grad(2, col_sum(cotangent))
        in_grad_ref[span, :] = (acc_d[span, :] + norm_back(cotangent, hat, scale, param(0))).astype(BF16)
    if len(dvec_ref.shape) == 3:
        dvec_ref[...] = jnp.zeros_like(dvec_ref)
        for owner in range(dvec_ref.shape[0]):
            dvec_ref[owner, 0:12, 0:96] = dpar[0:12, owner * 96 : (owner + 1) * 96]
    else:
        dvec_ref[...] = dpar[0:12, :]
    emit_wait(0)
    emit_wait(1)


def run_layer(tokens, out_grad, table, time_step, tile_split, block_slot, blocks, vecs):
    tok_rows = tokens.shape[0]
    tiles = tok_rows // TILE
    smem = pl.BlockSpec(memory_space=pltpu.SMEM)
    vmem = pl.BlockSpec(memory_space=pltpu.VMEM)
    hbm = pl.BlockSpec(memory_space=pl.ANY)
    dvec_shape = vecs.shape
    return pl.pallas_call(
        layer_kernel,
        out_shape=(
            jax.ShapeDtypeStruct((tok_rows, D), BF16),
            jax.ShapeDtypeStruct((tok_rows, D), BF16),
            jax.ShapeDtypeStruct((NBLK, HALF, WIDE), BF16),
            jax.ShapeDtypeStruct(dvec_shape, F32),
        ),
        in_specs=[hbm, smem, smem, vmem, vmem, hbm, hbm, vmem],
        out_specs=(vmem, vmem, hbm, vmem),
        scratch_shapes=[
            pltpu.SMEM(time_step.shape, jnp.int32),
            pltpu.VMEM((16, D), F32),
            pltpu.VMEM((16, D), F32),
            pltpu.VMEM((2 * tiles, 16, D), BF16),
            pltpu.VMEM((tok_rows, D), F32),
            pltpu.VMEM((tok_rows, D), BF16),
            pltpu.VMEM((3, tok_rows, D), BF16),
            pltpu.VMEM((tiles, HEADS // 2, 2 * TILE, TILE), BF16),
            pltpu.VMEM((tok_rows, D), BF16),
            pltpu.VMEM((tok_rows, D), F32),
            pltpu.VMEM((tok_rows, D), BF16),
            pltpu.VMEM((tok_rows, D), F32),
            pltpu.VMEM((tok_rows, D), F32),
            pltpu.VMEM((tok_rows, D), BF16),
            pltpu.VMEM((tok_rows, D), BF16),
            pltpu.VMEM((3, tok_rows, D), BF16),
            pltpu.VMEM((3, D, D), BF16),
            pltpu.VMEM((D, D), BF16),
            pltpu.VMEM((D, D), BF16),
            pltpu.VMEM((D, D), BF16),
            pltpu.VMEM((2, 16, HALF, WIDE), BF16),
            pltpu.VMEM((2, 16, HALF, WIDE), BF16),
            pltpu.SemaphoreType.DMA,
            pltpu.SemaphoreType.DMA,
            pltpu.SemaphoreType.DMA((2,)),
            pltpu.SemaphoreType.DMA((2,)),
        ],
        compiler_params=pltpu.CompilerParams(vmem_limit_bytes=60 * MIB),
        name="layer",
    )(time_step, tile_split, block_slot, tokens, out_grad, table.reshape(-1, 16, D), blocks, vecs)


CHUNKS = 12
ROWS_CHIP = 48
SPAN = 384


def chip_row(position):
    chip, q = position // ROWS_CHIP, position % ROWS_CHIP
    wide = q // 8 * BLK + chip * 8 + q % 8
    narrow = (q - 32) // 4 * BLK + 128 + chip * 4 + q % 4
    return jnp.where(q < 32, wide, narrow)


def chunk_block(n, i, j):
    if isinstance(n, int) and n < 3:
        return i * 12 + n * 4 + j
    if isinstance(n, int) and n == 3:
        return 48 + i * 4 + j
    raise ValueError


def deal_kernel(slots_ref, order_ref, vec_ref, pieces_ref, vecs_ref, raw, out, vec_own, raw_sem, own_sem, vec_sem, send_sem, recv_sem, vsend, vrecv):
    z, x, y, c = place()
    me = z * 2 + x
    far = [(z + d) % 4 for d in (1, 2, 3)]
    xt = (1 - c) * x + c * (1 - x)
    quarter = y * 2 + c
    across_x = (z * 2 + (1 - x), quarter)
    across_c = (me, y * 2 + (1 - c))
    partners = [(f * 2 + x, quarter) for f in far] + [(f * 2 + (1 - x), quarter) for f in far] + [across_x]
    loads = [
        pltpu.make_async_copy(slots_ref.at[pl.ds(8 * j, 8)], raw.at[pl.ds(8 * j, 8)], raw_sem.at[j]) for j in range(3)
    ]
    for load in loads:
        load.start()
    vec_own[...] = jnp.zeros_like(vec_own)
    vec_own[0:12, 0:96] = vec_ref[...]
    greet(partners + [across_c])
    vcopies = Copies(vsend, vrecv)
    for i in range(7):
        vcopies.start(i, vec_own, vecs_ref.at[me], partners[i])
    local_vec = pltpu.make_async_copy(vec_own, vecs_ref.at[me], vec_sem)
    local_vec.start()

    order = order_ref[...]
    index = lax.broadcasted_iota(jnp.int32, order.shape, 1)
    up = jnp.logical_and(index >= 64, index < 128)

    def deal(s, carry):
        block = raw[s]
        hit = jnp.max(jnp.where(jnp.logical_and(up, order == me * 24 + s), 1, 0), 1, keepdims=True)
        block = jnp.where(hit > 0, jnp.transpose(block, (1, 0)), block)
        for e in range(16):
            out[e, s, :, 0:BLK] = block[8 * e : 8 * e + 8].astype(BF16)
            out[e, s, :, BLK:WIDE] = block[128 + 8 * (e // 2) : 136 + 8 * (e // 2)].astype(BF16)
        return carry

    copies = Copies(send_sem, recv_sem)

    def part_of(ref, j):
        return ref.at[pl.ds(8 * j, 8)]

    def straight(j):
        return pltpu.make_async_remote_copy(
            src_ref=part_of(out.at[z * 4 + xt * 2 + y], j), dst_ref=part_of(pieces_ref.at[me], j),
            send_sem=send_sem.at[j, 3], recv_sem=recv_sem.at[j, 3],
            device_id=across_x, device_id_type=MESH,
        )

    def stays(j):
        return pltpu.make_async_copy(part_of(out.at[z * 4 + x * 2 + y], j), part_of(pieces_ref.at[me], j), own_sem.at[j])

    def from_owner(zz, j):
        return part_of(pieces_ref.at[zz * 2 + xt], j)

    def pass_on(j):
        pl.when(c == 1)(lambda: straight(j).wait())
        pl.when(c == 0)(lambda: stays(j).wait())
        copies.start((j, 7), from_owner(z, j), from_owner(z, j), across_c)
        for i, d in enumerate((1, 2, 3)):
            ref = from_owner((z - d) % 4, j)
            copies.wait((j, i), ref, across_c)
            copies.start((j, 4 + i), ref, ref, across_c)

    for j in range(3):
        loads[j].wait()
        lax.fori_loop(8 * j, 8 * j + 8, deal, 0)
        for i in range(3):
            copies.start((j, i), part_of(out.at[far[i] * 4 + xt * 2 + y], j), part_of(pieces_ref.at[me], j), (far[i] * 2 + xt, quarter))
        pl.when(c == 1)(lambda: straight(j).start())
        pl.when(c == 0)(lambda: stays(j).start())
    for j in range(3):
        pass_on(j)
    for j in range(3):
        for i, d in enumerate((1, 2, 3)):
            copies.wait((j, 4 + i), part_of(pieces_ref.at[((z - d) % 4) * 2 + (1 - xt)], j), across_c)
        copies.wait((j, 7), part_of(pieces_ref.at[z * 2 + (1 - xt)], j), across_c)
    for i, d in enumerate((1, 2, 3)):
        vcopies.wait(i, vecs_ref.at[((z - d) % 4) * 2 + x], across_c)
        vcopies.wait(3 + i, vecs_ref.at[((z - d) % 4) * 2 + (1 - x)], across_c)
    vcopies.wait(6, vecs_ref.at[z * 2 + (1 - x)], across_c)
    local_vec.wait()
    copies.finish()
    vcopies.finish()


def deal_weights(slots, order, vectors):
    hbm = pl.BlockSpec(memory_space=pl.ANY)
    vmem = pl.BlockSpec(memory_space=pltpu.VMEM)
    return pl.pallas_call(
        deal_kernel,
        out_shape=(
            jax.ShapeDtypeStruct((8, 24, 8, WIDE), BF16),
            jax.ShapeDtypeStruct((8, 16, 128), F32),
        ),
        in_specs=[hbm, vmem, vmem],
        out_specs=(hbm, hbm),
        scratch_shapes=[
            pltpu.VMEM((24, BLK, BLK), F32),
            pltpu.VMEM((16, 24, 8, WIDE), BF16),
            pltpu.VMEM((16, 128), F32),
            pltpu.SemaphoreType.DMA((3,)),
            pltpu.SemaphoreType.DMA((3,)),
            pltpu.SemaphoreType.DMA,
            pltpu.SemaphoreType.DMA((3, 8)),
            pltpu.SemaphoreType.DMA((3, 8)),
            pltpu.SemaphoreType.DMA((7,)),
            pltpu.SemaphoreType.DMA((7,)),
        ],
        compiler_params=pltpu.CompilerParams(collective_id=2, has_side_effects=True, vmem_limit_bytes=60 * MIB),
        name="deal_weights",
    )(slots, order, vectors)


def stream_kernel(
    rows_ref, split_ref, slot_ref, tok_hbm, grad_hbm, pieces_ref, vec_ref,
    out_hbm, in_grad_hbm, fin_hbm, dvec_ref,
    par, dpar, bias_up, perm, lay_buf, tok, grad, pieces, hat_one, scale_one, a, qkv, prob, o, hat_two, scale_two,
    c_in, acc_o, acc_d, du, w, dw, from_core, from_first, from_second, from_z, fin,
    in_sem, out_sem, ag_send, ag_recv, rs_send, rs_recv,
):
    tok_rows = tok.shape[0]
    tiles = tok_rows // TILE
    row_tiles = tok_rows // ROWS
    z, x, y, c = place()
    first_tile = (y * 2 + c) * tiles
    me = z * 2 + x
    quarter = y * 2 + c
    fx, fy = (1 - c) * (1 - x) + c * x, (1 - c) * y + c * (1 - y)
    sx, sy = (1 - c) * x + c * (1 - x), (1 - c) * (1 - y) + c * y
    ox, oy = 1 - x, 1 - y
    first = (z * 2 + fx, fy * 2 + c)
    second = (z * 2 + sx, sy * 2 + c)
    across_c = (me, y * 2 + (1 - c))
    far = [(z + d) % 4 for d in (1, 2, 3)]
    near = [(z - d) % 4 for d in (1, 2, 3)]
    along_z = [(f * 2 + x, quarter) for f in far]
    half = pl.ds(pl.multiple_of(c * SPAN, SPAN), SPAN)
    other_half = pl.ds(pl.multiple_of((1 - c) * SPAN, SPAN), SPAN)

    def remote(src, dst, send, recv, device):
        return pltpu.make_async_remote_copy(
            src_ref=src, dst_ref=dst, send_sem=send, recv_sem=recv, device_id=device, device_id_type=MESH
        )

    loads = [
        pltpu.make_async_copy(pieces_ref, pieces, in_sem.at[0]),
        pltpu.make_async_copy(tok_hbm, tok, in_sem.at[1]),
        pltpu.make_async_copy(grad_hbm, grad, in_sem.at[2]),
    ]
    for load in loads:
        load.start()
    greet([first, second, across_c] + along_z)

    def one(n, zz):
        return w.at[n, zz, x, y, :, half]

    def four(n, xx, yy, lanes):
        return w.at[n, :, xx, yy, :, lanes]

    def ag(n, i, ref, device):
        return remote(ref, ref, ag_send.at[n, i], ag_recv.at[n, i], device)

    def gather_start(n):
        for i in range(3):
            ag(n, i, one(n, z), along_z[i]).start()

    def gather_one(n):
        for i in range(3):
            ag(n, i, one(n, near[i]), along_z[i]).wait_recv()
        ref = four(n, x, y, half)
        ag(n, 3, ref, first).start()
        ag(n, 4, ref, second).start()
        ag(n, 6, ref, across_c).start()

    def gather_two(n):
        ref = four(n, fx, fy, half)
        ag(n, 3, ref, first).wait_recv()
        ag(n, 5, ref, second).start()
        ag(n, 7, ref, across_c).start()

    def gather_three(n):
        ref = four(n, sx, sy, half)
        ag(n, 4, ref, second).wait_recv()
        ag(n, 8, ref, across_c).start()
        ref = four(n, ox, oy, half)
        ag(n, 5, ref, second).wait_recv()
        ag(n, 9, ref, across_c).start()

    def gather_four(n):
        for i, (xx, yy) in ((6, (x, y)), (7, (sx, sy)), (8, (fx, fy)), (9, (ox, oy))):
            ag(n, i, four(n, xx, yy, other_half), across_c).wait_recv()

    def guarded(run, n):
        if isinstance(n, int):
            if 0 <= n < CHUNKS:
                run(n)
        else:
            pl.when(jnp.logical_and(n >= 0, n < CHUNKS))(lambda: run(n))

    def gather_step(t):
        guarded(gather_one, t)
        guarded(gather_start, t + 3)
        guarded(gather_two, t - 1)
        guarded(gather_three, t - 2)
        guarded(gather_four, t - 3)

    def rs(n, i, src, dst, device):
        return remote(src, dst, rs_send.at[n, i], rs_recv.at[n, i], device)

    def core_copy(n, slot):
        return rs(n, 0, dw.at[slot, :, :, :, :, other_half], from_core.at[n], across_c)

    def sum_start(n, slot):
        core_copy(n, slot).start()

    def sum_one(n, slot):
        core_copy(n, slot).wait_recv()

        def add(zz, carry):
            for xx in range(2):
                for yy in range(2):
                    from_core[n, zz, xx, yy] = from_core[n, zz, xx, yy] + dw[slot, zz, xx, yy, :, half]
            return carry

        lax.fori_loop(0, 4, add, 0)
        rs(n, 1, from_core.at[n, :, sx, sy], from_first.at[n, 0], second).start()
        rs(n, 2, from_core.at[n, :, ox, oy], from_first.at[n, 1], second).start()
        core_copy(n, slot).wait_send()

    def sum_two(n):
        for i in range(2):
            rs(n, 1 + i, from_first.at[n, i], from_first.at[n, i], second).wait_recv()

        def add(zz, carry):
            from_core[n, zz, fx, fy] = from_core[n, zz, fx, fy] + from_first[n, 1, zz]
            return carry

        lax.fori_loop(0, 4, add, 0)
        rs(n, 3, from_core.at[n, :, fx, fy], from_second.at[n], first).start()

    def sum_three(n):
        rs(n, 3, from_second.at[n], from_second.at[n], first).wait_recv()

        def add(zz, carry):
            from_core[n, zz, x, y] = from_core[n, zz, x, y] + from_first[n, 0, zz] + from_second[n, zz]
            return carry

        lax.fori_loop(0, 4, add, 0)
        for i in range(3):
            rs(n, 4 + i, from_core.at[n, far[i], x, y], from_z.at[n, i], along_z[i]).start()

    def sum_four(n):
        for i in range(3):
            rs(n, 4 + i, from_z.at[n, i], from_z.at[n, i], along_z[i]).wait_recv()
        total = from_core[n, z, x, y].astype(F32)
        for i in range(3):
            total = total + from_z[n, i].astype(F32)
        fin[n] = total.astype(BF16)

    def sum_step(t, slot):
        guarded(lambda n: sum_one(n, slot), t)
        guarded(sum_two, t - 1)
        guarded(sum_three, t - 2)
        guarded(sum_four, t - 3)

    loads[0].wait()

    def lay(n, block):
        for j in range(4):
            wide, narrow = [], []
            for i in range(4):
                piece = pieces[slot_ref[block(i, j)]].astype(F32)
                wide.append(piece[:, 0:BLK])
                extra = piece[:, BLK:WIDE]
                narrow.append(jnp.where(y == 0, extra[0:4], extra[4:8]))
            lay_buf[:, j * BLK : (j + 1) * BLK] = jnp.concatenate(wide + narrow, 0).astype(BF16)
        w[n, z, x, y, :, half] = lay_buf[:, half]

    for n in range(4):
        lay(n, functools.partial(chunk_block, n))
        if n < 3:
            gather_start(n)

    def lay_feed(part, carry):
        lay(4 + 2 * part, lambda i, j: 64 + j * 16 + part * 4 + i)
        lay(5 + 2 * part, lambda i, j: 128 + part * 16 + i * 4 + j)
        return carry

    lax.fori_loop(0, 4, lay_feed, 0)

    par[...] = jnp.zeros_like(par)
    for owner in range(8):
        par[0:12, owner * 96 : (owner + 1) * 96] = vec_ref[owner, 0:12, 0:96].astype(BF16).astype(F32)
    dpar[...] = jnp.zeros_like(dpar)
    chosen_row = chip_row(lax.broadcasted_iota(jnp.int32, (8, D), 1))
    row_index = lax.broadcasted_iota(jnp.int32, (16, D), 0)
    chosen_row = jnp.concatenate([chosen_row, chosen_row], 0)

    def perm_rows(i, carry):
        perm[pl.ds(pl.multiple_of(i * 16, 16), 16), :] = jnp.where(chosen_row == row_index + i * 16, 1.0, 0.0).astype(BF16)
        return carry

    lax.fori_loop(0, D // 16, perm_rows, 0)
    bias_up[...] = dot_nn(par[8:16, :].astype(BF16), perm[...])

    def param(row):
        return par[row : row + 1, :]

    def add_grad(row, value):
        dpar[row : row + 1, :] = dpar[row : row + 1, :] + value

    def col_sum(value):
        return jnp.sum(value.astype(F32), 0, keepdims=True)

    def span_of(m):
        return slice(m * ROWS, (m + 1) * ROWS)

    def weights(n):
        return w[n].reshape(D, D)

    loads[1].wait()
    loads[2].wait()
    for t in range(tiles):
        for e in range(2):
            span = slice(t * TILE + e * 64, t * TILE + (e + 1) * 64)
            value = tok[span, :].astype(F32) + rows_ref[2 * t + e : 2 * t + e + 1, :]
            acc_o[span, :] = value
            hat, scale = normalised(value)
            hat_one[span, :] = hat.astype(BF16)
            scale_one[span, :] = scale
            c_in[span, :] = (hat * param(0) + param(2)).astype(BF16)
    for m in range(row_tiles):
        a[span_of(m), :] = dot_nn(c_in[span_of(m), :], perm[...]).astype(BF16)

    for t in range(4):
        gather_step(t)
    for n in range(3):
        for m in range(row_tiles):
            value = dot_nn(a[span_of(m), :], weights(n))
            if n == 0:
                value = value + param(4)
            elif n == 2:
                value = value + param(5)
            qkv[n, span_of(m), :] = value.astype(BF16)
        gather_step(4 + n)

    lane = lax.broadcasted_iota(jnp.int32, (TILE, TILE), 1)
    first_head = lane < HD
    row_half = lax.broadcasted_iota(jnp.int32, (2 * TILE, TILE), 0) % TILE // (TILE // 2)
    col_half = lax.broadcasted_iota(jnp.int32, (2 * TILE, TILE), 1) // (TILE // 2)
    same_half = row_half == col_half

    def both(value):
        zero = jnp.zeros_like(value)
        return jnp.concatenate([jnp.where(first_head, value, zero), jnp.where(first_head, zero, value)], 0)

    def side(value):
        return jnp.concatenate([value[0:TILE], value[TILE : 2 * TILE]], 1)

    def attend(t, carry):
        whole = split_ref[first_tile + t] == 0
        allowed = jnp.logical_or(same_half, whole)
        span = pl.ds(pl.multiple_of(t * TILE, TILE), TILE)
        for p in range(HEADS // 2):
            cols = slice(p * TILE, (p + 1) * TILE)
            score = dot_nt(both(qkv[0, span, cols]), qkv[1, span, cols]) * score_scale
            score = jnp.where(allowed, score, masked_score)
            exponent = jnp.exp(score - jnp.max(score, -1, keepdims=True))
            weight = (exponent * (1.0 / jnp.sum(exponent, -1, keepdims=True))).astype(BF16)
            prob[t, p] = weight
            c_in[span, cols] = dot_nn(side(weight), both(qkv[2, span, cols])).astype(BF16)
        return carry

    def by_two(run):
        def two_tiles(t, carry):
            for e in range(2):
                run(2 * t + e, carry)
            return carry

        return two_tiles

    lax.fori_loop(0, tiles // 4, by_two(attend), 0)
    gather_step(7)
    lax.fori_loop(tiles // 4, tiles // 2, by_two(attend), 0)

    for m in range(row_tiles):
        span = span_of(m)
        o[span, :] = dot_nn(c_in[span, :], perm[...]).astype(BF16)
        value = acc_o[span, :] + (dot_nn(o[span, :], weights(3)) + param(6))
        hat, scale = normalised(value)
        hat_two[span, :] = hat.astype(BF16)
        scale_two[span, :] = scale
        c_in[span, :] = (hat * param(1) + param(3)).astype(BF16)
        acc_o[span, :] = value + param(7)
        acc_d[span, :] = jnp.zeros_like(value)
    gather_step(8)

    def feed(part, carry):
        up, down = 4 + 2 * part, 5 + 2 * part
        bias = bias_up[pl.ds(part, 1), :]
        bias_grad = jnp.zeros((1, D), F32)
        for m in range(row_tiles):
            span = span_of(m)
            upper = dot_nt(c_in[span, :], weights(up)) + bias
            back = dot_nt(grad[span, :], weights(down))
            below = 0.5 + 0.5 * lax.erf(upper * 0.7071067811865476)
            density = jnp.exp(upper * upper * -0.5) * 0.3989422804014327
            active = (upper * below).astype(BF16)
            grad_upper = (back * (below + upper * density)).astype(BF16)
            tok[span, :] = active
            du[span, :] = grad_upper
            bias_grad = bias_grad + col_sum(grad_upper)
            acc_o[span, :] = acc_o[span, :] + dot_nn(active, weights(down))
            acc_d[span, :] = acc_d[span, :] + dot_nn(grad_upper, weights(up))
            if m == 0:
                gather_step(9 + 2 * part)
            elif m == 1:
                pl.when(part > 0)(lambda: sum_step(2 * part - 2, 0))
            elif m == 2:
                gather_step(10 + 2 * part)
            else:
                pl.when(part > 0)(lambda: sum_step(2 * part - 1, 1))
        dpar[pl.ds(8 + part, 1), :] = bias_grad
        dw[0] = dot_tn(tok[...], grad[...]).astype(BF16).reshape(4, 2, 2, ROWS_CHIP, D)
        sum_start(2 * part, 0)
        dw[1] = dot_tn(du[...], c_in[...]).astype(BF16).reshape(4, 2, 2, ROWS_CHIP, D)
        sum_start(2 * part + 1, 1)
        return carry

    lax.fori_loop(0, 4, feed, 0)

    for m in range(row_tiles):
        span = span_of(m)
        du[span, :] = acc_o[span, :].astype(BF16)
        hat = hat_two[span, :].astype(F32)
        cotangent = acc_d[span, :]
        upstream = grad[span, :].astype(F32)
        add_grad(1, col_sum(cotangent * hat))
        add_grad(3, col_sum(cotangent))
        add_grad(7, col_sum(upstream))
        value = upstream + norm_back(cotangent, hat, scale_two[span, :], param(1))
        acc_d[span, :] = value
        rounded = value.astype(BF16)
        c_in[span, :] = rounded
        add_grad(6, col_sum(rounded))
        mixed_grad = dot_nt(rounded, weights(3)).astype(BF16)
        tok[span, :] = dot_nt(mixed_grad, perm[...]).astype(BF16)
        if m == 0:
            sum_step(6, 0)
        elif m == 2:
            sum_step(7, 1)
    out_copy = pltpu.make_async_copy(du, out_hbm, out_sem.at[0])
    out_copy.start()
    dw[0] = dot_tn(o[...], c_in[...]).astype(BF16).reshape(4, 2, 2, ROWS_CHIP, D)
    sum_start(8, 0)

    def attend_back(t, carry):
        span = pl.ds(pl.multiple_of(t * TILE, TILE), TILE)
        for p in range(HEADS // 2):
            cols = slice(p * TILE, (p + 1) * TILE)
            cotangent = both(tok[span, cols])
            weight = prob[t, p]
            wide = weight.astype(F32)
            queries, keys = both(qkv[0, span, cols]), both(qkv[1, span, cols])
            back = dot_nt(cotangent, qkv[2, span, cols])
            score_grad = (wide * (back - jnp.sum(wide * back, -1, keepdims=True))).astype(BF16)
            qkv[0, span, cols] = (dot_nn(side(score_grad), keys) * score_scale).astype(BF16)
            qkv[1, span, cols] = (dot_tn(score_grad, queries) * score_scale).astype(BF16)
            qkv[2, span, cols] = dot_tn(weight, cotangent).astype(BF16)
        return carry

    lax.fori_loop(0, 1, by_two(attend_back), 0)
    sum_step(8, 0)
    lax.fori_loop(1, 3, by_two(attend_back), 0)
    sum_two(8)
    sum_three(7)
    sum_four(6)
    lax.fori_loop(3, tiles // 2, by_two(attend_back), 0)

    for n in range(3):
        slot = (n + 1) % 2
        dw[slot] = dot_tn(a[...], qkv[n]).astype(BF16).reshape(4, 2, 2, ROWS_CHIP, D)
        sum_start(9 + n, slot)
        if n == 0:
            sum_three(8)
            sum_four(7)
        else:
            sum_one(8 + n, (n + 0) % 2)
            if n == 1:
                sum_four(8)
            else:
                sum_two(9)
    add_grad(4, col_sum(qkv[0]))
    add_grad(5, col_sum(qkv[2]))
    for m in range(row_tiles):
        span = span_of(m)
        cotangent = dot_nt(qkv[0, span, :], weights(0)) + dot_nt(qkv[1, span, :], weights(1)) + dot_nt(qkv[2, span, :], weights(2))
        cotangent = dot_nt(cotangent.astype(BF16), perm[...])
        hat = hat_one[span, :].astype(F32)
        add_grad(0, col_sum(cotangent * hat))
        add_grad(2, col_sum(cotangent))
        grad[span, :] = (acc_d[span, :] + norm_back(cotangent, hat, scale_one[span, :], param(0))).astype(BF16)
        if m == 0:
            sum_one(11, 1)
            sum_two(10)
            sum_three(9)
        elif m == 2:
            sum_two(11)
            sum_three(10)
            sum_four(9)
    in_grad_copy = pltpu.make_async_copy(grad, in_grad_hbm, out_sem.at[1])
    in_grad_copy.start()

    rest = dpar[8:16, :]
    ordered = jnp.zeros((8, D), F32)
    for _ in range(3):
        low = rest.astype(BF16)
        ordered = ordered + dot_nt(low, perm[...])
        rest = rest - low.astype(F32)
    dpar[8:16, :] = ordered
    dvec_ref[...] = jnp.zeros_like(dvec_ref)
    for owner in range(8):
        dvec_ref[owner, 0:12, 0:96] = dpar[0:12, owner * 96 : (owner + 1) * 96]

    sum_three(11)
    sum_four(10)
    sum_four(11)
    fin_copy = pltpu.make_async_copy(fin, fin_hbm, out_sem.at[2])
    fin_copy.start()

    def finish(n, carry):
        for i in range(3):
            ag(n, i, one(n, z), along_z[i]).wait_send()
        for i in range(3, 10):
            ag(n, i, four(n, x, y, half), across_c).wait_send()
        for i in range(1, 4):
            rs(n, i, from_core.at[n, :, x, y], from_second.at[n], first).wait_send()
        for i in range(4, 7):
            rs(n, i, from_core.at[n, z, x, y], from_z.at[n, 0], first).wait_send()
        return carry

    lax.fori_loop(0, CHUNKS, finish, 0)
    out_copy.wait()
    in_grad_copy.wait()
    fin_copy.wait()


def rows_kernel(step_ref, split_ref, table_ref, rows_ref, groups, sem):
    count = rows_ref.shape[0]
    first = lax.axis_index("seq") * (count // 2)

    def step_of(i):
        tile = first + i // 2
        return step_ref[0, tile] if i % 2 == 0 else step_ref[split_ref[tile], tile]

    for i in range(count):
        pltpu.make_async_copy(table_ref.at[step_of(i) // 16], groups.at[i], sem).start()
    pltpu.make_async_copy(groups, groups, sem).wait()
    row_index = lax.broadcasted_iota(jnp.int32, (16, D), 0)
    for i in range(count):
        picked = jnp.where(row_index == step_of(i) % 16, groups[i].astype(F32), 0.0)
        rows_ref[i : i + 1, :] = jnp.sum(picked, 0, keepdims=True)


def pick_rows(time_step, tile_split, table, count):
    smem = pl.BlockSpec(memory_space=pltpu.SMEM)
    return pl.pallas_call(
        rows_kernel,
        out_shape=jax.ShapeDtypeStruct((count, D), F32),
        in_specs=[smem, smem, pl.BlockSpec(memory_space=pl.ANY)],
        out_specs=pl.BlockSpec(memory_space=pltpu.VMEM),
        scratch_shapes=[pltpu.VMEM((count, 16, D), BF16), pltpu.SemaphoreType.DMA],
        compiler_params=pltpu.CompilerParams(vmem_limit_bytes=60 * MIB),
        name="pick_rows",
    )(time_step, tile_split, table.reshape(-1, 16, D))


def run_stream(tokens, out_grad, rows, tile_split, block_slot, pieces, vecs):
    tok_rows = tokens.shape[0]
    tiles = tok_rows // TILE
    smem = pl.BlockSpec(memory_space=pltpu.SMEM)
    vmem = pl.BlockSpec(memory_space=pltpu.VMEM)
    hbm = pl.BlockSpec(memory_space=pl.ANY)
    rows_low = pltpu.VMEM((tok_rows, D), BF16)
    rows_full = pltpu.VMEM((tok_rows, D), F32)
    rows_one = pltpu.VMEM((tok_rows, 1), F32)
    return pl.pallas_call(
        stream_kernel,
        out_shape=(
            jax.ShapeDtypeStruct((tok_rows, D), BF16),
            jax.ShapeDtypeStruct((tok_rows, D), BF16),
            jax.ShapeDtypeStruct((CHUNKS, ROWS_CHIP, SPAN), BF16),
            jax.ShapeDtypeStruct(vecs.shape, F32),
        ),
        in_specs=[vmem, smem, smem, hbm, hbm, hbm, vmem],
        out_specs=(hbm, hbm, hbm, vmem),
        scratch_shapes=[
            pltpu.VMEM((16, D), F32),
            pltpu.VMEM((16, D), F32),
            pltpu.VMEM((8, D), F32),
            pltpu.VMEM((D, D), BF16),
            pltpu.VMEM((ROWS_CHIP, D), BF16),
            rows_low,
            rows_low,
            pltpu.VMEM((NBLK, 8, WIDE), BF16),
            rows_low,
            rows_one,
            rows_low,
            pltpu.VMEM((3, tok_rows, D), BF16),
            pltpu.VMEM((tiles, HEADS // 2, 2 * TILE, TILE), BF16),
            rows_low,
            rows_low,
            rows_one,
            rows_low,
            rows_full,
            rows_full,
            rows_low,
            pltpu.VMEM((CHUNKS, 4, 2, 2, ROWS_CHIP, D), BF16),
            pltpu.VMEM((2, 4, 2, 2, ROWS_CHIP, D), BF16),
            pltpu.VMEM((CHUNKS, 4, 2, 2, ROWS_CHIP, SPAN), BF16),
            pltpu.VMEM((CHUNKS, 2, 4, ROWS_CHIP, SPAN), BF16),
            pltpu.VMEM((CHUNKS, 4, ROWS_CHIP, SPAN), BF16),
            pltpu.VMEM((CHUNKS, 3, ROWS_CHIP, SPAN), BF16),
            pltpu.VMEM((CHUNKS, ROWS_CHIP, SPAN), BF16),
            pltpu.SemaphoreType.DMA((3,)),
            pltpu.SemaphoreType.DMA((3,)),
            pltpu.SemaphoreType.DMA((CHUNKS, 10)),
            pltpu.SemaphoreType.DMA((CHUNKS, 10)),
            pltpu.SemaphoreType.DMA((CHUNKS, 7)),
            pltpu.SemaphoreType.DMA((CHUNKS, 7)),
        ],
        compiler_params=pltpu.CompilerParams(collective_id=3, has_side_effects=True, vmem_limit_bytes=63 * MIB),
        name="stream",
    )(rows, tile_split, block_slot, tokens, out_grad, pieces, vecs)


def collect_kernel(
    inverse_ref, fin_ref, dvec_ref, gp_ref, vsum_ref,
    full, by_block, out, va, vb, vz, load_sem, own_sem, send_sem, recv_sem, vload_sem, vsend, vrecv,
):
    z, x, y, c = place()
    me = z * 2 + x
    quarter = y * 2 + c
    far = [(z + d) % 4 for d in (1, 2, 3)]
    near = [(z - d) % 4 for d in (1, 2, 3)]
    xt = (1 - c) * x + c * (1 - x)
    across_x = (z * 2 + (1 - x), quarter)
    across_y = (me, (1 - y) * 2 + c)
    across_c = (me, y * 2 + (1 - c))
    along_z = [(f * 2 + x, quarter) for f in far]
    skew = [(f * 2 + (1 - x), quarter) for f in far]
    half = pl.ds(pl.multiple_of(c * SPAN, SPAN), SPAN)
    own_half = pltpu.make_async_copy(fin_ref, full.at[:, :, half], load_sem)
    own_half.start()
    vec_load = pltpu.make_async_copy(dvec_ref, vb.at[0], vload_sem)
    vec_load.start()
    greet([across_x, across_y, across_c] + along_z + skew)
    copies = Copies(send_sem, recv_sem)
    vcopies = Copies(vsend, vrecv)
    copies.start(16, fin_ref, full.at[:, :, half], across_c)
    vcopies.start(0, dvec_ref, va, across_c)
    own_half.wait()
    copies.wait(16, full.at[:, :, pl.ds(pl.multiple_of((1 - c) * SPAN, SPAN), SPAN)], across_c)

    mine = lax.broadcasted_iota(jnp.int32, (8, BLK), 0) // 4 == y

    def split_chunk(n, block):
        for j in range(4):
            column = full[n, :, j * BLK : (j + 1) * BLK].astype(F32)
            for i in range(4):
                extra = column[32 + 4 * i : 36 + 4 * i]
                extra = jnp.where(mine, jnp.concatenate([extra, extra], 0), 0.0)
                by_block[block(i, j), :, 0:BLK] = column[8 * i : 8 * i + 8].astype(BF16)
                by_block[block(i, j), :, BLK:WIDE] = extra.astype(BF16)

    def split_feed(part, carry):
        split_chunk(2 * part, lambda i, j: 128 + part * 16 + i * 4 + j)
        split_chunk(2 * part + 1, lambda i, j: 64 + j * 16 + part * 4 + i)
        return carry

    lax.fori_loop(0, 4, split_feed, 0)
    split_chunk(8, functools.partial(chunk_block, 3))
    for n in range(3):
        split_chunk(9 + n, functools.partial(chunk_block, n))

    def pick(s, carry):
        out[s] = by_block[inverse_ref[s]]
        return carry

    def owner_part(zz):
        return out.at[pl.ds((zz * 2 + xt) * 24, 24)]

    def pick_part(zz):
        lax.fori_loop((zz * 2 + xt) * 24, (zz * 2 + xt) * 24 + 24, pick, 0)

    def chip(zz, xx, yy):
        return gp_ref.at[zz * 4 + xx * 2 + yy]

    for i in (1, 0, 2):
        pick_part(far[i])
        copies.start(i, owner_part(far[i]), chip(z, x, y), (far[i] * 2 + xt, quarter))
    pick_part(z)

    def straight():
        return pltpu.make_async_remote_copy(
            src_ref=owner_part(z), dst_ref=chip(z, x, y), send_sem=send_sem.at[3], recv_sem=recv_sem.at[3],
            device_id=across_x, device_id_type=MESH,
        )

    def stays():
        return pltpu.make_async_copy(owner_part(z), chip(z, x, y), own_sem)

    pl.when(c == 1)(lambda: straight().start())
    pl.when(c == 0)(lambda: stays().start())

    vec_load.wait()
    vcopies.wait(0, va, across_c)
    va[...] = va[...] + vb[0]
    vcopies.start(1, va, vb.at[1], across_y)

    pl.when(c == 1)(lambda: straight().wait())
    pl.when(c == 0)(lambda: stays().wait())
    ref = chip(z, xt, y)
    copies.start(7, ref, ref, across_y)
    copies.start(11, ref, ref, across_c)
    for i in range(3):
        ref = chip(near[i], xt, y)
        copies.wait(i, ref, across_c)
        copies.start(4 + i, ref, ref, across_y)
        copies.start(8 + i, ref, ref, across_c)
        if i == 0:
            vcopies.wait(1, vb.at[1], across_y)
            vb[1] = va[...] + vb[1]
            vcopies.start(2, vb.at[1], vb.at[2], across_x)
        elif i == 1:
            vcopies.wait(2, vb.at[2], across_x)
            vb[3] = vb[1] + vb[2]
            for k in range(3):
                vcopies.start(3 + k, vb.at[3, far[k] * 2 + x], vz.at[k], along_z[k])
    for i, zz in ((3, z), (0, near[0]), (1, near[1]), (2, near[2])):
        ref = chip(zz, xt, 1 - y)
        copies.wait(4 + i, ref, across_y)
        copies.start(12 + i, ref, ref, across_c)
    for i in range(3):
        vcopies.wait(3 + i, vz.at[i], across_c)
    vsum_ref[...] = vb[3, me] + vz[0] + vz[1] + vz[2]
    for i, zz in ((3, z), (0, near[0]), (1, near[1]), (2, near[2])):
        copies.wait(8 + i, chip(zz, 1 - xt, y), across_c)
        copies.wait(12 + i, chip(zz, 1 - xt, 1 - y), across_c)
    copies.finish()
    vcopies.finish()


def collect_sums(inverse, fin, dvec):
    hbm = pl.BlockSpec(memory_space=pl.ANY)
    return pl.pallas_call(
        collect_kernel,
        out_shape=(
            jax.ShapeDtypeStruct((16, 24, 8, WIDE), BF16),
            jax.ShapeDtypeStruct((16, 128), F32),
        ),
        in_specs=[pl.BlockSpec(memory_space=pltpu.SMEM), hbm, hbm],
        out_specs=(hbm, pl.BlockSpec(memory_space=pltpu.VMEM)),
        scratch_shapes=[
            pltpu.VMEM((CHUNKS, ROWS_CHIP, D), BF16),
            pltpu.VMEM((NBLK, 8, WIDE), BF16),
            pltpu.VMEM((NBLK, 8, WIDE), BF16),
            pltpu.VMEM((8, 16, 128), F32),
            pltpu.VMEM((4, 8, 16, 128), F32),
            pltpu.VMEM((3, 16, 128), F32),
            pltpu.SemaphoreType.DMA,
            pltpu.SemaphoreType.DMA,
            pltpu.SemaphoreType.DMA((17,)),
            pltpu.SemaphoreType.DMA((17,)),
            pltpu.SemaphoreType.DMA,
            pltpu.SemaphoreType.DMA((6,)),
            pltpu.SemaphoreType.DMA((6,)),
        ],
        compiler_params=pltpu.CompilerParams(collective_id=4, has_side_effects=True, vmem_limit_bytes=61 * MIB),
        name="collect_sums",
    )(inverse, fin, dvec)


def dot_split(left, right):
    left_high, right_high = left.astype(BF16), right.astype(BF16)
    left_low = (left - left_high.astype(F32)).astype(BF16)
    right_low = (right - right_high.astype(F32)).astype(BF16)
    return dot_nn(left_high, right_high) + (dot_nn(left_low, right_high) + dot_nn(left_high, right_low))


def step_kernel(
    items_count, inverse_ref, sum_ref, vsum_ref, weight_ref, momentum_ref, left_ref, right_ref, root_l_ref, root_r_ref,
    vec_ref, first_ref, second_ref, output_ref, in_grad_ref,
    grad_out, momentum_out, weight_out, left_out, right_out, vgrad_out, first_out, second_out, vec_out, output_out, in_grad_out,
    pass_sem,
):
    passed = (
        pltpu.make_async_copy(output_ref, output_out, pass_sem.at[0]),
        pltpu.make_async_copy(in_grad_ref, in_grad_out, pass_sem.at[1]),
    )

    @pl.when(pl.program_id(0) == 0)
    def _():
        for copy in passed:
            copy.start()

    inverse = 1.0 / items_count
    count = weight_ref.shape[0]
    for s in range(count):
        if len(sum_ref.shape) == 4:
            wide = sum_ref[:, s, :, 0:BLK].astype(F32).reshape(128, BLK)
            narrow = sum_ref[:, s, :, BLK:WIDE].astype(F32).reshape(8, 2, 8, BLK)
            grad = jnp.concatenate([wide, (narrow[:, 0] + narrow[:, 1]).reshape(64, BLK)], 0)
            block = inverse_ref[(lax.axis_index("items") * pl.num_programs(0) + pl.program_id(0)) * count + s]
            up = jnp.logical_and(block >= 64, block < 128)
            grad = jnp.where(up, jnp.transpose(grad, (1, 0)), grad) * inverse
        else:
            packed = sum_ref[s]
            grad = jnp.concatenate([packed[:, 0:BLK], packed[:, BLK:WIDE]], 0).astype(F32) * inverse
        low = grad.astype(BF16)
        grad_out[s] = grad
        momentum = 0.9 * momentum_ref[s] + grad
        momentum_out[s] = momentum
        left_out[s] = 0.95 * left_ref[s] + 0.05 * dot_nt(low, low)
        right_out[s] = 0.95 * right_ref[s] + 0.05 * dot_tn(low, low)
        direction = dot_split(dot_split(root_l_ref[s], momentum), root_r_ref[s])
        weight = weight_ref[s]
        scale = jnp.sqrt(jnp.mean(weight * weight) + 1e-06) * lax.rsqrt(jnp.mean(direction * direction) + 1e-06)
        weight_out[s] = weight - (0.3 * scale) * direction

    @pl.when(pl.program_id(0) == 0)
    def _():
        rows, cols = vec_ref.shape
        grad = vsum_ref[0:rows, 0:cols] * inverse
        vgrad_out[...] = grad
        first = 0.9 * first_ref[...] + 0.1 * grad
        second = 0.999 * second_ref[...] + 0.001 * grad * grad
        first_out[...] = first
        second_out[...] = second
        vec_out[...] = vec_ref[...] - 0.1 * first / (jnp.sqrt(second) + 1e-08)

    @pl.when(pl.program_id(0) == pl.num_programs(0) - 1)
    def _():
        for copy in passed:
            copy.wait()


def run_step(items_count, inverse, sums, vsums, weights, momentum, left, right, root_l, root_r, vectors, first, second, output, in_grad):
    count = weights.shape[0]
    per = 6 if count % 6 == 0 else 3
    block = pl.BlockSpec((per, BLK, BLK), lambda i: (i, 0, 0))
    if len(sums.shape) == 4:
        packed = pl.BlockSpec((16, per, 8, WIDE), lambda i: (0, i, 0, 0))
    else:
        packed = pl.BlockSpec((per, HALF, WIDE), lambda i: (i, 0, 0))
    small = pl.BlockSpec(vectors.shape, lambda i: (0, 0))
    vsum = pl.BlockSpec(vsums.shape, lambda i: (0, 0))
    whole = pl.BlockSpec(memory_space=pl.ANY)
    slots = jax.ShapeDtypeStruct(weights.shape, F32)
    vec = jax.ShapeDtypeStruct(vectors.shape, F32)
    return pl.pallas_call(
        functools.partial(step_kernel, items_count),
        grid=(count // per,),
        out_shape=(slots,) * 5 + (vec,) * 4 + (jax.ShapeDtypeStruct(output.shape, BF16),) * 2,
        in_specs=[pl.BlockSpec(memory_space=pltpu.SMEM), packed, vsum] + [block] * 6 + [small] * 3 + [whole] * 2,
        out_specs=[block] * 5 + [small] * 4 + [whole] * 2,
        scratch_shapes=[pltpu.SemaphoreType.DMA((2,))],
        compiler_params=pltpu.CompilerParams(vmem_limit_bytes=62 * MIB),
        name="step",
    )(inverse, sums, vsums, weights, momentum, left, right, root_l, root_r, vectors, first, second, output, in_grad)


def body(
    tokens, out_grad, time_table, time_step, tile_split, block_slot, weight_slots, momentum_slots,
    stat_left, stat_right, root_left, root_right, vectors, vector_first, vector_second,
):
    items_count = lax.axis_size("items")
    spots = jnp.arange(NBLK, dtype=jnp.int32)
    inverse = jnp.sum(jnp.where(block_slot[None, :] == spots[:, None], spots[None, :], 0), 1)
    if items_count == 8 and lax.axis_size("seq") == 4:
        pieces, vecs = deal_weights(weight_slots, block_slot.reshape(1, NBLK), vectors)
        rows = pick_rows(time_step.T, tile_split, time_table, 2 * tokens.shape[0] // TILE)
        output, input_grad, fin, dvec = run_stream(
            tokens, out_grad, rows, tile_split, block_slot, pieces.reshape(NBLK, 8, WIDE), vecs
        )
        sums, vsums = collect_sums(inverse, fin, dvec)
    else:
        low = weight_slots.astype(BF16)
        blocks = lax.all_gather(jnp.concatenate([low[:, :HALF], low[:, HALF:]], 2), "items", axis=0, tiled=True)
        vecs = lax.all_gather(vectors, "items", axis=1, tiled=True)
        output, input_grad, parts, dvec = run_layer(
            tokens, out_grad, time_table, time_step.T, tile_split, block_slot, blocks, vecs
        )
        sums = lax.psum_scatter(parts.astype(F32), "items", scatter_dimension=0, tiled=True)
        vsums = lax.psum_scatter(dvec, "items", scatter_dimension=1, tiled=True)
        sums, vsums = lax.psum((sums, vsums), "seq")
    stepped = run_step(
        items_count, inverse, sums, vsums, weight_slots, momentum_slots, stat_left, stat_right, root_left, root_right,
        vectors, vector_first, vector_second, output, input_grad,
    )
    grad, momentum, weights, left, right, vgrad, first, second, vecs_new, output, input_grad = stepped
    return output, input_grad, grad, momentum, weights, left, right, vgrad, first, second, vecs_new


def solution(mesh):
    return jax.shard_map(
        body,
        mesh=mesh,
        in_specs=(
            P(("items", "seq"), None),
            P(("items", "seq"), None),
            P(),
            P("items", None),
            P("items"),
            P(),
            P("items", None, None),
            P("items", None, None),
            P("items", None, None),
            P("items", None, None),
            P("items", None, None),
            P("items", None, None),
            P(None, "items"),
            P(None, "items"),
            P(None, "items"),
        ),
        out_specs=(
            P(("items", "seq"), None),
            P(("items", "seq"), None),
            P("items", None, None),
            P("items", None, None),
            P("items", None, None),
            P("items", None, None),
            P("items", None, None),
            P(None, "items"),
            P(None, "items"),
            P(None, "items"),
            P(None, "items"),
        ),
        check_vma=False,
    )
```
